256 devices in a mesh: seq: 8 (over x, y_lo), tp: 16 (over z, core), section: 2 (over y_hi).
Axes of the slice: x: 4, y: 4 (y_hi: 2, y_lo: 2; y = y_hi * 2 + y_lo), z: 8, core: 2. Of those that a mesh axis runs over, the one named last changes fastest.
Arguments:
- text_states: bfloat16 [4096, 8192], P(('seq', 'section'), 'tp')
- norm_gain: bfloat16 [8192], P('tp'), may hold values from 0.099609375 to 1.8984375
- w_query: bfloat16 [8192, 4096], P(None, 'tp'), may hold values from -0.0625 to 0.0625
- w_keyval: bfloat16 [8192, 1024], P('tp'), may hold values from -0.0625 to 0.0625
- w_output: bfloat16 [4096, 8192], P('tp'), may hold values from -0.125 to 0.125
- query_gain: float32 [128], replicated, may hold values from 1 to 2
- key_gain: float32 [128], replicated, may hold values from 1 to 2
- attn_gate: float32 [1], replicated, may hold values from 0.5 to 1.5
- image_states: bfloat16 [16, 1601, 8192], P(('seq', 'section'), None, 'tp'), may hold values from -6 to 6
- seg_ids: int32 [4096], P(('seq', 'section')), may hold values from 0 to 7, as said below
- image_owner: int32 [16], P(('seq', 'section')), may hold values from 0 to 7, as said below
- image_pos: int32 [16], P(('seq', 'section')), may hold values from 0 to 4095, as said below
Outputs:
- update: bfloat16 [4096, 8192], P(('seq', 'section'), 'tp')
The draws below stay inside these ranges and needn't reach their ends.
Inputs may be any that keep to these rules, and one draw needn't show every extreme that they name: `seg_ids`: non-decreasing along the text; each of the 8 documents holds at least one token. `image_owner`: equal to seg_ids at the image's position image_pos. `image_pos`: some image stands at position 0 and some at the last position.
All inputs are finite; a program needn't handle non-finite values.
Results may differ from the reference program's by a relative error of at most 0.012.
Values may be sent and summed in bfloat16 or wider, within the bound.
A program may use at most 192 MiB of HBM per device.

```python
import jax
import jax.numpy as jnp
from jax import lax

D = 8192
HEADS = 32
KV_HEADS = 4
HD = 128
IMG_TOK = 1601
SEGS = 8
TOK_DEV = 256
TOKENS = 4096
IMAGES = 16


def layout(key):
    doc_cuts = jnp.sort(jax.random.permutation(jax.random.fold_in(key, 11), TOKENS - 1)[:SEGS - 1] + 1)
    places = jnp.arange(TOKENS, dtype=jnp.int32)
    doc_ids = jnp.sum((places[:, None] >= doc_cuts[None, :]).astype(jnp.int32), axis=1).astype(jnp.int32)
    image_spots = jax.random.randint(jax.random.fold_in(key, 12), (IMAGES,), 0, TOKENS)
    ranking = jax.random.permutation(jax.random.fold_in(key, 13), IMAGES)
    image_spots = jnp.where(ranking == 0, 0, jnp.where(ranking == 1, TOKENS - 1, image_spots)).astype(jnp.int32)
    return (doc_ids, image_spots, doc_ids[image_spots].astype(jnp.int32))


def draw_seg_ids(key, part):
    return layout(key)[0]


def draw_image_pos(key, part):
    return layout(key)[1]


def draw_image_owner(key, part):
    return layout(key)[2]


def draw_text_states(key, part):
    key = jax.random.fold_in(key, 3)
    key_base = jax.random.fold_in(key, 1)
    key_cols = jax.random.fold_in(key, 2)
    key_rows = jax.random.fold_in(key, 3)
    col_scale = jnp.exp(jnp.log(10.0) * jnp.arange(D, dtype=jnp.float32) / D)
    col_scale = col_scale * jax.random.uniform(key_cols, (D,), jnp.float32, 0.7, 1.4)
    row_scale = jnp.exp(jnp.log(10.0) * jax.random.uniform(key_rows, (TOKENS, 1), jnp.float32))
    base_draw = jax.random.normal(key_base, (TOKENS, D), jnp.float32)
    return (0.3 * base_draw * col_scale[None, :] * row_scale).astype(jnp.bfloat16)


def raised(array, own_key, source, target, parts, factor):
    owner, partner = [(jnp.arange(array.shape[position]) // (array.shape[position] // parts)).reshape([-1 if axis == position else 1 for axis in range(array.ndim)]) for position in (source, target)]
    chosen = jax.random.permutation(own_key, parts)[partner]
    strong = (owner == chosen) | (owner == (partner + parts // 2) % parts)
    return jnp.where(strong, factor * array, array)


def block_levels(own_key, dims, pieces, low, high):
    gain, own = 1.0, jax.random.fold_in(own_key, 6)
    for dim, blocks in pieces:
        draws = jnp.exp(jax.random.uniform(jax.random.fold_in(own, dim), (blocks,), jnp.float32, low / len(pieces), high / len(pieces)))
        gain = gain * jnp.repeat(draws, dims[dim] // blocks).reshape([-1 if axis == dim else 1 for axis in range(len(dims))])
    return gain


def scatter_about(stream_key, shape, width, reach, split=(), kind=jnp.bfloat16):
    drawn = width * jax.random.normal(stream_key, shape, jnp.float32)
    if split:
        drawn = drawn * block_levels(stream_key, shape, split, -0.22, 0.18)
    return jnp.clip(drawn, -reach, reach).astype(kind)


def bell_draw_with(own_key, dims, scale, bound, shards, heavy, kind=jnp.bfloat16):
    result = scale * jax.random.normal(own_key, dims, jnp.float32)
    if shards:
        result = result * block_levels(own_key, dims, shards, -0.22, 0.18)
    return jnp.clip(raised(result, jax.random.fold_in(own_key, 3), *heavy), -bound, bound).astype(kind)


def setup_inputs(seed: int = 0) -> dict:
    arg_keys = jax.random.split(jax.random.key(seed), 13)
    return {
        "text_states": draw_text_states(jax.random.fold_in(arg_keys[12], 71), 0),
        "norm_gain": jnp.clip(1.0 + 0.18 * jax.random.normal(arg_keys[1], (D,), jnp.float32), 0.099609375, 1.8984375).astype(jnp.bfloat16),
        "w_query": scatter_about(arg_keys[2], (D, HEADS * HD), D ** -0.5, 0.0625, ((1, 16),)),
        "w_keyval": scatter_about(arg_keys[3], (D, KV_HEADS * 2 * HD), D ** -0.5, 0.0625, ((0, 16),)),
        "w_output": bell_draw_with(arg_keys[4], (HEADS * HD, D), (HEADS * HD) ** -0.5, 0.125, ((0, 16),), (0, 1, 16, 2.0)),
        "query_gain": jnp.clip(jax.random.uniform(arg_keys[5], (HD,), jnp.float32, 1.0, 2.0), 1.0, 2.0),
        "key_gain": jnp.clip(jax.random.uniform(arg_keys[6], (HD,), jnp.float32, 1.0, 2.0), 1.0, 2.0),
        "attn_gate": jnp.clip(jax.random.uniform(arg_keys[7], (1,), jnp.float32, 0.5, 1.5), 0.5, 1.5),
        "image_states": scatter_about(arg_keys[8], (IMAGES, IMG_TOK, D), 1.0, 6.0, ((0, 16), (2, 16))),
        "seg_ids": draw_seg_ids(jax.random.fold_in(arg_keys[12], 71), 0),
        "image_owner": draw_image_owner(jax.random.fold_in(arg_keys[12], 71), 0),
        "image_pos": draw_image_pos(jax.random.fold_in(arg_keys[12], 71), 0),
    }


epsilon = 1e-05

def rms_norm(vector, gain_vec):
    return vector * lax.rsqrt(lax.optimization_barrier(jnp.mean(vector * vector, axis=-1, keepdims=True)) + epsilon) * gain_vec

def reference(text_states, norm_gain, w_query, w_keyval, w_output, query_gain, key_gain, attn_gate, image_states, seg_ids, image_owner, image_pos):
    normed = (text_states.astype(jnp.float32) * norm_gain.astype(jnp.float32)[None, :]).astype(jnp.bfloat16)
    queries = jnp.dot(normed, w_query, preferred_element_type=jnp.float32).reshape(TOKENS, HEADS, HD)
    queries = rms_norm(queries, query_gain).astype(jnp.bfloat16)
    projected = jnp.dot(image_states.reshape(IMAGES * IMG_TOK, D), w_keyval, preferred_element_type=jnp.float32)
    projected = projected.reshape(IMAGES, IMG_TOK, KV_HEADS, 2, HD)
    key_rows = rms_norm(projected[:, :, :, 0], key_gain).astype(jnp.bfloat16)
    value_rows = projected[:, :, :, 1].astype(jnp.bfloat16)
    group = HEADS // KV_HEADS
    places = jnp.arange(TOKENS, dtype=jnp.int32)
    visible = (seg_ids[:, None] == image_owner[None, :]) & (places[:, None] >= image_pos[None, :])
    block_count = TOKENS // TOK_DEV
    query_blocks = queries.reshape(block_count, TOK_DEV, KV_HEADS, group, HD)
    visible_blocks = visible.reshape(block_count, TOK_DEV, IMAGES)

    def one_block(inputs):
        query_block, seen_block = inputs
        query_wide = query_block.astype(jnp.float32)

        def one_image(running, image):
            acc_sum, weight_sum = running
            key_img, value_img, seen_img = image
            scores = jnp.einsum('rcgd,kcd->rcgk', query_wide, key_img.astype(jnp.float32)) * HD ** (-0.5)
            weights_exp = jnp.where(seen_img[:, None, None, None], jnp.exp(scores), 0.0)
            weight_sum = weight_sum + lax.optimization_barrier(jnp.sum(weights_exp, axis=-1))
            rounded = lax.optimization_barrier(weights_exp.astype(jnp.bfloat16))
            acc_sum = acc_sum + jnp.einsum('rcgk,kcd->rcgd', rounded.astype(jnp.float32), value_img.astype(jnp.float32))
            return ((acc_sum, weight_sum), None)
        start_state = (jnp.zeros((TOK_DEV, KV_HEADS, group, HD), jnp.float32), jnp.zeros((TOK_DEV, KV_HEADS, group), jnp.float32))
        (acc_sum, weight_sum), unused = lax.scan(one_image, start_state, (key_rows, value_rows, seen_block.T))
        return acc_sum / jnp.maximum(weight_sum, 1.0)[..., None]
    attended = lax.map(one_block, (query_blocks, visible_blocks))
    attended = attended.reshape(TOKENS, HEADS * HD).astype(jnp.bfloat16)
    branch = jnp.dot(attended, w_output, preferred_element_type=jnp.float32)
    return (jnp.tanh(attn_gate[0]) * branch).astype(jnp.bfloat16)
```

```python
import functools

import jax
import jax.numpy as jnp
from jax import lax
from jax.experimental import pallas as pl
from jax.experimental.pallas import tpu as pltpu
from jax.sharding import PartitionSpec as P

MESH = pl.DeviceIdType.MESH
F32, BF16 = jnp.float32, jnp.bfloat16
HD = 128
IMG_TOK = 1601
IMAGES = 16
TOK = 256
QUARTER = 416
HALF = 2 * QUARTER
ROWS = 4 * QUARTER
EPS = 1e-05
META = 2.0**-20
META_ROW = ROWS - 16

SUBS = ((0, 112, 96), (208, 96, 112))
LAG = 5


def remote(src, dst, send, recv, device):
    return pltpu.make_async_remote_copy(
        src_ref=src, dst_ref=dst, send_sem=send, recv_sem=recv, device_id=device, device_id_type=MESH
    )


class Place:
    def __init__(self):
        seq, tp, sec = lax.axis_index("seq"), lax.axis_index("tp"), lax.axis_index("section")
        self.tp, self.z, self.c = tp, tp // 2, tp % 2
        self.x, self.y = seq // 2, sec * 2 + seq % 2
        self.partner = {"tp": self.z * 2 + 1 - self.c}
        self.up = {"tp": ((self.z + 1) % 8) * 2 + self.c}
        self.down = {"tp": ((self.z + 7) % 8) * 2 + self.c}

    def step(self, axis, delta):
        if axis == "x":
            return {"seq": ((self.x + delta) % 4) * 2 + self.y % 2}
        y = (self.y + delta) % 4
        return {"seq": self.x * 2 + y % 2, "section": y // 2}

    def image(self, dx, dy):
        y = (self.y + dy) % 4
        return ((self.x + dx) % 4) * 4 + (y % 2) * 2 + y // 2


def greet(devices):
    barrier = pltpu.get_barrier_semaphore()
    for device in devices:
        pl.semaphore_signal(barrier, inc=1, device_id=device, device_id_type=MESH)
    pl.semaphore_wait(barrier, len(devices))


def front_kernel(
    text, gain, wq, wkv, wout, qgain, kgain, owner, pos, img,
    q_out, kv, pwout,
    nall, wqv, qacc, imgv, pimg, wkvv, pwkv, acck, accv, rk, rv, vfirst, mine,
    load_sem, ex_send, ex_recv, bs, br, xs, xr, ps, pr, cs, cr, as_, ar, acs, acr, ws, wr,
):
    me = Place()
    z, c = me.z, me.c
    zpar = z % 2
    greet([me.partner, me.up, me.down] + [me.step(a, d) for a in "xy" for d in (1, 3)])
    sends = []

    def send(src, dst, ssem, rsem, device):
        copy = remote(src, dst, ssem, rsem, device)
        copy.start()
        sends.append(copy)

    def arrived(ref, ssem, rsem):
        remote(ref, ref, ssem, rsem, me.partner).wait_recv()

    send(img.at[pl.ds((1 - c) * HALF, HALF)], pimg, ex_send.at[0], ex_recv.at[0], me.partner)
    send(wkv, pwkv, ex_send.at[1], ex_recv.at[1], me.partner)
    loads = [
        pltpu.make_async_copy(img.at[pl.ds(c * HALF, HALF)], imgv, load_sem.at[0]),
        pltpu.make_async_copy(wkv, wkvv, load_sem.at[1]),
        pltpu.make_async_copy(wq, wqv, load_sem.at[2]),
    ]
    for load in loads:
        load.start()

    shard = lambda k: ((z + k % 8) % 8) * 2 + c
    nall[me.tp] = (text[...].astype(F32) * gain[...].astype(F32)).astype(BF16)
    qacc[...] = jnp.zeros_like(qacc)

    def text_send(k, way, hop):
        ref = nall.at[shard(k)]
        if hop == 4:
            ref = ref.at[pl.ds(way * 128, 128)]
        send(ref, ref, as_.at[way, hop - 1], ar.at[way, hop - 1], (me.up, me.down)[way])

    def text_share(k):
        ref = nall.at[shard(k)]
        send(ref, ref, acs.at[k % 8], acr.at[k % 8], me.partner)

    def text_use(index):
        w = wqv[pl.ds(pl.multiple_of(index * 512, 512), 512), :]
        qacc[...] += jnp.dot(nall[index], w, preferred_element_type=F32)

    def text_arrived(hop, way):
        k = -hop if way == 0 else hop
        ref = nall.at[shard(k)]
        if hop == 4:
            ref = ref.at[pl.ds(way * 128, 128)]
        arrived(ref, as_.at[way, hop - 1], ar.at[way, hop - 1])

    def text_round(hop):
        for way in (0, 1):
            text_arrived(hop, way)
            if hop < 4:
                k = -hop if way == 0 else hop
                text_send(k, way, hop + 1)
                text_share(k)
        if hop == 4:
            text_share(4)

    def text_compute(hop):
        for k in {0: (0,), 4: (4,)}.get(hop, (hop, -hop)):
            text_use(shard(k))

    def text_compute_shared(hop):
        for k in {0: (0,), 4: (4,)}.get(hop, (hop, -hop)):
            index = ((z + k % 8) % 8) * 2 + 1 - c
            arrived(nall.at[index], acs.at[k % 8], acr.at[k % 8])
            text_use(index)

    text_send(0, 0, 1)
    text_send(0, 1, 1)
    text_share(0)

    loads[0].wait()
    loads[1].wait()
    arrived(pimg, ex_send.at[0], ex_recv.at[0])
    arrived(pwkv, ex_send.at[1], ex_recv.at[1])

    def project(k):
        d = (z + k) % 8
        rows = pl.ds(pl.multiple_of((d % 2) * QUARTER, QUARTER), QUARTER)
        cols = pl.ds(pl.multiple_of((d // 2) * 256, 256), 256)
        part = jnp.dot(imgv[rows, :], wkvv[:, cols], preferred_element_type=F32)
        part += jnp.dot(pimg[rows, :], pwkv[:, cols], preferred_element_type=F32)
        acck[d] = part[:, :HD]
        accv[d] = part[:, HD:]

    def ring_rows(u, way):
        start, first, second = SUBS[u]
        return (start, first) if way == 0 else (start + first, second)

    def ring_send(u, step):
        for way in (0, 1):
            r0, n = ring_rows(u, way)
            device = (me.up, me.down)[way]
            rows = pl.ds(r0, n)
            if step == 0:
                d = (z + (7, 1)[way]) % 8
                vfirst[rows, :] = accv[d, rows, :].astype(BF16)
                srck, srcv = acck.at[d, rows], vfirst.at[rows]
            else:
                srck, srcv = rk.at[step - 1, rows], rv.at[step - 1, rows]
            send(srck, rk.at[step, rows], bs.at[u, way, step, 0], br.at[u, way, step, 0], device)
            send(srcv, rv.at[step, rows], bs.at[u, way, step, 1], br.at[u, way, step, 1], device)

    def ring_receive(u, step):
        for way in (0, 1):
            r0, n = ring_rows(u, way)
            rows = pl.ds(r0, n)
            arrived(rk.at[step, rows], bs.at[u, way, step, 0], br.at[u, way, step, 0])
            arrived(rv.at[step, rows], bs.at[u, way, step, 1], br.at[u, way, step, 1])
            if step < 6:
                d = (z + (6 - step if way == 0 else 2 + step)) % 8
                rk[step, rows, :] += acck[d, rows, :]
                rv[step, rows, :] = (rv[step, rows, :].astype(F32) + accv[d, rows, :]).astype(BF16)

    def finish(u):
        start, first, second = SUBS[u]
        n = first + second
        rows = pl.ds(start, n)
        key = rk[6, rows, :] + acck[z, rows, :]
        val = rv[6, rows, :].astype(F32) + accv[z, rows, :]
        key = key * lax.rsqrt(jnp.mean(key * key, axis=-1, keepdims=True) + EPS) * kgain[...]
        if u == len(SUBS) - 1:
            row = c * HALF + zpar * QUARTER + start + lax.broadcasted_iota(jnp.int32, (n, HD), 0)
            lane = lax.broadcasted_iota(jnp.int32, (n, HD), 1)
            said = jnp.where(lane == 0, owner[0], jnp.where(lane == 1, pos[0] // 64, pos[0] % 64))
            said = jnp.where(lane < 3, said, 0).astype(F32) * META
            key = jnp.where(row >= META_ROW, said, key)
        at = pl.ds(pl.multiple_of(zpar * QUARTER + start, 16), n)
        mine[at, 0:HD] = key.astype(BF16)
        mine[at, HD:] = val.astype(BF16)
        pair = {"tp": (z + 1 - 2 * zpar) * 2 + c}
        send(mine.at[at], mine.at[at], xs.at[u], xr.at[u], pair)

    here = me.image(0, 0)

    def block(u, par, i, j, part=None):
        start, first, second = SUBS[u]
        n = first + second
        if part == 0:
            n = first
        if part == 1:
            start, n = start + first, second
        m = me.image(i, j) if par == 0 else me.image(j, i)
        r0 = pl.multiple_of(c * HALF + par * QUARTER + start, 16)
        return kv.at[m, pl.ds(r0, n)]

    def own(u, par):
        start, first, second = SUBS[u]
        return mine.at[pl.ds(par * QUARTER + start, first + second)]

    axes = lambda par: ("x", "y") if par == 0 else ("y", "x")

    def spread_first(u, par, i, way, part=None):
        slot = {(0, 0): 0, (0, 1): 1, (3, 0): 2, (1, 1): 3}[(i, way)]
        src = own(u, par) if i == 0 else block(u, par, i, 0, part)
        dst = block(u, par, i, 0, part)
        send(src, dst, ps.at[u, par, slot], pr.at[u, par, slot], me.step(axes(par)[0], (1, 3)[way]))

    def first_arrived(u, par, i, part=None):
        slot = {(3, None): 0, (1, None): 1, (2, 1): 2, (2, 0): 3}[(i, part)]
        arrived(block(u, par, i, 0, part), ps.at[u, par, slot], pr.at[u, par, slot])

    def spread_second(u, par, i, j, way):
        slot = 4 + 3 * i + (way if j == 0 else 2)
        src = own(u, par) if (i, j) == (0, 0) else block(u, par, i, j)
        send(src, block(u, par, i, j), ps.at[u, par, slot], pr.at[u, par, slot], me.step(axes(par)[1], (1, 3)[way]))

    def second_arrived(u, par, i, j):
        slot = 4 + 3 * i + {3: 0, 1: 1, 2: 2}[j]
        arrived(block(u, par, i, j), ps.at[u, par, slot], pr.at[u, par, slot])

    def share(u, par, i, j):
        src = own(u, par) if (i, j) == (0, 0) else block(u, par, i, j)
        send(src, block(u, par, i, j), cs.at[u, par, 4 * i + j], cr.at[u, par, 4 * i + j], me.partner)

    def column(u, par, i):
        spread_second(u, par, i, 0, 0)
        spread_second(u, par, i, 0, 1)
        share(u, par, i, 0)

    def column_arrived(u, par, i):
        for j, way in ((3, 0), (1, 1)):
            second_arrived(u, par, i, j)
            if (j == 3) == (i < 2):
                spread_second(u, par, i, j, way)
            share(u, par, i, j)

    local = []

    def plane_round(u, r):
        if r == 0:
            start, first, second = SUBS[u]
            at = pl.ds(pl.multiple_of((1 - zpar) * QUARTER + start, 16), first + second)
            arrived(mine.at[at], xs.at[u], xr.at[u])
        for par in (0, 1):
            if r == 0:
                spread_first(u, par, 0, 0)
                spread_first(u, par, 0, 1)
                column(u, par, 0)
                keep = pltpu.make_async_copy(own(u, par), block(u, par, 0, 0), load_sem.at[3 + 2 * u + par])
                keep.start()
                local.append(keep)
            if r == 1:
                first_arrived(u, par, 3)
                spread_first(u, par, 3, 0, 1)
                column(u, par, 3)
                first_arrived(u, par, 1)
                spread_first(u, par, 1, 1, 0)
                column(u, par, 1)
            if r == 2:
                column_arrived(u, par, 0)
            if r == 3:
                first_arrived(u, par, 2, 0)
                first_arrived(u, par, 2, 1)
                column(u, par, 2)
            if r == 4:
                column_arrived(u, par, 3)
                column_arrived(u, par, 1)
            if r == 5:
                column_arrived(u, par, 2)
            if r == 6:
                for i in (0, 3, 1, 2):
                    second_arrived(u, par, i, 2)
                    share(u, par, i, 2)

    def ring_step(u, step):
        ring_receive(u, step)
        if step < 6:
            ring_send(u, step + 1)
        else:
            finish(u)

    project(7)
    project(1)
    ring_send(0, 0)
    for k in (6, 2, 5, 3, 4, 0):
        project(k)
    for k in range(8):
        src = wout.at[:, pl.ds(pl.multiple_of((2 * k + 1 - c) * 512, 512), 512)]
        send(src, pwout.at[k], ws.at[k], wr.at[k], me.partner)
    loads[2].wait()
    text_compute(0)

    for step in range(LAG):
        ring_step(0, step)
    ring_send(1, 0)
    for step in range(LAG, 7):
        ring_step(0, step)
        ring_step(1, step - LAG)
    done = 7 - LAG
    plane_round(0, 0)
    ring_step(1, done)
    plane_round(0, 1)
    ring_step(1, done + 1)
    plane_round(0, 2)
    ring_step(1, done + 2)
    plane_round(0, 3)
    for step in range(done + 3, 7):
        ring_step(1, step)
    text_round(1)
    plane_round(1, 0)
    plane_round(0, 4)
    text_compute(1)
    plane_round(0, 5)
    plane_round(1, 1)
    text_round(2)
    plane_round(0, 6)
    text_compute(2)
    text_compute_shared(0)
    plane_round(1, 2)
    plane_round(1, 3)
    text_round(3)
    text_compute(3)
    text_compute_shared(1)
    plane_round(1, 4)
    text_compute_shared(2)
    text_round(4)
    plane_round(1, 5)
    text_compute(4)
    text_compute_shared(3)
    text_compute_shared(4)

    for h in range(2):
        q = qacc[:, h * HD : (h + 1) * HD]
        q = q * lax.rsqrt(jnp.mean(q * q, axis=-1, keepdims=True) + EPS) * qgain[...]
        q_out[:, h * HD : (h + 1) * HD] = q.astype(BF16)

    plane_round(1, 6)
    for u, (start, first, second) in enumerate(SUBS):
        for par in (0, 1):
            for i in range(4):
                for j in range(4):
                    m = me.image(i, j) if par == 0 else me.image(j, i)
                    r0 = pl.multiple_of((1 - c) * HALF + par * QUARTER + start, 16)
                    ref = kv.at[m, pl.ds(r0, first + second)]
                    arrived(ref, cs.at[u, par, 4 * i + j], cr.at[u, par, 4 * i + j])
    for k in range(8):
        arrived(pwout.at[k], ws.at[k], wr.at[k])
    for keep in local:
        keep.wait()
    for copy in sends:
        copy.wait_send()


def front(text, gain, wq, wkv, wout, qgain, kgain, owner, pos, img):
    vmem, anyspace, smem = (pl.BlockSpec(memory_space=m) for m in (pltpu.VMEM, pl.ANY, pltpu.SMEM))
    dma = pltpu.SemaphoreType.DMA
    n = len(SUBS)
    return pl.pallas_call(
        front_kernel,
        out_shape=(
            jax.ShapeDtypeStruct((TOK, 256), BF16),
            jax.ShapeDtypeStruct((IMAGES, ROWS, 256), BF16),
            jax.ShapeDtypeStruct((8, 256, 512), BF16),
        ),
        in_specs=[vmem, vmem, anyspace, anyspace, anyspace, vmem, vmem, smem, smem, anyspace],
        out_specs=(vmem, anyspace, anyspace),
        scratch_shapes=[
            pltpu.VMEM((16, TOK, 512), BF16),
            pltpu.VMEM((8192, 256), BF16),
            pltpu.VMEM((TOK, 256), F32),
            pltpu.VMEM((HALF, 512), BF16),
            pltpu.VMEM((HALF, 512), BF16),
            pltpu.VMEM((512, 1024), BF16),
            pltpu.VMEM((512, 1024), BF16),
            pltpu.VMEM((8, QUARTER, HD), F32),
            pltpu.VMEM((8, QUARTER, HD), F32),
            pltpu.VMEM((7, QUARTER, HD), F32),
            pltpu.VMEM((7, QUARTER, HD), BF16),
            pltpu.VMEM((QUARTER, HD), BF16),
            pltpu.VMEM((HALF, 256), BF16),
            dma((3 + 2 * n,)),
            dma((2,)),
            dma((2,)),
            dma((n, 2, 7, 2)),
            dma((n, 2, 7, 2)),
            dma((n,)),
            dma((n,)),
            dma((n, 2, 16)),
            dma((n, 2, 16)),
            dma((n, 2, 16)),
            dma((n, 2, 16)),
            dma((2, 4)),
            dma((2, 4)),
            dma((8,)),
            dma((8,)),
            dma((8,)),
            dma((8,)),
        ],
        compiler_params=pltpu.CompilerParams(
            collective_id=0, has_side_effects=True, vmem_limit_bytes=56 * 2**20
        ),
        cost_estimate=pl.CostEstimate(flops=5 * 10**9, bytes_accessed=3 * 10**7, transcendentals=0),
    )(text, gain, wq, wkv, wout, qgain, kgain, owner, pos, img)


TILES = ((0, 256), (256, 256), (512, 256), (768, 256), (1024, 256), (1280, 256), (1536, 128))


def attend_kernel(q, seg, kv, out, meta, kbuf, vbuf, wexp, total, seen, sem, meta_sem):
    first = (lax.axis_index("seq") * 2 + lax.axis_index("section")) * TOK
    fetch = pltpu.make_async_copy(kv.at[:, pl.ds(META_ROW, 16), pl.ds(0, HD)], meta, meta_sem)
    fetch.start()
    total[...] = jnp.zeros_like(total)
    row = lax.broadcasted_iota(jnp.int32, (ROWS, HD), 0)
    ones = jnp.where(row < IMG_TOK, 1.0, 0.0).astype(BF16)
    vbuf[0, :, HD:] = ones
    vbuf[1, :, HD:] = ones
    fetch.wait()
    places = (first + lax.broadcasted_iota(jnp.int32, (TOK, 1), 0)).astype(F32)
    docs = seg[...].astype(F32)

    def sees(m):
        said = meta[m, 0:1, :].astype(F32) * (1.0 / META)
        lane = lax.broadcasted_iota(jnp.int32, (1, HD), 1)
        doc = jnp.sum(jnp.where(lane == 0, said, 0.0), axis=1, keepdims=True)
        weight = jnp.where(lane == 1, 64.0, jnp.where(lane == 2, 1.0, 0.0))
        start = jnp.sum(said * weight, axis=1, keepdims=True)
        return (docs == doc) & (places >= start)

    def look(m, count):
        flag = jnp.max(jnp.where(sees(m), 1.0, 0.0)) > 0.5

        @pl.when(flag)
        def _():
            seen[count] = m

        return count + flag.astype(jnp.int32)

    count = lax.fori_loop(0, IMAGES, look, jnp.int32(0))

    def copies(n):
        slot = n % 2
        m = seen[n]
        return (
            pltpu.make_async_copy(kv.at[m, :, pl.ds(0, HD)], kbuf.at[slot], sem.at[slot, 0]),
            pltpu.make_async_copy(kv.at[m, :, pl.ds(HD, HD)], vbuf.at[slot, :, pl.ds(0, HD)], sem.at[slot, 1]),
        )

    @pl.when(count > 0)
    def _():
        for copy in copies(0):
            copy.start()

    rows = jnp.concatenate([q[:, :HD], q[:, HD:]], axis=0)

    def image(n, carry):
        slot = n % 2

        @pl.when(n + 1 < count)
        def _():
            for copy in copies(n + 1):
                copy.start()

        for copy in copies(n):
            copy.wait()
        for k0, width in TILES:
            score = lax.dot_general(
                rows, kbuf[slot, k0 : k0 + width, :], (((1,), (1,)), ((), ())), preferred_element_type=F32
            )
            wexp[:, k0 : k0 + width] = jnp.exp2(score * (HD**-0.5 * 1.4426950408889634)).astype(BF16)
        term = jnp.dot(wexp[...], vbuf[slot], preferred_element_type=F32)
        mask = sees(seen[n])
        total[0:TOK, :] += jnp.where(mask, term[:TOK], 0.0)
        total[TOK:, :] += jnp.where(mask, term[TOK:], 0.0)
        return carry

    lax.fori_loop(0, count, image, 0)
    for h in range(2):
        part = total[h * TOK : (h + 1) * TOK, :]
        out[:, h * HD : (h + 1) * HD] = (part[:, :HD] / jnp.maximum(part[:, HD:], 1.0)).astype(BF16)


def attend(q, seg, kv):
    vmem, anyspace = (pl.BlockSpec(memory_space=m) for m in (pltpu.VMEM, pl.ANY))
    return pl.pallas_call(
        attend_kernel,
        out_shape=jax.ShapeDtypeStruct((TOK, 256), BF16),
        in_specs=[vmem, vmem, anyspace],
        out_specs=vmem,
        scratch_shapes=[
            pltpu.VMEM((IMAGES, 16, HD), BF16),
            pltpu.VMEM((2, ROWS, HD), BF16),
            pltpu.VMEM((2, ROWS, 256), BF16),
            pltpu.VMEM((2 * TOK, ROWS), BF16),
            pltpu.VMEM((2 * TOK, 256), F32),
            pltpu.SMEM((IMAGES,), jnp.int32),
            pltpu.SemaphoreType.DMA((2, 2)),
            pltpu.SemaphoreType.DMA,
        ],
        compiler_params=pltpu.CompilerParams(vmem_limit_bytes=48 * 2**20),
        cost_estimate=pl.CostEstimate(flops=5 * 10**9, bytes_accessed=10**7, transcendentals=5 * 10**6),
    )(q, seg, kv)


def back_kernel(att, gate, wout, pwout, out, patt, wo, pwo, got, sent, load_sem, e_send, e_recv, bs, br):
    me = Place()
    z, c = me.z, me.c
    loads = [pltpu.make_async_copy(pwout, pwo, load_sem.at[8])]
    for k in range(8):
        src = wout.at[:, pl.ds(pl.multiple_of((2 * k + c) * 512, 512), 512)]
        loads.append(pltpu.make_async_copy(src, wo.at[k], load_sem.at[k]))
    for load in loads:
        load.start()
    greet([me.partner, me.up, me.down])
    sends = []

    def send(src, dst, ssem, rsem, device):
        copy = remote(src, dst, ssem, rsem, device)
        copy.start()
        sends.append(copy)

    send(att, patt, e_send, e_recv, me.partner)
    for load in loads:
        load.wait()
    remote(att, patt, e_send, e_recv, me.partner).wait_recv()

    def term(way, d):
        rows = slice(way * 128, way * 128 + 128)
        part = jnp.dot(att[rows, :], wo[d], preferred_element_type=F32)
        return part + jnp.dot(patt[rows, :], pwo[d], preferred_element_type=F32)

    for step in range(8):
        for way in (0, 1):
            d = (z + (7 - step if way == 0 else 1 + step)) % 8
            part = term(way, d)
            if step > 0:
                remote(got.at[step - 1, way], got.at[step - 1, way], bs.at[way, step - 1], br.at[way, step - 1], me.partner).wait_recv()
                part += got[step - 1, way].astype(F32)
            if step < 7:
                sent[step, way] = part.astype(BF16)
                send(sent.at[step, way], got.at[step, way], bs.at[way, step], br.at[way, step], (me.up, me.down)[way])
            else:
                scale = jnp.tanh(jnp.full((1, 512), gate[0], F32))
                out[way * 128 : way * 128 + 128, :] = (scale * part).astype(BF16)
    for copy in sends:
        copy.wait_send()


def back(att, gate, wout, pwout):
    vmem, anyspace, smem = (pl.BlockSpec(memory_space=m) for m in (pltpu.VMEM, pl.ANY, pltpu.SMEM))
    dma = pltpu.SemaphoreType.DMA
    return pl.pallas_call(
        back_kernel,
        out_shape=jax.ShapeDtypeStruct((TOK, 512), BF16),
        in_specs=[vmem, smem, anyspace, anyspace],
        out_specs=vmem,
        scratch_shapes=[
            pltpu.VMEM((TOK, 256), BF16),
            pltpu.VMEM((8, 256, 512), BF16),
            pltpu.VMEM((8, 256, 512), BF16),
            pltpu.VMEM((7, 2, 128, 512), BF16),
            pltpu.VMEM((7, 2, 128, 512), BF16),
            dma((9,)),
            dma,
            dma,
            dma((2, 7)),
            dma((2, 7)),
        ],
        compiler_params=pltpu.CompilerParams(
            collective_id=1, has_side_effects=True, vmem_limit_bytes=48 * 2**20
        ),
        cost_estimate=pl.CostEstimate(flops=10**9, bytes_accessed=5 * 10**6, transcendentals=0),
    )(att, gate, wout, pwout)


def on_device(
    text, gain, wq, wkv, wout, qgain, kgain, gate, images, seg, owner, pos
):
    img = jnp.pad(images[0], ((0, ROWS - IMG_TOK), (0, 0)))
    q, kv, pwout = front(
        text, gain.reshape(1, -1), wq, wkv, wout, qgain.reshape(1, -1), kgain.reshape(1, -1), owner, pos, img
    )
    att = attend(q, seg.reshape(-1, 1), kv)
    return back(att, gate, wout, pwout)


def solution(mesh):
    rows = ("seq", "section")
    return jax.shard_map(
        on_device,
        mesh=mesh,
        in_specs=(
            P(rows, "tp"),
            P("tp"),
            P(None, "tp"),
            P("tp", None),
            P("tp", None),
            P(),
            P(),
            P(),
            P(rows, None, "tp"),
            P(rows),
            P(rows),
            P(rows),
        ),
        out_specs=P(rows, "tp"),
        check_vma=False,
    )
```

```python
import functools

import jax
import jax.numpy as jnp
from jax import lax
from jax.experimental import pallas as pl
from jax.experimental.pallas import tpu as pltpu
from jax.sharding import PartitionSpec as P

MESH = pl.DeviceIdType.MESH
F32, BF16 = jnp.float32, jnp.bfloat16
HD = 128
IMG_TOK = 1601
IMAGES = 16
TOK = 256
QUARTER = 416
HALF = 2 * QUARTER
ROWS = 4 * QUARTER
EPS = 1e-05
META = 2.0**-20
META_ROW = ROWS - 16

SUBS = ((0, 48, 48), (96, 80, 80), (256, 80, 80))
BODY = 768


def remote(src, dst, send, recv, device):
    return pltpu.make_async_remote_copy(
        src_ref=src, dst_ref=dst, send_sem=send, recv_sem=recv, device_id=device, device_id_type=MESH
    )


class Place:
    def __init__(self):
        seq, tp, sec = lax.axis_index("seq"), lax.axis_index("tp"), lax.axis_index("section")
        self.tp, self.z, self.c = tp, tp // 2, tp % 2
        self.x, self.y = seq // 2, sec * 2 + seq % 2
        self.partner = {"tp": self.z * 2 + 1 - self.c}
        self.up = {"tp": ((self.z + 1) % 8) * 2 + self.c}
        self.down = {"tp": ((self.z + 7) % 8) * 2 + self.c}

    def step(self, axis, delta):
        if axis == "x":
            return {"seq": ((self.x + delta) % 4) * 2 + self.y % 2}
        y = (self.y + delta) % 4
        return {"seq": self.x * 2 + y % 2, "section": y // 2}

    def image(self, dx, dy):
        y = (self.y + dy) % 4
        return ((self.x + dx) % 4) * 4 + (y % 2) * 2 + y // 2


def greet(devices):
    barrier = pltpu.get_barrier_semaphore()
    for device in devices:
        pl.semaphore_signal(barrier, inc=1, device_id=device, device_id_type=MESH)
    pl.semaphore_wait(barrier, len(devices))


def front_kernel(
    text, gain, tail, wq, wkv, wout, qgain, kgain, owner, pos, img,
    q_out, kv, pwout,
    nall, wqv, qacc, imgv, pimg, tailv, wkvv, pwkv, acck, accv, rk, rv, vfirst, mine,
    load_sem, ex_send, ex_recv, bs, br, xs, xr, ps, pr, cs, cr, as_, ar, acs, acr, ws, wr,
):
    me = Place()
    z, c = me.z, me.c
    zpar = z % 2
    loads = [
        pltpu.make_async_copy(img.at[0, pl.ds(c * HALF, BODY)], imgv.at[pl.ds(0, BODY)], load_sem.at[0]),
        pltpu.make_async_copy(wkv, wkvv, load_sem.at[1]),
    ]
    for k in range(4):
        part = pl.ds(k * 2048, 2048)
        loads.append(pltpu.make_async_copy(wq.at[part], wqv.at[part], load_sem.at[2 + k]))
    rest = pl.ds(BODY, HALF - BODY)
    load_rest = pltpu.make_async_copy(img.at[0, rest], imgv.at[rest], load_sem.at[6])
    loads[0].start()
    loads[1].start()

    @pl.when(c == 0)
    def _():
        load_rest.start()

    row = lax.broadcasted_iota(jnp.int32, (16, 512), 0)
    tailv[...] = jnp.zeros_like(tailv)
    tailv[0:16, :] = jnp.where(row == 0, tail[...].astype(F32), 0.0).astype(BF16)

    @pl.when(c == 1)
    def _():
        imgv[BODY:, :] = tailv[...]

    nall[me.tp] = (text[...].astype(F32) * gain[...].astype(F32).reshape(1, 512)).astype(BF16)
    for load in loads[2:]:
        load.start()

    greet([me.partner, me.up, me.down] + [me.step(a, d) for a in "xy" for d in (1, 3)])
    sends = []

    def send(src, dst, ssem, rsem, device):
        copy = remote(src, dst, ssem, rsem, device)
        copy.start()
        sends.append(copy)

    def arrived(ref, ssem, rsem):
        remote(ref, ref, ssem, rsem, me.partner).wait_recv()

    send(img.at[0, pl.ds((1 - c) * HALF, BODY)], pimg.at[pl.ds(0, BODY)], ex_send.at[0], ex_recv.at[0], me.partner)
    send(wkv, pwkv, ex_send.at[1], ex_recv.at[1], me.partner)
    give_rest = remote(img.at[0, rest], pimg.at[rest], ex_send.at[2], ex_recv.at[2], me.partner)
    give_tail = remote(tailv, pimg.at[rest], ex_send.at[2], ex_recv.at[2], me.partner)

    @pl.when(c == 1)
    def _():
        give_rest.start()

    @pl.when(c == 0)
    def _():
        give_tail.start()

    sends.append(give_tail)

    shard = lambda k: ((z + k % 8) % 8) * 2 + c

    def text_send(k, way, hop):
        ref = nall.at[shard(k)]
        if hop == 4:
            ref = ref.at[pl.ds(way * 128, 128)]
        send(ref, ref, as_.at[way, hop - 1], ar.at[way, hop - 1], (me.up, me.down)[way])

    def text_share(k):
        ref = nall.at[shard(k)]
        send(ref, ref, acs.at[k % 8], acr.at[k % 8], me.partner)

    def text_arrived(hop, way):
        k = -hop if way == 0 else hop
        ref = nall.at[shard(k)]
        if hop == 4:
            ref = ref.at[pl.ds(way * 128, 128)]
        arrived(ref, as_.at[way, hop - 1], ar.at[way, hop - 1])

    def text_round(hop):
        for way in (0, 1):
            text_arrived(hop, way)
            if hop < 4:
                k = -hop if way == 0 else hop
                text_send(k, way, hop + 1)
                text_share(k)
        if hop == 4:
            text_share(4)

    def text_compute():
        for k in range(8):
            ref = nall.at[((z + k) % 8) * 2 + 1 - c]
            arrived(ref, acs.at[k], acr.at[k])
        for load in loads[2:]:
            load.wait()
        qacc[...] = jnp.zeros_like(qacc)

        def use(index, carry):
            w = wqv[pl.ds(pl.multiple_of(index * 512, 512), 512), :]
            qacc[...] += jnp.dot(nall[index], w, preferred_element_type=F32)
            return carry

        lax.fori_loop(0, 16, use, 0)

    text_send(0, 0, 1)
    text_send(0, 1, 1)
    text_share(0)

    loads[0].wait()
    loads[1].wait()

    @pl.when(c == 0)
    def _():
        load_rest.wait()

    arrived(pimg.at[pl.ds(0, BODY)], ex_send.at[0], ex_recv.at[0])
    arrived(pwkv, ex_send.at[1], ex_recv.at[1])
    arrived(pimg.at[rest], ex_send.at[2], ex_recv.at[2])

    def project(k):
        d = (z + k) % 8
        rows = pl.ds(pl.multiple_of((d % 2) * QUARTER, QUARTER), QUARTER)
        cols = pl.ds(pl.multiple_of((d // 2) * 256, 256), 256)
        part = jnp.dot(imgv[rows, :], wkvv[:, cols], preferred_element_type=F32)
        part += jnp.dot(pimg[rows, :], pwkv[:, cols], preferred_element_type=F32)
        acck[d] = part[:, :HD]
        accv[d] = part[:, HD:]

    def ring_rows(u, way, stage):
        start, first, second = SUBS[u]
        if stage > 0:
            return pl.ds(start, first + second)
        return pl.ds(start, first) if way == 0 else pl.ds(start + first, second)

    def ring_send(u, stage):
        for way in (0, 1):
            rows = ring_rows(u, way, stage)
            if stage == 0:
                d = (z + 4) % 8
                vfirst[rows, :] = accv[d, rows, :].astype(BF16)
                srck, srcv = acck.at[d, rows], vfirst.at[rows]
            else:
                srck, srcv = rk.at[way, stage - 1, rows], rv.at[way, stage - 1, rows]
            device = (me.up, me.down)[way]
            send(srck, rk.at[way, stage, rows], bs.at[u, way, stage, 0], br.at[u, way, stage, 0], device)
            send(srcv, rv.at[way, stage, rows], bs.at[u, way, stage, 1], br.at[u, way, stage, 1], device)

    def ring_receive(u, stage):
        for way in (0, 1):
            rows = ring_rows(u, way, stage)
            d = (z + (3 - stage if way == 0 else 5 + stage)) % 8
            if stage == 0:
                other = ring_rows(u, 1 - way, 0)
                rk[way, 0, other, :] = acck[d, other, :]
                rv[way, 0, other, :] = accv[d, other, :].astype(BF16)
            arrived(rk.at[way, stage, rows], bs.at[u, way, stage, 0], br.at[u, way, stage, 0])
            arrived(rv.at[way, stage, rows], bs.at[u, way, stage, 1], br.at[u, way, stage, 1])
            if stage < 3:
                rk[way, stage, rows, :] += acck[d, rows, :]
                rv[way, stage, rows, :] = (rv[way, stage, rows, :].astype(F32) + accv[d, rows, :]).astype(BF16)

    def finish(u):
        start, first, second = SUBS[u]
        n = first + second
        rows = pl.ds(start, n)
        key = rk[0, 3, rows, :] + rk[1, 3, rows, :] + acck[z, rows, :]
        val = rv[0, 3, rows, :].astype(F32) + rv[1, 3, rows, :].astype(F32) + accv[z, rows, :]
        key = key * lax.rsqrt(jnp.mean(key * key, axis=-1, keepdims=True) + EPS) * kgain[...]
        if u == len(SUBS) - 1:
            row = c * HALF + zpar * QUARTER + start + lax.broadcasted_iota(jnp.int32, (n, HD), 0)
            lane = lax.broadcasted_iota(jnp.int32, (n, HD), 1)
            said = jnp.where(lane == 0, owner[0], jnp.where(lane == 1, pos[0] // 64, pos[0] % 64))
            said = jnp.where(lane < 3, said, 0).astype(F32) * META
            key = jnp.where(row >= META_ROW, said, key)
        at = pl.ds(pl.multiple_of(zpar * QUARTER + start, 16), n)
        mine[at, 0:HD] = key.astype(BF16)
        mine[at, HD:] = val.astype(BF16)
        pair = {"tp": (z + 1 - 2 * zpar) * 2 + c}
        send(mine.at[at], mine.at[at], xs.at[u], xr.at[u], pair)

    here = me.image(0, 0)

    def block(u, par, i, j, part=None):
        start, first, second = SUBS[u]
        n = first + second
        if part == 0:
            n = first
        if part == 1:
            start, n = start + first, second
        m = me.image(i, j) if par == 0 else me.image(j, i)
        r0 = pl.multiple_of(c * HALF + par * QUARTER + start, 16)
        return kv.at[m, pl.ds(r0, n)]

    def own(u, par):
        start, first, second = SUBS[u]
        return mine.at[pl.ds(par * QUARTER + start, first + second)]

    axes = lambda par: ("x", "y") if par == 0 else ("y", "x")

    def spread_first(u, par, i, way, part=None):
        slot = {(0, 0): 0, (0, 1): 1, (3, 0): 2, (1, 1): 3}[(i, way)]
        src = own(u, par) if i == 0 else block(u, par, i, 0, part)
        dst = block(u, par, i, 0, part)
        send(src, dst, ps.at[u, par, slot], pr.at[u, par, slot], me.step(axes(par)[0], (1, 3)[way]))

    def first_arrived(u, par, i, part=None):
        slot = {(3, None): 0, (1, None): 1, (2, 1): 2, (2, 0): 3}[(i, part)]
        arrived(block(u, par, i, 0, part), ps.at[u, par, slot], pr.at[u, par, slot])

    def spread_second(u, par, i, j, way):
        slot = 4 + 3 * i + (way if j == 0 else 2)
        src = own(u, par) if (i, j) == (0, 0) else block(u, par, i, j)
        send(src, block(u, par, i, j), ps.at[u, par, slot], pr.at[u, par, slot], me.step(axes(par)[1], (1, 3)[way]))

    def second_arrived(u, par, i, j):
        slot = 4 + 3 * i + {3: 0, 1: 1, 2: 2}[j]
        arrived(block(u, par, i, j), ps.at[u, par, slot], pr.at[u, par, slot])

    def share(u, par, i, j):
        src = own(u, par) if (i, j) == (0, 0) else block(u, par, i, j)
        send(src, block(u, par, i, j), cs.at[u, par, 4 * i + j], cr.at[u, par, 4 * i + j], me.partner)

    def column(u, par, i):
        spread_second(u, par, i, 0, 0)
        spread_second(u, par, i, 0, 1)
        share(u, par, i, 0)

    def column_arrived(u, par, i):
        for j, way in ((3, 0), (1, 1)):
            second_arrived(u, par, i, j)
            if (j == 3) == (i < 2):
                spread_second(u, par, i, j, way)
            share(u, par, i, j)

    local = []

    def plane_round(u, r):
        if r == 0:
            start, first, second = SUBS[u]
            at = pl.ds(pl.multiple_of((1 - zpar) * QUARTER + start, 16), first + second)
            arrived(mine.at[at], xs.at[u], xr.at[u])
        for par in (0, 1):
            if r == 0:
                spread_first(u, par, 0, 0)
                spread_first(u, par, 0, 1)
                column(u, par, 0)
                keep = pltpu.make_async_copy(own(u, par), block(u, par, 0, 0), load_sem.at[7 + 2 * u + par])
                keep.start()
                local.append(keep)
            if r == 1:
                first_arrived(u, par, 3)
                spread_first(u, par, 3, 0, 1)
                column(u, par, 3)
                first_arrived(u, par, 1)
                spread_first(u, par, 1, 1, 0)
                column(u, par, 1)
            if r == 2:
                column_arrived(u, par, 0)
            if r == 3:
                first_arrived(u, par, 2, 0)
                first_arrived(u, par, 2, 1)
                column(u, par, 2)
            if r == 4:
                column_arrived(u, par, 3)
                column_arrived(u, par, 1)
            if r == 5:
                column_arrived(u, par, 2)
            if r == 6:
                for i in (0, 3, 1, 2):
                    second_arrived(u, par, i, 2)
                    share(u, par, i, 2)

    def ring_step(u, stage):
        ring_receive(u, stage)
        if stage < 3:
            ring_send(u, stage + 1)
        else:
            finish(u)

    def project_next(n, carry):
        project(4 + jnp.where(n % 2 == 1, -((n + 1) // 2), n // 2))
        return carry

    project(4)
    ring_send(0, 0)
    lax.fori_loop(1, 8, project_next, 0)
    for k in range(8):
        src = wout.at[:, pl.ds(pl.multiple_of((2 * k + 1 - c) * 512, 512), 512)]
        send(src, pwout.at[k], ws.at[k], wr.at[k], me.partner)

    ring_step(0, 0)
    ring_send(1, 0)
    ring_step(0, 1)
    ring_step(1, 0)
    ring_send(2, 0)
    ring_step(0, 2)
    ring_step(1, 1)
    ring_step(2, 0)
    ring_step(0, 3)
    ring_step(1, 2)
    ring_step(2, 1)
    plane_round(0, 0)
    ring_step(1, 3)
    ring_step(2, 2)
    plane_round(0, 1)
    plane_round(1, 0)
    text_round(1)
    ring_step(2, 3)
    plane_round(0, 2)
    plane_round(0, 3)
    plane_round(1, 1)
    plane_round(2, 0)
    plane_round(0, 4)
    plane_round(1, 2)
    text_round(2)
    plane_round(0, 5)
    plane_round(1, 3)
    plane_round(0, 6)
    plane_round(2, 1)
    plane_round(1, 4)
    text_round(3)
    plane_round(2, 2)
    plane_round(2, 3)
    plane_round(1, 5)
    plane_round(1, 6)
    plane_round(2, 4)
    text_round(4)
    plane_round(2, 5)
    text_compute()
    for h in range(2):
        q = qacc[:, h * HD : (h + 1) * HD]
        q = q * lax.rsqrt(jnp.mean(q * q, axis=-1, keepdims=True) + EPS) * qgain[...]
        q_out[:, h * HD : (h + 1) * HD] = q.astype(BF16)

    plane_round(2, 6)
    for u, (start, first, second) in enumerate(SUBS):
        for par in (0, 1):
            for i in range(4):
                for j in range(4):
                    m = me.image(i, j) if par == 0 else me.image(j, i)
                    r0 = pl.multiple_of((1 - c) * HALF + par * QUARTER + start, 16)
                    ref = kv.at[m, pl.ds(r0, first + second)]
                    arrived(ref, cs.at[u, par, 4 * i + j], cr.at[u, par, 4 * i + j])
    for k in range(8):
        arrived(pwout.at[k], ws.at[k], wr.at[k])
    for keep in local:
        keep.wait()
    for copy in sends:
        copy.wait_send()


def front(text, gain, tail, wq, wkv, wout, qgain, kgain, owner, pos, img):
    vmem, anyspace, smem = (pl.BlockSpec(memory_space=m) for m in (pltpu.VMEM, pl.ANY, pltpu.SMEM))
    dma = pltpu.SemaphoreType.DMA
    n = len(SUBS)
    return pl.pallas_call(
        front_kernel,
        out_shape=(
            jax.ShapeDtypeStruct((TOK, 256), BF16),
            jax.ShapeDtypeStruct((IMAGES, ROWS, 256), BF16),
            jax.ShapeDtypeStruct((8, 256, 512), BF16),
        ),
        in_specs=[vmem, vmem, vmem, anyspace, anyspace, anyspace, vmem, vmem, smem, smem, anyspace],
        out_specs=(vmem, anyspace, anyspace),
        scratch_shapes=[
            pltpu.VMEM((16, TOK, 512), BF16),
            pltpu.VMEM((8192, 256), BF16),
            pltpu.VMEM((TOK, 256), F32),
            pltpu.VMEM((HALF, 512), BF16),
            pltpu.VMEM((HALF, 512), BF16),
            pltpu.VMEM((HALF - BODY, 512), BF16),
            pltpu.VMEM((512, 1024), BF16),
            pltpu.VMEM((512, 1024), BF16),
            pltpu.VMEM((8, QUARTER, HD), F32),
            pltpu.VMEM((8, QUARTER, HD), F32),
            pltpu.VMEM((2, 4, QUARTER, HD), F32),
            pltpu.VMEM((2, 4, QUARTER, HD), BF16),
            pltpu.VMEM((QUARTER, HD), BF16),
            pltpu.VMEM((HALF, 256), BF16),
            dma((7 + 2 * n,)),
            dma((3,)),
            dma((3,)),
            dma((n, 2, 4, 2)),
            dma((n, 2, 4, 2)),
            dma((n,)),
            dma((n,)),
            dma((n, 2, 16)),
            dma((n, 2, 16)),
            dma((n, 2, 16)),
            dma((n, 2, 16)),
            dma((2, 4)),
            dma((2, 4)),
            dma((8,)),
            dma((8,)),
            dma((8,)),
            dma((8,)),
        ],
        compiler_params=pltpu.CompilerParams(
            collective_id=0, has_side_effects=True, vmem_limit_bytes=56 * 2**20
        ),
        cost_estimate=pl.CostEstimate(flops=5 * 10**9, bytes_accessed=3 * 10**7, transcendentals=0),
    )(text, gain, tail, wq, wkv, wout, qgain, kgain, owner, pos, img)


TILES = ((0, 256), (256, 256), (512, 256), (768, 256), (1024, 256), (1280, 256), (1536, 128))


def attend_kernel(q, seg, kv, out, meta, kbuf, vbuf, wexp, total, seen, sem, meta_sem):
    first = (lax.axis_index("seq") * 2 + lax.axis_index("section")) * TOK
    fetch = pltpu.make_async_copy(kv.at[:, pl.ds(META_ROW, 16), pl.ds(0, HD)], meta, meta_sem)
    fetch.start()
    total[...] = jnp.zeros_like(total)
    row = lax.broadcasted_iota(jnp.int32, (ROWS, HD), 0)
    ones = jnp.where(row < IMG_TOK, 1.0, 0.0).astype(BF16)
    vbuf[0, :, HD:] = ones
    vbuf[1, :, HD:] = ones
    fetch.wait()
    places = (first + lax.broadcasted_iota(jnp.int32, (TOK, 1), 0)).astype(F32)
    docs = jnp.broadcast_to(seg[...].astype(F32).reshape(1, TOK), (HD, TOK)).T[:, 0:1]

    def sees(m):
        said = meta[m, 0:1, :].astype(F32) * (1.0 / META)
        lane = lax.broadcasted_iota(jnp.int32, (1, HD), 1)
        doc = jnp.sum(jnp.where(lane == 0, said, 0.0), axis=1, keepdims=True)
        weight = jnp.where(lane == 1, 64.0, jnp.where(lane == 2, 1.0, 0.0))
        start = jnp.sum(said * weight, axis=1, keepdims=True)
        return (docs == doc) & (places >= start)

    def look(m, count):
        flag = jnp.max(jnp.where(sees(m), 1.0, 0.0)) > 0.5

        @pl.when(flag)
        def _():
            seen[count] = m

        return count + flag.astype(jnp.int32)

    count = lax.fori_loop(0, IMAGES, look, jnp.int32(0))

    def copies(n):
        slot = n % 2
        m = seen[n]
        return (
            pltpu.make_async_copy(kv.at[m, :, pl.ds(0, HD)], kbuf.at[slot], sem.at[slot, 0]),
            pltpu.make_async_copy(kv.at[m, :, pl.ds(HD, HD)], vbuf.at[slot, :, pl.ds(0, HD)], sem.at[slot, 1]),
        )

    @pl.when(count > 0)
    def _():
        for copy in copies(0):
            copy.start()

    rows = jnp.concatenate([q[:, :HD], q[:, HD:]], axis=0)

    def image(n, carry):
        slot = n % 2

        @pl.when(n + 1 < count)
        def _():
            for copy in copies(n + 1):
                copy.start()

        for copy in copies(n):
            copy.wait()
        for k0, width in TILES:
            score = lax.dot_general(
                rows, kbuf[slot, k0 : k0 + width, :], (((1,), (1,)), ((), ())), preferred_element_type=F32
            )
            wexp[:, k0 : k0 + width] = jnp.exp2(score * (HD**-0.5 * 1.4426950408889634)).astype(BF16)
        term = jnp.dot(wexp[...], vbuf[slot], preferred_element_type=F32)
        mask = sees(seen[n])
        total[0:TOK, :] += jnp.where(mask, term[:TOK], 0.0)
        total[TOK:, :] += jnp.where(mask, term[TOK:], 0.0)
        return carry

    lax.fori_loop(0, count, image, 0)
    for h in range(2):
        part = total[h * TOK : (h + 1) * TOK, :]
        out[:, h * HD : (h + 1) * HD] = (part[:, :HD] / jnp.maximum(part[:, HD:], 1.0)).astype(BF16)


def attend(q, seg, kv):
    vmem, anyspace = (pl.BlockSpec(memory_space=m) for m in (pltpu.VMEM, pl.ANY))
    return pl.pallas_call(
        attend_kernel,
        out_shape=jax.ShapeDtypeStruct((TOK, 256), BF16),
        in_specs=[vmem, vmem, anyspace],
        out_specs=vmem,
        scratch_shapes=[
            pltpu.VMEM((IMAGES, 16, HD), BF16),
            pltpu.VMEM((2, ROWS, HD), BF16),
            pltpu.VMEM((2, ROWS, 256), BF16),
            pltpu.VMEM((2 * TOK, ROWS), BF16),
            pltpu.VMEM((2 * TOK, 256), F32),
            pltpu.SMEM((IMAGES,), jnp.int32),
            pltpu.SemaphoreType.DMA((2, 2)),
            pltpu.SemaphoreType.DMA,
        ],
        compiler_params=pltpu.CompilerParams(vmem_limit_bytes=48 * 2**20),
        cost_estimate=pl.CostEstimate(flops=5 * 10**9, bytes_accessed=10**7, transcendentals=5 * 10**6),
    )(q, seg, kv)


def back_kernel(att, gate, wout, pwout, out, patt, wo, pwo, terms, got, sent, load_sem, e_send, e_recv, bs, br):
    me = Place()
    z, c = me.z, me.c
    loads = []
    for n in range(8):
        k = (z + 4 + n) % 8
        src = wout.at[:, pl.ds(pl.multiple_of((2 * k + c) * 512, 512), 512)]
        loads.append(pltpu.make_async_copy(src, wo.at[k], load_sem.at[0, n]))
        loads.append(pltpu.make_async_copy(pwout.at[k], pwo.at[k], load_sem.at[1, n]))
    for load in loads:
        load.start()
    greet([me.partner, me.up, me.down])
    sends = []

    def send(src, dst, ssem, rsem, device):
        copy = remote(src, dst, ssem, rsem, device)
        copy.start()
        sends.append(copy)

    send(att, patt, e_send, e_recv, me.partner)

    def term(d):
        part = jnp.dot(att[...], wo[d], preferred_element_type=F32)
        terms[d] = part + jnp.dot(patt[...], pwo[d], preferred_element_type=F32)

    def place(e, way, stage):
        cols = pl.ds(e * 256, 256)
        return (pl.ds(way * 128, 128) if stage == 0 else pl.ds(0, TOK)), cols

    def ring_send(e, stage):
        for way in (0, 1):
            rows, cols = place(e, way, stage)
            d = (z + (4 - stage if way == 0 else 4 + stage)) % 8
            part = terms[d, :, cols]
            if stage == 0:
                part = part[way * 128 : way * 128 + 128]
            elif stage == 1:
                half = got[way, 0, way * 128 : way * 128 + 128, cols].astype(F32)
                parts = [part[:128], part[128:]]
                parts[way] += half
                part = jnp.concatenate(parts, axis=0)
            else:
                part += got[way, stage - 1, :, cols].astype(F32)
            sent[way, stage, rows, cols] = part.astype(BF16)
            send(
                sent.at[way, stage, rows, cols], got.at[way, stage, rows, cols],
                bs.at[e, way, stage], br.at[e, way, stage], (me.up, me.down)[way],
            )

    def ring_arrived(e, stage):
        for way in (0, 1):
            rows, cols = place(e, way, stage)
            ref = got.at[way, stage, rows, cols]
            remote(ref, ref, bs.at[e, way, stage], br.at[e, way, stage], me.partner).wait_recv()

    for load in loads[:2]:
        load.wait()
    remote(att, patt, e_send, e_recv, me.partner).wait_recv()
    term((z + 4) % 8)
    ring_send(0, 0)
    ring_send(1, 0)
    for load in loads[2:]:
        load.wait()

    def next_term(n, carry):
        term((z + 4 + jnp.where(n % 2 == 1, -((n + 1) // 2), n // 2)) % 8)
        return carry

    lax.fori_loop(1, 8, next_term, 0)
    for stage in range(3):
        for e in (0, 1):
            ring_arrived(e, stage)
            ring_send(e, stage + 1)
    scale = jnp.tanh(jnp.full((1, 256), gate[0], F32))
    for e in (0, 1):
        ring_arrived(e, 3)
        cols = pl.ds(e * 256, 256)
        part = terms[z, :, cols] + got[0, 3, :, cols].astype(F32) + got[1, 3, :, cols].astype(F32)
        out[:, e * 256 : e * 256 + 256] = (scale * part).astype(BF16)
    for copy in sends:
        copy.wait_send()


def back(att, gate, wout, pwout):
    vmem, anyspace, smem = (pl.BlockSpec(memory_space=m) for m in (pltpu.VMEM, pl.ANY, pltpu.SMEM))
    dma = pltpu.SemaphoreType.DMA
    return pl.pallas_call(
        back_kernel,
        out_shape=jax.ShapeDtypeStruct((TOK, 512), BF16),
        in_specs=[vmem, smem, anyspace, anyspace],
        out_specs=vmem,
        scratch_shapes=[
            pltpu.VMEM((TOK, 256), BF16),
            pltpu.VMEM((8, 256, 512), BF16),
            pltpu.VMEM((8, 256, 512), BF16),
            pltpu.VMEM((8, TOK, 512), F32),
            pltpu.VMEM((2, 4, TOK, 512), BF16),
            pltpu.VMEM((2, 4, TOK, 512), BF16),
            dma((2, 8)),
            dma,
            dma,
            dma((2, 2, 4)),
            dma((2, 2, 4)),
        ],
        compiler_params=pltpu.CompilerParams(
            collective_id=1, has_side_effects=True, vmem_limit_bytes=48 * 2**20
        ),
        cost_estimate=pl.CostEstimate(flops=10**9, bytes_accessed=5 * 10**6, transcendentals=0),
    )(att, gate, wout, pwout)


def on_device(
    text, gain, wq, wkv, wout, qgain, kgain, gate, images, seg, owner, pos
):
    q, kv, pwout = front(
        text, gain, images[0, IMG_TOK - 1 :], wq, wkv, wout, qgain.reshape(1, -1), kgain.reshape(1, -1), owner, pos, images
    )
    att = attend(q, seg, kv)
    return back(att, gate, wout, pwout)


def solution(mesh):
    rows = ("seq", "section")
    return jax.shard_map(
        on_device,
        mesh=mesh,
        in_specs=(
            P(rows, "tp"),
            P("tp"),
            P(None, "tp"),
            P("tp", None),
            P("tp", None),
            P(),
            P(),
            P(),
            P(rows, None, "tp"),
            P(rows),
            P(rows),
            P(rows),
        ),
        out_specs=P(rows, "tp"),
        check_vma=False,
    )
```

```python
import jax
import jax.numpy as jnp
from jax import lax
from jax.experimental import pallas as pl
from jax.experimental.pallas import tpu as pltpu
from jax.sharding import PartitionSpec as P

MESH = pl.DeviceIdType.MESH
F32, BF16 = jnp.float32, jnp.bfloat16
HD = 128
IMG_TOK = 1601
IMAGES = 16
TOK = 256
QUARTER = 416
HALF = 2 * QUARTER
ROWS = 4 * QUARTER
EPS = 1e-05
META = 2.0**-40
META_ROW = ROWS - 16
VALID = 3 * 96 + IMG_TOK - 3 * QUARTER - 320

SUBS = ((320, 48, 48), (0, 112, 112), (224, 48, 48))
BODY = 768


def remote(src, dst, send, recv, device):
    return pltpu.make_async_remote_copy(
        src_ref=src, dst_ref=dst, send_sem=send, recv_sem=recv, device_id=device, device_id_type=MESH
    )


class Place:
    def __init__(self):
        seq, tp, sec = lax.axis_index("seq"), lax.axis_index("tp"), lax.axis_index("section")
        self.tp, self.z, self.c = tp, tp // 2, tp % 2
        self.x, self.y = seq // 2, sec * 2 + seq % 2
        self.partner = {"tp": self.z * 2 + 1 - self.c}
        self.up = {"tp": ((self.z + 1) % 8) * 2 + self.c}
        self.down = {"tp": ((self.z + 7) % 8) * 2 + self.c}

    def step(self, axis, delta):
        if axis == "x":
            return {"seq": ((self.x + delta) % 4) * 2 + self.y % 2}
        y = (self.y + delta) % 4
        return {"seq": self.x * 2 + y % 2, "section": y // 2}

    def image(self, dx, dy):
        y = (self.y + dy) % 4
        return ((self.x + dx) % 4) * 4 + (y % 2) * 2 + y // 2


NEAR = ((0, 0), (1, 0), (3, 0), (0, 1), (0, 3))
DIAGONAL = ((1, 1), (1, 3), (3, 1), (3, 3))
FAR = ((2, 0), (0, 2), (2, 1), (2, 3), (1, 2), (3, 2), (2, 2))


def greet(devices):
    barrier = pltpu.get_barrier_semaphore()
    for device in devices:
        pl.semaphore_signal(barrier, inc=1, device_id=device, device_id_type=MESH)
    pl.semaphore_wait(barrier, len(devices))


def kernel(
    text, gain, tail, wq, wkv, wout, qgain, kgain, gate, owner, pos, seg, img,
    out,
    nall, wqv, qacc, imgv, pimg, tailv, wkvv, pwkv, acck, accv, rk, rv, vfirst, mine,
    kv, qrows, wexp, total, mass, att, patt, wo, pwo, terms, got, sent,
    load_sem, ex_send, ex_recv, bs, br, xs, xr, ps, pr, cs, cr, as_, ar, acs, acr, ws, wr,
    wo_sem, es, er, ds, dr,
):
    me = Place()
    z, c = me.z, me.c
    zpar = z % 2
    loads = [
        pltpu.make_async_copy(img.at[0, pl.ds(c * HALF, BODY)], imgv.at[pl.ds(0, BODY)], load_sem.at[0]),
        pltpu.make_async_copy(wkv, wkvv, load_sem.at[1]),
    ]
    for k in range(4):
        part = pl.ds(k * 2048, 2048)
        loads.append(pltpu.make_async_copy(wq.at[part], wqv.at[part], load_sem.at[2 + k]))
    rest = pl.ds(BODY, HALF - BODY)
    load_rest = pltpu.make_async_copy(img.at[0, rest], imgv.at[rest], load_sem.at[6])
    loads[0].start()
    loads[1].start()

    @pl.when(c == 0)
    def _():
        load_rest.start()

    row = lax.broadcasted_iota(jnp.int32, (16, 512), 0)
    tailv[...] = jnp.zeros_like(tailv)
    tailv[0:16, :] = jnp.where(row == 0, tail[...].astype(F32), 0.0).astype(BF16)

    @pl.when(c == 1)
    def _():
        imgv[BODY:, :] = tailv[...]

    nall[me.tp] = (text[...].astype(F32) * gain[...].astype(F32).reshape(1, 512)).astype(BF16)
    for load in loads[2:6]:
        load.start()

    greet([me.partner, me.up, me.down] + [me.step(a, d) for a in "xy" for d in (1, 3)])
    sends = []

    def send(src, dst, ssem, rsem, device):
        copy = remote(src, dst, ssem, rsem, device)
        copy.start()
        sends.append(copy)

    def arrived(ref, ssem, rsem):
        remote(ref, ref, ssem, rsem, me.partner).wait_recv()

    send(img.at[0, pl.ds((1 - c) * HALF, BODY)], pimg.at[pl.ds(0, BODY)], ex_send.at[0], ex_recv.at[0], me.partner)
    send(wkv, pwkv, ex_send.at[1], ex_recv.at[1], me.partner)
    give_rest = remote(img.at[0, rest], pimg.at[rest], ex_send.at[2], ex_recv.at[2], me.partner)
    give_tail = remote(tailv, pimg.at[rest], ex_send.at[2], ex_recv.at[2], me.partner)

    @pl.when(c == 1)
    def _():
        give_rest.start()

    @pl.when(c == 0)
    def _():
        give_tail.start()

    sends.append(give_tail)

    shard = lambda k: ((z + k % 8) % 8) * 2 + c

    def text_send(k, way, hop):
        ref = nall.at[shard(k)]
        if hop == 4:
            ref = ref.at[pl.ds(way * 128, 128)]
        send(ref, ref, as_.at[way, hop - 1], ar.at[way, hop - 1], (me.up, me.down)[way])

    def text_share(k):
        ref = nall.at[shard(k)]
        send(ref, ref, acs.at[k % 8], acr.at[k % 8], me.partner)

    def text_arrived(hop, way):
        k = -hop if way == 0 else hop
        ref = nall.at[shard(k)]
        if hop == 4:
            ref = ref.at[pl.ds(way * 128, 128)]
        arrived(ref, as_.at[way, hop - 1], ar.at[way, hop - 1])

    def text_round(hop):
        for way in (0, 1):
            text_arrived(hop, way)
            if hop < 4:
                k = -hop if way == 0 else hop
                text_send(k, way, hop + 1)
                text_share(k)
        if hop == 4:
            text_share(4)

    def text_compute():
        for k in range(8):
            ref = nall.at[((z + k) % 8) * 2 + 1 - c]
            arrived(ref, acs.at[k], acr.at[k])
        for load in loads[2:6]:
            load.wait()
        qacc[...] = jnp.zeros_like(qacc)

        def use(index, carry):
            w = wqv[pl.ds(pl.multiple_of(index * 512, 512), 512), :]
            qacc[...] += jnp.dot(nall[index], w, preferred_element_type=F32)
            return carry

        lax.fori_loop(0, 16, use, 0)
        for h in range(2):
            q = qacc[:, h * HD : (h + 1) * HD]
            q = q * lax.rsqrt(jnp.mean(q * q, axis=-1, keepdims=True) + EPS) * qgain[...]
            qrows[h * TOK : (h + 1) * TOK, :] = q.astype(BF16)

    text_send(0, 0, 1)
    text_send(0, 1, 1)
    text_share(0)

    loads[0].wait()
    loads[1].wait()

    @pl.when(c == 0)
    def _():
        load_rest.wait()

    arrived(pimg.at[pl.ds(0, BODY)], ex_send.at[0], ex_recv.at[0])
    arrived(pwkv, ex_send.at[1], ex_recv.at[1])
    arrived(pimg.at[rest], ex_send.at[2], ex_recv.at[2])

    def project(d):
        rows = pl.ds(pl.multiple_of((d % 2) * QUARTER, QUARTER), QUARTER)
        cols = pl.ds(pl.multiple_of((d // 2) * 256, 256), 256)
        part = jnp.dot(imgv[rows, :], wkvv[:, cols], preferred_element_type=F32)
        part += jnp.dot(pimg[rows, :], pwkv[:, cols], preferred_element_type=F32)
        acck[d] = part[:, :HD]
        accv[d] = part[:, HD:]

    def ring_rows(u, way, stage):
        start, first, second = SUBS[u]
        if stage > 0:
            return pl.ds(start, first + second)
        return pl.ds(start, first) if way == 0 else pl.ds(start + first, second)

    def ring_send(u, stage):
        for way in (0, 1):
            rows = ring_rows(u, way, stage)
            if stage == 0:
                d = (z + 4) % 8
                vfirst[rows, :] = accv[d, rows, :].astype(BF16)
                srck, srcv = acck.at[d, rows], vfirst.at[rows]
            else:
                srck, srcv = rk.at[way, stage - 1, rows], rv.at[way, stage - 1, rows]
            device = (me.up, me.down)[way]
            send(srck, rk.at[way, stage, rows], bs.at[u, way, stage, 0], br.at[u, way, stage, 0], device)
            send(srcv, rv.at[way, stage, rows], bs.at[u, way, stage, 1], br.at[u, way, stage, 1], device)

    def ring_receive(u, stage):
        for way in (0, 1):
            rows = ring_rows(u, way, stage)
            d = (z + (3 - stage if way == 0 else 5 + stage)) % 8
            if stage == 0:
                other = ring_rows(u, 1 - way, 0)
                rk[way, 0, other, :] = acck[d, other, :]
                rv[way, 0, other, :] = accv[d, other, :].astype(BF16)
            arrived(rk.at[way, stage, rows], bs.at[u, way, stage, 0], br.at[u, way, stage, 0])
            arrived(rv.at[way, stage, rows], bs.at[u, way, stage, 1], br.at[u, way, stage, 1])
            if stage < 3:
                rk[way, stage, rows, :] += acck[d, rows, :]
                rv[way, stage, rows, :] = (rv[way, stage, rows, :].astype(F32) + accv[d, rows, :]).astype(BF16)

    def finish(u):
        start, first, second = SUBS[u]
        n = first + second
        rows = pl.ds(start, n)
        key = rk[0, 3, rows, :] + rk[1, 3, rows, :] + acck[z, rows, :]
        val = rv[0, 3, rows, :].astype(F32) + rv[1, 3, rows, :].astype(F32) + accv[z, rows, :]
        key = key * lax.rsqrt(jnp.mean(key * key, axis=-1, keepdims=True) + EPS) * kgain[...]
        if u == 0:
            row = c * HALF + zpar * QUARTER + start + lax.broadcasted_iota(jnp.int32, (n, HD), 0)
            lane = lax.broadcasted_iota(jnp.int32, (n, HD), 1)
            said = jnp.where(lane == 0, owner[0], jnp.where(lane == 1, pos[0] // 64, pos[0] % 64))
            said = jnp.where(lane < 3, said, 0).astype(F32) * META
            key = jnp.where(row >= META_ROW, said, key)
        at = pl.ds(pl.multiple_of(zpar * QUARTER + start, 16), n)
        mine[at, 0:HD] = key.astype(BF16)
        mine[at, HD:] = val.astype(BF16)
        pair = {"tp": (z + 1 - 2 * zpar) * 2 + c}
        send(mine.at[at], mine.at[at], xs.at[u], xr.at[u], pair)

    here = me.image(0, 0)

    def block(u, par, i, j, part=None):
        start, first, second = SUBS[u]
        n = first + second
        if part == 0:
            n = first
        if part == 1:
            start, n = start + first, second
        m = me.image(i, j) if par == 0 else me.image(j, i)
        r0 = pl.multiple_of(c * HALF + par * QUARTER + start, 16)
        return kv.at[m, pl.ds(r0, n)]

    def own(u, par):
        start, first, second = SUBS[u]
        return mine.at[pl.ds(par * QUARTER + start, first + second)]

    axes = lambda par: ("x", "y") if par == 0 else ("y", "x")

    def spread_first(u, par, i, way, part=None):
        slot = {(0, 0): 0, (0, 1): 1, (3, 0): 2, (1, 1): 3}[(i, way)]
        src = own(u, par) if i == 0 else block(u, par, i, 0, part)
        dst = block(u, par, i, 0, part)
        send(src, dst, ps.at[u, par, slot], pr.at[u, par, slot], me.step(axes(par)[0], (1, 3)[way]))

    def first_arrived(u, par, i, part=None):
        slot = {(3, None): 0, (1, None): 1, (2, 1): 2, (2, 0): 3}[(i, part)]
        arrived(block(u, par, i, 0, part), ps.at[u, par, slot], pr.at[u, par, slot])

    def spread_second(u, par, i, j, way):
        slot = 4 + 3 * i + (way if j == 0 else 2)
        src = own(u, par) if (i, j) == (0, 0) else block(u, par, i, j)
        send(src, block(u, par, i, j), ps.at[u, par, slot], pr.at[u, par, slot], me.step(axes(par)[1], (1, 3)[way]))

    def second_arrived(u, par, i, j):
        slot = 4 + 3 * i + {3: 0, 1: 1, 2: 2}[j]
        arrived(block(u, par, i, j), ps.at[u, par, slot], pr.at[u, par, slot])

    def share(u, par, i, j):
        src = own(u, par) if (i, j) == (0, 0) else block(u, par, i, j)
        send(src, block(u, par, i, j), cs.at[u, par, 4 * i + j], cr.at[u, par, 4 * i + j], me.partner)

    def column(u, par, i):
        spread_second(u, par, i, 0, 0)
        spread_second(u, par, i, 0, 1)
        share(u, par, i, 0)

    def column_arrived(u, par, i):
        for j, way in ((3, 0), (1, 1)):
            second_arrived(u, par, i, j)
            if (j == 3) == (i < 2):
                spread_second(u, par, i, j, way)
            share(u, par, i, j)


    def plane_round(u, r):
        if r == 0:
            start, first, second = SUBS[u]
            at = pl.ds(pl.multiple_of((1 - zpar) * QUARTER + start, 16), first + second)
            arrived(mine.at[at], xs.at[u], xr.at[u])
        for par in (0, 1):
            if r == 0:
                spread_first(u, par, 0, 0)
                spread_first(u, par, 0, 1)
                column(u, par, 0)
                start, first, second = SUBS[u]
                r0 = pl.multiple_of(c * HALF + par * QUARTER + start, 16)
                kv[here, pl.ds(r0, first + second), :] = mine[par * QUARTER + start : par * QUARTER + start + first + second, :]
            if r == 1:
                first_arrived(u, par, 3)
                spread_first(u, par, 3, 0, 1)
                column(u, par, 3)
                first_arrived(u, par, 1)
                spread_first(u, par, 1, 1, 0)
                column(u, par, 1)
            if r == 2:
                column_arrived(u, par, 0)
            if r == 3:
                first_arrived(u, par, 2, 0)
                first_arrived(u, par, 2, 1)
                column(u, par, 2)
            if r == 4:
                column_arrived(u, par, 3)
                column_arrived(u, par, 1)
            if r == 5:
                column_arrived(u, par, 2)
            if r == 6:
                for i in (0, 3, 1, 2):
                    second_arrived(u, par, i, 2)
                    share(u, par, i, 2)

    docs = jnp.broadcast_to(seg[...].astype(F32).reshape(1, TOK), (HD, TOK)).T[:, 0:1]
    places = ((me.x * 4 + me.y % 2 * 2 + me.y // 2) * TOK + lax.broadcasted_iota(jnp.int32, (TOK, 1), 0)).astype(F32)
    total[...] = jnp.zeros_like(total)
    mass[...] = jnp.zeros_like(mass)

    def attend_image(u, m):
        start, first, second = SUBS[u]
        n = first + second
        parts = [kv[m, q * QUARTER + start : q * QUARTER + start + n, :] for q in range(4)]
        keys = jnp.concatenate([p[:, :HD] for p in parts], axis=0)
        values = jnp.concatenate([p[:, HD:] for p in parts], axis=0)
        weight = jnp.zeros((2 * TOK, HD), F32)
        rows = qrows[...]
        for k0 in range(0, 4 * n, 256):
            width = min(256, 4 * n - k0)
            score = lax.dot_general(
                rows, keys[k0 : k0 + width, :], (((1,), (1,)), ((), ())), preferred_element_type=F32
            )
            expo = jnp.exp2(score * (HD**-0.5 * 1.4426950408889634))
            if u == 0 and k0 + width > VALID:
                lane = k0 + lax.broadcasted_iota(jnp.int32, expo.shape, 1)
                expo = jnp.where(lane < VALID, expo, 0.0)
            for lanes in range(0, width, HD):
                weight += expo[:, lanes : lanes + HD]
            wexp[:, k0 : k0 + width] = expo.astype(BF16)
        term = jnp.dot(wexp[:, 0 : 4 * n], values, preferred_element_type=F32)
        said = kv[m, META_ROW : META_ROW + 16, 0:HD].astype(F32)[0:1, :] * (1.0 / META)
        lane = lax.broadcasted_iota(jnp.int32, (1, HD), 1)
        doc = jnp.sum(jnp.where(lane == 0, said, 0.0), axis=1, keepdims=True)
        scale = jnp.where(lane == 1, 64.0, jnp.where(lane == 2, 1.0, 0.0))
        mask = (docs == doc) & (places >= jnp.sum(said * scale, axis=1, keepdims=True))
        for h in range(2):
            at = slice(h * TOK, (h + 1) * TOK)
            total[at, :] += jnp.where(mask, term[at], 0.0)
            mass[at, :] += jnp.where(mask, weight[at], 0.0)

    def attend(u, images):
        start, first, second = SUBS[u]
        for dx, dy in images:
            for par, i, j in ((0, dx, dy), (1, dy, dx)):
                r0 = pl.multiple_of((1 - c) * HALF + par * QUARTER + start, 16)
                ref = kv.at[me.image(dx, dy), pl.ds(r0, first + second)]
                arrived(ref, cs.at[u, par, 4 * i + j], cr.at[u, par, 4 * i + j])
        codes = [4 * dx + dy for dx, dy in images]

        def one(n, carry):
            code = codes[0]
            for k in range(1, len(codes)):
                code = jnp.where(n == k, codes[k], code)
            attend_image(u, me.image(code // 4, code % 4))
            return carry

        lax.fori_loop(0, len(codes), one, 0)

    def ring_step(u, stage):
        ring_receive(u, stage)
        if stage < 3:
            ring_send(u, stage + 1)
        else:
            finish(u)

    def order(n):
        return (z + 4 + jnp.where(n % 2 == 1, -((n + 1) // 2), n // 2)) % 8

    def project_next(n, carry):
        project(order(n))
        return carry

    project((z + 4) % 8)
    ring_send(0, 0)
    lax.fori_loop(1, 8, project_next, 0)
    for k in range(8):
        src = wout.at[:, pl.ds(pl.multiple_of((2 * k + 1 - c) * 512, 512), 512)]
        send(src, pwo.at[k], ws.at[k], wr.at[k], me.partner)
        src = wout.at[:, pl.ds(pl.multiple_of((2 * k + c) * 512, 512), 512)]
        load = pltpu.make_async_copy(src, wo.at[k], wo_sem.at[k])
        load.start()
        loads.append(load)

    ring_step(0, 0)
    ring_send(1, 0)
    ring_step(0, 1)
    ring_step(1, 0)
    ring_send(2, 0)
    ring_step(0, 2)
    ring_step(1, 1)
    ring_step(2, 0)
    ring_step(0, 3)
    ring_step(1, 2)
    ring_step(2, 1)
    plane_round(0, 0)
    ring_step(1, 3)
    ring_step(2, 2)
    plane_round(0, 1)
    plane_round(1, 0)
    text_round(1)
    ring_step(2, 3)
    plane_round(0, 2)
    plane_round(0, 3)
    plane_round(2, 0)
    plane_round(0, 4)
    plane_round(0, 5)
    text_round(2)
    plane_round(0, 6)
    plane_round(1, 1)
    text_round(3)
    plane_round(1, 2)
    text_round(4)
    plane_round(1, 3)
    text_compute()
    attend(0, NEAR)
    plane_round(1, 4)
    attend(0, DIAGONAL)
    plane_round(2, 1)
    attend(0, FAR)
    plane_round(1, 5)
    attend(1, NEAR)
    plane_round(2, 2)
    plane_round(1, 6)
    plane_round(2, 3)
    attend(1, DIAGONAL)
    plane_round(2, 4)
    plane_round(2, 5)
    attend(1, FAR)
    attend(2, NEAR)
    attend(2, DIAGONAL)
    plane_round(2, 6)
    attend(2, FAR)

    for h in range(2):
        rows = slice(h * TOK, (h + 1) * TOK)
        weight = jnp.maximum(jnp.sum(mass[rows, :], axis=1, keepdims=True), 1.0)
        att[:, h * HD : (h + 1) * HD] = (total[rows, :] / weight).astype(BF16)

    send(att, patt, es, er, me.partner)

    def term(d):
        part = jnp.dot(att[...], wo[d], preferred_element_type=F32)
        terms[d] = part + jnp.dot(patt[...], pwo[d], preferred_element_type=F32)

    def next_term(n, carry):
        term(order(n))
        return carry

    def term_rows(way, stage):
        return pl.ds(way * 128, 128) if stage == 0 else pl.ds(0, TOK)

    def term_send(e, stage):
        cols = pl.ds(e * 256, 256)
        for way in (0, 1):
            rows = term_rows(way, stage)
            part = terms[(z + (4 - stage if way == 0 else 4 + stage)) % 8, :, cols]
            if stage == 0:
                part = part[way * 128 : way * 128 + 128]
            elif stage == 1:
                parts = [part[:128], part[128:]]
                parts[way] += got[way, 0, way * 128 : way * 128 + 128, cols].astype(F32)
                part = jnp.concatenate(parts, axis=0)
            else:
                part += got[way, stage - 1, :, cols].astype(F32)
            sent[way, stage, rows, cols] = part.astype(BF16)
            send(
                sent.at[way, stage, rows, cols], got.at[way, stage, rows, cols],
                ds.at[e, way, stage], dr.at[e, way, stage], (me.up, me.down)[way],
            )

    def term_arrived(e, stage):
        for way in (0, 1):
            ref = got.at[way, stage, term_rows(way, stage), pl.ds(e * 256, 256)]
            arrived(ref, ds.at[e, way, stage], dr.at[e, way, stage])

    for k in range(8):
        arrived(pwo.at[k], ws.at[k], wr.at[k])
    for load in loads[6:]:
        load.wait()
    arrived(patt, es, er)
    term((z + 4) % 8)
    term_send(0, 0)
    term_send(1, 0)
    lax.fori_loop(1, 8, next_term, 0)
    for stage in range(3):
        for e in (0, 1):
            term_arrived(e, stage)
            term_send(e, stage + 1)
    scale = jnp.tanh(jnp.full((1, 256), gate[0], F32))
    for e in (0, 1):
        term_arrived(e, 3)
        cols = pl.ds(e * 256, 256)
        part = terms[z, :, cols] + got[0, 3, :, cols].astype(F32) + got[1, 3, :, cols].astype(F32)
        out[:, e * 256 : e * 256 + 256] = (scale * part).astype(BF16)

    for copy in sends:
        copy.wait_send()


def fused(*args):
    vmem, anyspace, smem = (pl.BlockSpec(memory_space=m) for m in (pltpu.VMEM, pl.ANY, pltpu.SMEM))
    dma = pltpu.SemaphoreType.DMA
    n = len(SUBS)
    return pl.pallas_call(
        kernel,
        out_shape=jax.ShapeDtypeStruct((TOK, 512), BF16),
        in_specs=[vmem, vmem, vmem, anyspace, anyspace, anyspace, vmem, vmem, smem, smem, smem, vmem, anyspace],
        out_specs=vmem,
        scratch_shapes=[
            pltpu.VMEM((16, TOK, 512), BF16),
            pltpu.VMEM((8192, 256), BF16),
            pltpu.VMEM((TOK, 256), F32),
            pltpu.VMEM((HALF, 512), BF16),
            pltpu.VMEM((HALF, 512), BF16),
            pltpu.VMEM((HALF - BODY, 512), BF16),
            pltpu.VMEM((512, 1024), BF16),
            pltpu.VMEM((512, 1024), BF16),
            pltpu.VMEM((8, QUARTER, HD), F32),
            pltpu.VMEM((8, QUARTER, HD), F32),
            pltpu.VMEM((2, 4, QUARTER, HD), F32),
            pltpu.VMEM((2, 4, QUARTER, HD), BF16),
            pltpu.VMEM((QUARTER, HD), BF16),
            pltpu.VMEM((HALF, 256), BF16),
            pltpu.VMEM((IMAGES, ROWS, 256), BF16),
            pltpu.VMEM((2 * TOK, HD), BF16),
            pltpu.VMEM((2 * TOK, 896), BF16),
            pltpu.VMEM((2 * TOK, HD), F32),
            pltpu.VMEM((2 * TOK, HD), F32),
            pltpu.VMEM((TOK, 256), BF16),
            pltpu.VMEM((TOK, 256), BF16),
            pltpu.VMEM((8, 256, 512), BF16),
            pltpu.VMEM((8, 256, 512), BF16),
            pltpu.VMEM((8, TOK, 512), F32),
            pltpu.VMEM((2, 4, TOK, 512), BF16),
            pltpu.VMEM((2, 4, TOK, 512), BF16),
            dma((7,)),
            dma((3,)),
            dma((3,)),
            dma((n, 2, 4, 2)),
            dma((n, 2, 4, 2)),
            dma((n,)),
            dma((n,)),
            dma((n, 2, 16)),
            dma((n, 2, 16)),
            dma((n, 2, 16)),
            dma((n, 2, 16)),
            dma((2, 4)),
            dma((2, 4)),
            dma((8,)),
            dma((8,)),
            dma((8,)),
            dma((8,)),
            dma((8,)),
            dma,
            dma,
            dma((2, 2, 4)),
            dma((2, 2, 4)),
        ],
        compiler_params=pltpu.CompilerParams(
            collective_id=0, has_side_effects=True, vmem_limit_bytes=60 * 2**20
        ),
        cost_estimate=pl.CostEstimate(flops=2 * 10**10, bytes_accessed=3 * 10**7, transcendentals=13 * 10**6),
    )(*args)


def on_device(
    text, gain, wq, wkv, wout, qgain, kgain, gate, images, seg, owner, pos
):
    return fused(
        text, gain, images[0, IMG_TOK - 1 :], wq, wkv, wout, qgain.reshape(1, -1), kgain.reshape(1, -1),
        gate, owner, pos, seg, images,
    )


def solution(mesh):
    rows = ("seq", "section")
    return jax.shard_map(
        on_device,
        mesh=mesh,
        in_specs=(
            P(rows, "tp"),
            P("tp"),
            P(None, "tp"),
            P("tp", None),
            P("tp", None),
            P(),
            P(),
            P(),
            P(rows, None, "tp"),
            P(rows),
            P(rows),
            P(rows),
        ),
        out_specs=P(rows, "tp"),
        check_vma=False,
    )
```

```python
import jax
import jax.numpy as jnp
from jax import lax
from jax.experimental import pallas as pl
from jax.experimental.pallas import tpu as pltpu
from jax.sharding import PartitionSpec as P

MESH = pl.DeviceIdType.MESH
F32, BF16 = jnp.float32, jnp.bfloat16
HD = 128
IMG_TOK = 1601
IMAGES = 16
TOK = 256
QUARTER = 416
BODY = 400
HALF = 2 * QUARTER
EPS = 1e-05
META = 2.0**-40
META_ROW = 408

SUBS = ((224, 48, 48, 48, 48), (0, 64, 48, 64, 48))

EARLY = (('start', 0), ('start', 1))
ORDER = (
    ('text', 1),
    ('ring', 0, 0),
    ('ring', 1, 0),
    ('ring', 0, 1),
    ('ring', 1, 1),
    ('ring', 0, 2),
    ('ring', 1, 2),
    ('text', 2),
    ('ring', 0, 3),
    ('ring', 1, 3),
    ('PF', 0, 0, 3),
    ('PF', 0, 0, 1),
    ('PF', 0, 1, 3),
    ('PF', 0, 1, 1),
    ('PS', 0, 0, 0, 3),
    ('PS', 0, 0, 0, 1),
    ('PS', 0, 1, 0, 3),
    ('PS', 0, 1, 0, 1),
    ('PF', 1, 0, 3),
    ('PF', 1, 0, 1),
    ('PS', 1, 0, 0, 3),
    ('PS', 1, 0, 0, 1),
    ('text', 3),
    ('PF', 1, 1, 3),
    ('PG', 0, 0),
    ('PF', 1, 1, 1),
    ('PS', 0, 0, 3, 3),
    ('PS', 0, 0, 3, 1),
    ('PS', 0, 1, 3, 3),
    ('PS', 0, 1, 3, 1),
    ('PS', 1, 1, 0, 3),
    ('PS', 1, 1, 0, 1),
    ('PS', 0, 0, 1, 3),
    ('PS', 0, 0, 1, 1),
    ('PS', 0, 1, 1, 3),
    ('PS', 0, 1, 1, 1),
    ('PG', 0, 1),
    ('PT', 0, 1, 0),
    ('PT', 0, 0, 0),
    ('PS', 1, 0, 3, 1),
    ('PG', 1, 0),
    ('text', 4),
    ('PS', 1, 1, 3, 1),
    ('PS', 1, 0, 3, 3),
    ('PS', 1, 0, 1, 1),
    ('PS', 1, 1, 3, 3),
    ('PS', 1, 1, 1, 1),
    ('textc',),
    ('PG', 1, 1),
    ('PS', 0, 0, 2, 1),
    ('PS', 0, 1, 2, 1),
    ('PS', 0, 0, 2, 3),
    ('PS', 1, 0, 1, 3),
    ('PS', 1, 1, 1, 3),
    ('PT', 0, 0, 3),
    ('PT', 0, 1, 3),
    ('PS', 0, 1, 2, 3),
    ('PT', 0, 1, 1),
    ('PT', 0, 0, 1),
    ('PT', 1, 0, 0),
    ('PT', 1, 0, 3),
    ('PT', 1, 1, 0),
    ('PT', 1, 1, 3),
    ('PS', 1, 0, 2, 1),
    ('PS', 1, 0, 2, 3),
    ('PS', 1, 1, 2, 3),
    ('PS', 1, 1, 2, 1),
    ('PT', 0, 0, 2),
    ('PT', 1, 0, 1),
    ('q2',),
    ('att', 0, (0, 0), (1, 0), (3, 0), (0, 1), (0, 3)),
    ('PT', 0, 1, 2),
    ('PT', 1, 0, 2),
    ('PT', 1, 1, 1),
    ('PT', 1, 1, 2),
    ('att', 0, (1, 1), (1, 3), (3, 1), (3, 3)),
    ('att', 0, (2, 0), (0, 2), (2, 1), (2, 3), (1, 2), (3, 2), (2, 2)),
    ('att', 1, (0, 0), (1, 0), (3, 0), (0, 1), (0, 3)),
    ('att', 1, (1, 1), (1, 3), (3, 1), (3, 3)),
    ('att', 1, (2, 0), (0, 2), (2, 1), (2, 3), (1, 2), (3, 2), (2, 2)),
)


def remote(src, dst, send, recv, device):
    return pltpu.make_async_remote_copy(
        src_ref=src, dst_ref=dst, send_sem=send, recv_sem=recv, device_id=device, device_id_type=MESH
    )


class Place:
    def __init__(self):
        seq, tp, sec = lax.axis_index("seq"), lax.axis_index("tp"), lax.axis_index("section")
        self.tp, self.z, self.c = tp, tp // 2, tp % 2
        self.x, self.y = seq // 2, sec * 2 + seq % 2
        self.partner = {"tp": self.z * 2 + 1 - self.c}
        self.up = {"tp": ((self.z + 1) % 8) * 2 + self.c}
        self.down = {"tp": ((self.z + 7) % 8) * 2 + self.c}

    def step(self, axis, delta):
        if axis == "x":
            return {"seq": ((self.x + delta) % 4) * 2 + self.y % 2}
        y = (self.y + delta) % 4
        return {"seq": self.x * 2 + y % 2, "section": y // 2}

    def image(self, dx, dy):
        y = (self.y + dy) % 4
        return ((self.x + dx) % 4) * 4 + (y % 2) * 2 + y // 2


def greet(devices):
    barrier = pltpu.get_barrier_semaphore()
    for device in devices:
        pl.semaphore_signal(barrier, inc=1, device_id=device, device_id_type=MESH)
    pl.semaphore_wait(barrier, len(devices))


def kernel(
    text, gain, tail, wq, wkv, wout, qgain, kgain, gate, owner, pos, seg, img,
    out,
    nall, wqv, qacc, imgv, pimg, tailv, wkvv, pwkv, acck, accv, rk, rv, vfirst,
    kv, qrows, total, mass, half, theirs, mhalf, mtheirs, att, patt, wo, pwo, terms, got, sent,
    load_sem, ex_send, ex_recv, bs, br, ps, pr, cs, cr, as_, ar, acs, acr, ws, wr,
    wo_sem, es, er, ds, dr, qs, qr, ts, tr,
):
    me = Place()
    z, c = me.z, me.c
    zpar = z % 2
    loads = [pltpu.make_async_copy(wkv, wkvv, load_sem.at[0])]
    for k in range(2):
        src = img.at[0, pl.ds(pl.multiple_of(c * 2 * BODY + k * BODY, 16), BODY)]
        loads.append(pltpu.make_async_copy(src, imgv.at[pl.ds(k * QUARTER, BODY)], load_sem.at[1 + k]))
    for k in range(4):
        part = pl.ds(k * 2048, 2048)
        loads.append(pltpu.make_async_copy(wq.at[part], wqv.at[part], load_sem.at[3 + k]))
    for load in loads[:3]:
        load.start()

    row = lax.broadcasted_iota(jnp.int32, (16, 512), 0)
    last = tail[...].astype(F32)
    tailv[...] = jnp.where(row == 16 * c, last, 0.0).astype(BF16)
    imgv[BODY:QUARTER, :] = jnp.zeros((16, 512), BF16)
    pimg[BODY:QUARTER, :] = jnp.zeros((16, 512), BF16)
    imgv[QUARTER + BODY :, :] = jnp.where(row == 16 * (1 - c), last, 0.0).astype(BF16)

    nall[me.tp] = (text[...].astype(F32) * gain[...].astype(F32).reshape(1, 512)).astype(BF16)
    for load in loads[3:7]:
        load.start()

    greet([me.partner, me.up, me.down] + [me.step(a, d) for a in "xy" for d in (1, 3)])
    sends = []

    def send(src, dst, ssem, rsem, device):
        copy = remote(src, dst, ssem, rsem, device)
        copy.start()
        sends.append(copy)

    def arrived(ref, ssem, rsem):
        remote(ref, ref, ssem, rsem, me.partner).wait_recv()

    send(wkv, pwkv, ex_send.at[0], ex_recv.at[0], me.partner)
    for k in range(2):
        src = img.at[0, pl.ds(pl.multiple_of((1 - c) * 2 * BODY + k * BODY, 16), BODY)]
        send(src, pimg.at[pl.ds(k * QUARTER, BODY)], ex_send.at[1 + k], ex_recv.at[1 + k], me.partner)
    end = pimg.at[pl.ds(QUARTER + BODY, 16)]
    send(tailv, end, ex_send.at[3], ex_recv.at[3], me.partner)

    shard = lambda k: ((z + k % 8) % 8) * 2 + c

    def text_send(k, way, hop):
        ref = nall.at[shard(k)]
        if hop == 4:
            ref = ref.at[pl.ds(way * 128, 128)]
        send(ref, ref, as_.at[way, hop - 1], ar.at[way, hop - 1], (me.up, me.down)[way])

    def text_share(k):
        ref = nall.at[shard(k)]
        send(ref, ref, acs.at[k % 8], acr.at[k % 8], me.partner)

    def text_arrived(hop, way):
        k = -hop if way == 0 else hop
        ref = nall.at[shard(k)]
        if hop == 4:
            ref = ref.at[pl.ds(way * 128, 128)]
        arrived(ref, as_.at[way, hop - 1], ar.at[way, hop - 1])

    def text_round(hop):
        for way in (0, 1):
            text_arrived(hop, way)
            if hop < 4:
                k = -hop if way == 0 else hop
                text_send(k, way, hop + 1)
                text_share(k)
        if hop == 4:
            text_share(4)

    def text_compute():
        for k in range(8):
            ref = nall.at[((z + k) % 8) * 2 + 1 - c]
            arrived(ref, acs.at[k], acr.at[k])
        for load in loads[3:7]:
            load.wait()
        qacc[...] = jnp.zeros_like(qacc)

        def use(index, carry):
            w = wqv[pl.ds(pl.multiple_of(index * 512, 512), 512), :]
            qacc[...] += jnp.dot(nall[index], w, preferred_element_type=F32)
            return carry

        lax.fori_loop(0, 16, use, 0)
        for h in range(2):
            q = qacc[:, h * HD : (h + 1) * HD]
            q = q * lax.rsqrt(jnp.mean(q * q, axis=-1, keepdims=True) + EPS) * qgain[...]
            qrows[h * TOK : (h + 1) * TOK, :] = q.astype(BF16)

    text_send(0, 0, 1)
    text_send(0, 1, 1)
    text_share(0)

    def order(n):
        return (z + 4 + jnp.where(n % 2 == 1, -((n + 1) // 2), n // 2)) % 8

    def project(d):
        rows = pl.ds(pl.multiple_of((d % 2) * QUARTER, QUARTER), QUARTER)
        cols = pl.ds(pl.multiple_of((d // 2) * 256, 256), 256)
        part = jnp.dot(imgv[rows, :], wkvv[:, cols], preferred_element_type=F32)
        part += jnp.dot(pimg[rows, :], pwkv[:, cols], preferred_element_type=F32)
        acck[d] = part[:, :HD]
        accv[d] = part[:, HD:]

    def project_next(n, carry):
        project(order(n))
        return carry

    def piece(u, par, part=None):
        start, *sizes = SUBS[u]
        start += par * (sizes[0] + sizes[1])
        pair = sizes[2 * par : 2 * par + 2]
        if part is None:
            return start, pair[0] + pair[1]
        return start + part * pair[0], pair[part]

    def ring_rows(u, way, stage):
        if stage == 0:
            return pl.ds(*piece(u, way))
        return pl.ds(SUBS[u][0], sum(SUBS[u][1:]))

    def ring_send(u, stage):
        for way in (0, 1):
            rows = ring_rows(u, way, stage)
            if stage == 0:
                d = (z + 4) % 8
                vfirst[rows, :] = accv[d, rows, :].astype(BF16)
                srck, srcv = acck.at[d, rows], vfirst.at[rows]
            else:
                srck, srcv = rk.at[way, stage - 1, rows], rv.at[way, stage - 1, rows]
            device = (me.up, me.down)[way]
            send(srck, rk.at[way, stage, rows], bs.at[u, way, stage, 0], br.at[u, way, stage, 0], device)
            send(srcv, rv.at[way, stage, rows], bs.at[u, way, stage, 1], br.at[u, way, stage, 1], device)

    def ring_receive(u, stage):
        for way in (0, 1):
            rows = ring_rows(u, way, stage)
            d = (z + (3 - stage if way == 0 else 5 + stage)) % 8
            if stage == 0:
                other = ring_rows(u, 1 - way, 0)
                rk[way, 0, other, :] = acck[d, other, :]
                rv[way, 0, other, :] = accv[d, other, :].astype(BF16)
            arrived(rk.at[way, stage, rows], bs.at[u, way, stage, 0], br.at[u, way, stage, 0])
            arrived(rv.at[way, stage, rows], bs.at[u, way, stage, 1], br.at[u, way, stage, 1])
            if stage < 3:
                rk[way, stage, rows, :] += acck[d, rows, :]
                rv[way, stage, rows, :] = (rv[way, stage, rows, :].astype(F32) + accv[d, rows, :]).astype(BF16)

    here = me.image(0, 0)
    here_rows = lambda start, n: pl.ds(pl.multiple_of(c * QUARTER + start, 16), n)

    def finish(u):
        start, n = SUBS[u][0], sum(SUBS[u][1:])
        rows = pl.ds(start, n)
        key = rk[0, 3, rows, :] + rk[1, 3, rows, :] + acck[z, rows, :]
        val = rv[0, 3, rows, :].astype(F32) + rv[1, 3, rows, :].astype(F32) + accv[z, rows, :]
        key = key * lax.rsqrt(jnp.mean(key * key, axis=-1, keepdims=True) + EPS) * kgain[...]
        if start + n == QUARTER:
            row = start + lax.broadcasted_iota(jnp.int32, (n, HD), 0)
            lane = lax.broadcasted_iota(jnp.int32, (n, HD), 1)
            said = jnp.where(lane == 0, owner[0], jnp.where(lane == 1, pos[0] // 64, pos[0] % 64))
            said = jnp.where(lane < 3, said, 0).astype(F32) * META
            key = jnp.where(row >= META_ROW, said, key)
        kv[here, here_rows(start, n), 0:HD] = key.astype(BF16)
        kv[here, here_rows(start, n), HD:] = val.astype(BF16)


    def block(u, par, i, j, part=None):
        m = me.image(i, j) if par == 0 else me.image(j, i)
        return kv.at[m, here_rows(*piece(u, par, part))]

    axes = lambda par: ("x", "y") if par == 0 else ("y", "x")

    def spread_first(u, par, i, way, part=None):
        slot = {(0, 0): 0, (0, 1): 1, (3, 0): 2, (1, 1): 3}[(i, way)]
        ref = block(u, par, i, 0, part)
        send(ref, ref, ps.at[u, par, slot], pr.at[u, par, slot], me.step(axes(par)[0], (1, 3)[way]))

    def first_arrived(u, par, i, part=None):
        slot = {(3, None): 0, (1, None): 1, (2, 1): 2, (2, 0): 3}[(i, part)]
        arrived(block(u, par, i, 0, part), ps.at[u, par, slot], pr.at[u, par, slot])

    def spread_second(u, par, i, j, way):
        slot = 4 + 3 * i + (way if j == 0 else 2)
        ref = block(u, par, i, j)
        send(ref, ref, ps.at[u, par, slot], pr.at[u, par, slot], me.step(axes(par)[1], (1, 3)[way]))

    def second_arrived(u, par, i, j):
        slot = 4 + 3 * i + {3: 0, 1: 1, 2: 2}[j]
        arrived(block(u, par, i, j), ps.at[u, par, slot], pr.at[u, par, slot])

    def share(u, par, i, j):
        ref = block(u, par, i, j)
        send(ref, ref, cs.at[u, par, 4 * i + j], cr.at[u, par, 4 * i + j], me.partner)

    def column(u, par, i):
        spread_second(u, par, i, 0, 0)
        spread_second(u, par, i, 0, 1)
        share(u, par, i, 0)

    def spread_start(u):
        for par in (0, 1):
            spread_first(u, par, 0, 0)
            spread_first(u, par, 0, 1)
            column(u, par, 0)

    def spread_first_on(u, par, i):
        first_arrived(u, par, i)
        spread_first(u, par, i, 0 if i == 3 else 1, 1 if i == 3 else 0)
        column(u, par, i)

    def spread_opposite(u, par):
        first_arrived(u, par, 2, 0)
        first_arrived(u, par, 2, 1)
        column(u, par, 2)

    def spread_second_on(u, par, i, j):
        second_arrived(u, par, i, j)
        if (j == 3) == (i < 2):
            spread_second(u, par, i, j, 0 if j == 3 else 1)
        share(u, par, i, j)

    def spread_end(u, par, i):
        second_arrived(u, par, i, 2)
        share(u, par, i, 2)

    docs = jnp.broadcast_to(seg[...].astype(F32).reshape(1, TOK), (HD, TOK)).T[:, 0:1]
    places = ((me.x * 4 + me.y % 2 * 2 + me.y // 2) * TOK + lax.broadcasted_iota(jnp.int32, (TOK, 1), 0)).astype(F32)
    total[...] = jnp.zeros_like(total)
    mass[...] = jnp.zeros_like(mass)

    def attend_image(u, m):
        start, n = SUBS[u][0], sum(SUBS[u][1:])
        parts = [kv[m, q * QUARTER + start : q * QUARTER + start + n, :] for q in range(2)]
        both = jnp.concatenate(parts, axis=0)
        keys, values = both[:, :HD], both[:, HD:]
        said = kv[m, QUARTER - 16 : QUARTER, 0:HD].astype(F32)[15:16, :] * (1.0 / META)
        lane = lax.broadcasted_iota(jnp.int32, (1, HD), 1)
        doc = jnp.sum(jnp.where(lane == 0, said, 0.0), axis=1, keepdims=True)
        scale = jnp.where(lane == 1, 64.0, jnp.where(lane == 2, 1.0, 0.0))
        mask = (docs == doc) & (places >= jnp.sum(said * scale, axis=1, keepdims=True))
        for h in range(4):
            at = slice(h * TOK, (h + 1) * TOK)
            rows = qrows[at, :]
            weight = jnp.zeros((TOK, HD), F32)
            term = jnp.zeros((TOK, HD), F32)
            for k0 in range(0, 2 * n, 256):
                width = min(256, 2 * n - k0)
                score = lax.dot_general(
                    rows, keys[k0 : k0 + width, :], (((1,), (1,)), ((), ())), preferred_element_type=F32
                )
                expo = jnp.exp2(score * (HD**-0.5 * 1.4426950408889634))
                if start + n == QUARTER:
                    lane = k0 + lax.broadcasted_iota(jnp.int32, expo.shape, 1)
                    good = (lane < BODY - start) | ((lane >= n) & (lane < n + BODY - start + zpar))
                    expo = jnp.where(good, expo, 0.0)
                for lanes in range(0, width, HD):
                    some = expo[:, lanes : min(lanes + HD, width)]
                    if some.shape[1] < HD:
                        some = jnp.concatenate([some, jnp.zeros((TOK, HD - some.shape[1]), F32)], axis=1)
                    weight += some
                term += jnp.dot(expo.astype(BF16), values[k0 : k0 + width, :], preferred_element_type=F32)
            total[at, :] += jnp.where(mask, term, 0.0)
            mass[at, :] += jnp.where(mask, weight, 0.0)

    def attend(u, images):
        for dx, dy in images:
            for par, i, j in ((0, dx, dy), (1, dy, dx)):
                start, n = piece(u, par)
                ref = kv.at[me.image(dx, dy), pl.ds(pl.multiple_of((1 - c) * QUARTER + start, 16), n)]
                arrived(ref, cs.at[u, par, 4 * i + j], cr.at[u, par, 4 * i + j])
        codes = [4 * dx + dy for dx, dy in images]

        def one(n, carry):
            code = codes[0]
            for k in range(1, len(codes)):
                code = jnp.where(n == k, codes[k], code)
            attend_image(u, me.image(code // 4, code % 4))
            return carry

        lax.fori_loop(0, len(codes), one, 0)

    def ring_step(u, stage):
        ring_receive(u, stage)
        if stage < 3:
            ring_send(u, stage + 1)
        else:
            finish(u)
            spread_start(u)

    pair = {"tp": (z + 1 - 2 * zpar) * 2 + c}
    own_rows, pair_rows = pl.ds(0, 2 * TOK), pl.ds(2 * TOK, 2 * TOK)

    def queries_swap():
        text_compute()
        send(qrows.at[own_rows], qrows.at[pair_rows], qs, qr, pair)

    def queries_arrived():
        arrived(qrows.at[pair_rows], qs, qr)

    handlers = {
        "start": lambda u: ring_send(u, 0),
        "ring": ring_step,
        "PF": spread_first_on,
        "PG": spread_opposite,
        "PS": spread_second_on,
        "PT": spread_end,
        "text": text_round,
        "textc": queries_swap,
        "q2": queries_arrived,
        "att": lambda u, *images: attend(u, images),
    }

    for load in loads[:3]:
        load.wait()
    arrived(pwkv, ex_send.at[0], ex_recv.at[0])
    for k in range(2):
        arrived(pimg.at[pl.ds(k * QUARTER, BODY)], ex_send.at[1 + k], ex_recv.at[1 + k])
    arrived(end, ex_send.at[3], ex_recv.at[3])
    project((z + 4) % 8)
    for name, *args in EARLY:
        handlers[name](*args)
    lax.fori_loop(1, 8, project_next, 0)
    for k in range(8):
        src = wout.at[:, pl.ds(pl.multiple_of((2 * k + 1 - c) * 512, 512), 512)]
        send(src, pwo.at[k], ws.at[k], wr.at[k], me.partner)
        src = wout.at[:, pl.ds(pl.multiple_of((2 * k + c) * 512, 512), 512)]
        load = pltpu.make_async_copy(src, wo.at[k], wo_sem.at[k])
        load.start()
        loads.append(load)
    for name, *args in ORDER:
        handlers[name](*args)

    half[...] = total[pair_rows, :].astype(BF16)
    send(half, theirs, ts.at[0], tr.at[0], pair)
    weight = jnp.sum(mass[pair_rows, :], axis=1, keepdims=True)
    mhalf[...] = jnp.broadcast_to(weight, (2 * TOK, HD)).T[0:8, :]
    send(mhalf, mtheirs, ts.at[1], tr.at[1], pair)
    arrived(mtheirs, ts.at[1], tr.at[1])
    arrived(theirs, ts.at[0], tr.at[0])
    others = jnp.broadcast_to(mtheirs[0:1, :], (HD, 2 * TOK)).T

    for h in range(2):
        rows = slice(h * TOK, (h + 1) * TOK)
        weight = jnp.maximum(jnp.sum(mass[rows, :], axis=1, keepdims=True) + others[rows], 1.0)
        att[:, h * HD : (h + 1) * HD] = ((total[rows, :] + theirs[rows, :].astype(F32)) / weight).astype(BF16)

    send(att, patt, es, er, me.partner)

    def term(d):
        part = jnp.dot(att[...], wo[d], preferred_element_type=F32)
        terms[d] = part + jnp.dot(patt[...], pwo[d], preferred_element_type=F32)

    def next_term(n, carry):
        term(order(n))
        return carry

    def term_rows(way, stage):
        return pl.ds(way * 128, 128) if stage == 0 else pl.ds(0, TOK)

    def term_send(e, stage):
        cols = pl.ds(e * 256, 256)
        for way in (0, 1):
            rows = term_rows(way, stage)
            part = terms[(z + (4 - stage if way == 0 else 4 + stage)) % 8, :, cols]
            if stage == 0:
                part = part[way * 128 : way * 128 + 128]
            elif stage == 1:
                parts = [part[:128], part[128:]]
                parts[way] += got[way, 0, way * 128 : way * 128 + 128, cols].astype(F32)
                part = jnp.concatenate(parts, axis=0)
            else:
                part += got[way, stage - 1, :, cols].astype(F32)
            sent[way, stage, rows, cols] = part.astype(BF16)
            send(
                sent.at[way, stage, rows, cols], got.at[way, stage, rows, cols],
                ds.at[e, way, stage], dr.at[e, way, stage], (me.up, me.down)[way],
            )

    def term_arrived(e, stage):
        for way in (0, 1):
            ref = got.at[way, stage, term_rows(way, stage), pl.ds(e * 256, 256)]
            arrived(ref, ds.at[e, way, stage], dr.at[e, way, stage])

    for k in range(8):
        arrived(pwo.at[k], ws.at[k], wr.at[k])
    for load in loads[7:]:
        load.wait()
    arrived(patt, es, er)
    term((z + 4) % 8)
    term_send(0, 0)
    term_send(1, 0)
    lax.fori_loop(1, 8, next_term, 0)
    for stage in range(3):
        for e in (0, 1):
            term_arrived(e, stage)
            term_send(e, stage + 1)
    scale = jnp.tanh(jnp.full((1, 256), gate[0], F32))
    for e in (0, 1):
        term_arrived(e, 3)
        cols = pl.ds(e * 256, 256)
        part = terms[z, :, cols] + got[0, 3, :, cols].astype(F32) + got[1, 3, :, cols].astype(F32)
        out[:, e * 256 : e * 256 + 256] = (scale * part).astype(BF16)

    for copy in sends:
        copy.wait_send()


def fused(*args):
    vmem, anyspace, smem = (pl.BlockSpec(memory_space=m) for m in (pltpu.VMEM, pl.ANY, pltpu.SMEM))
    dma = pltpu.SemaphoreType.DMA
    n = len(SUBS)
    return pl.pallas_call(
        kernel,
        out_shape=jax.ShapeDtypeStruct((TOK, 512), BF16),
        in_specs=[vmem, vmem, vmem, anyspace, anyspace, anyspace, vmem, vmem, smem, smem, smem, vmem, anyspace],
        out_specs=vmem,
        scratch_shapes=[
            pltpu.VMEM((16, TOK, 512), BF16),
            pltpu.VMEM((8192, 256), BF16),
            pltpu.VMEM((TOK, 256), F32),
            pltpu.VMEM((HALF, 512), BF16),
            pltpu.VMEM((HALF, 512), BF16),
            pltpu.VMEM((16, 512), BF16),
            pltpu.VMEM((512, 1024), BF16),
            pltpu.VMEM((512, 1024), BF16),
            pltpu.VMEM((8, QUARTER, HD), F32),
            pltpu.VMEM((8, QUARTER, HD), F32),
            pltpu.VMEM((2, 4, QUARTER, HD), F32),
            pltpu.VMEM((2, 4, QUARTER, HD), BF16),
            pltpu.VMEM((QUARTER, HD), BF16),
            pltpu.VMEM((IMAGES, HALF, 256), BF16),
            pltpu.VMEM((4 * TOK, HD), BF16),
            pltpu.VMEM((4 * TOK, HD), F32),
            pltpu.VMEM((4 * TOK, HD), F32),
            pltpu.VMEM((2 * TOK, HD), BF16),
            pltpu.VMEM((2 * TOK, HD), BF16),
            pltpu.VMEM((8, 2 * TOK), F32),
            pltpu.VMEM((8, 2 * TOK), F32),
            pltpu.VMEM((TOK, 256), BF16),
            pltpu.VMEM((TOK, 256), BF16),
            pltpu.VMEM((8, 256, 512), BF16),
            pltpu.VMEM((8, 256, 512), BF16),
            pltpu.VMEM((8, TOK, 512), F32),
            pltpu.VMEM((2, 4, TOK, 512), BF16),
            pltpu.VMEM((2, 4, TOK, 512), BF16),
            dma((7,)),
            dma((4,)),
            dma((4,)),
            dma((n, 2, 4, 2)),
            dma((n, 2, 4, 2)),
            dma((n, 2, 16)),
            dma((n, 2, 16)),
            dma((n, 2, 16)),
            dma((n, 2, 16)),
            dma((2, 4)),
            dma((2, 4)),
            dma((8,)),
            dma((8,)),
            dma((8,)),
            dma((8,)),
            dma((8,)),
            dma,
            dma,
            dma((2, 2, 4)),
            dma((2, 2, 4)),
            dma,
            dma,
            dma((2,)),
            dma((2,)),
        ],
        compiler_params=pltpu.CompilerParams(
            collective_id=0, has_side_effects=True, vmem_limit_bytes=60 * 2**20
        ),
        cost_estimate=pl.CostEstimate(flops=2 * 10**10, bytes_accessed=3 * 10**7, transcendentals=13 * 10**6),
    )(*args)


def on_device(
    text, gain, wq, wkv, wout, qgain, kgain, gate, images, seg, owner, pos
):
    return fused(
        text, gain, images[0, IMG_TOK - 1 :], wq, wkv, wout, qgain.reshape(1, -1), kgain.reshape(1, -1),
        gate, owner, pos, seg, images,
    )


def solution(mesh):
    rows = ("seq", "section")
    return jax.shard_map(
        on_device,
        mesh=mesh,
        in_specs=(
            P(rows, "tp"),
            P("tp"),
            P(None, "tp"),
            P("tp", None),
            P("tp", None),
            P(),
            P(),
            P(),
            P(rows, None, "tp"),
            P(rows),
            P(rows),
            P(rows),
        ),
        out_specs=P(rows, "tp"),
        check_vma=False,
    )
```

```python
import jax
import jax.numpy as jnp
from jax import lax
from jax.experimental import pallas as pl
from jax.experimental.pallas import tpu as pltpu
from jax.sharding import PartitionSpec as P

MESH = pl.DeviceIdType.MESH
F32, BF16 = jnp.float32, jnp.bfloat16
HD = 128
IMG_TOK = 1601
IMAGES = 16
TOK = 256
QUARTER = 416
BODY = 400
HALF = 2 * QUARTER
EPS = 1e-05
HIDDEN = -30000.0

SUBS = ((224, 48, 48, 48, 48), (0, 64, 48, 64, 48))

EARLY = (('start', 0), ('start', 1))
ORDER = (
    ('text', 1),
    ('ring', 0, 0),
    ('text', 2),
    ('ring', 1, 0),
    ('ring', 0, 1),
    ('text', 3),
    ('ring', 1, 1),
    ('ring', 0, 2),
    ('text', 4),
    ('textc',),
    ('ring', 1, 2),
    ('ring', 0, 3),
    ('q2',),
    ('PF', 0, 0, 3),
    ('PF', 0, 0, 1),
    ('PS', 0, 0, 0, 3),
    ('PS', 0, 0, 0, 1),
    ('PS', 0, 1, 0, 3),
    ('PF', 0, 1, 3),
    ('PF', 0, 1, 1),
    ('PS', 0, 1, 0, 1),
    ('ring', 1, 3),
    ('PG', 0, 0),
    ('PS', 0, 0, 3, 3),
    ('PS', 0, 0, 3, 1),
    ('att', 0, (0, 0), (1, 0), (3, 0), (0, 1)),
    ('PS', 0, 0, 1, 3),
    ('PS', 0, 0, 1, 1),
    ('PS', 0, 1, 3, 3),
    ('PG', 0, 1),
    ('PS', 0, 1, 3, 1),
    ('PS', 0, 1, 1, 3),
    ('PS', 0, 1, 1, 1),
    ('PS', 1, 0, 0, 1),
    ('PT', 0, 0, 0),
    ('PF', 1, 0, 1),
    ('PS', 1, 0, 0, 3),
    ('PF', 1, 1, 1),
    ('PF', 1, 0, 3),
    ('PS', 1, 1, 0, 1),
    ('PF', 1, 1, 3),
    ('PS', 0, 0, 2, 1),
    ('PS', 1, 1, 0, 3),
    ('PT', 0, 1, 0),
    ('att', 0, (0, 3), (1, 1), (1, 3), (3, 1)),
    ('PS', 0, 0, 2, 3),
    ('PS', 0, 1, 2, 3),
    ('PS', 0, 1, 2, 1),
    ('PS', 1, 0, 1, 1),
    ('PT', 0, 0, 3),
    ('PT', 0, 0, 1),
    ('PT', 0, 1, 3),
    ('PT', 0, 1, 1),
    ('PS', 1, 0, 1, 3),
    ('PS', 1, 1, 1, 3),
    ('PS', 1, 1, 1, 1),
    ('PG', 1, 0),
    ('PS', 1, 0, 3, 1),
    ('PT', 1, 0, 0),
    ('att', 0, (3, 3), (2, 0), (0, 2), (2, 1)),
    ('PG', 1, 1),
    ('PS', 1, 0, 3, 3),
    ('PS', 1, 1, 3, 3),
    ('PS', 1, 1, 3, 1),
    ('PT', 0, 0, 2),
    ('PT', 0, 1, 2),
    ('PT', 1, 1, 0),
    ('PT', 1, 0, 1),
    ('PS', 1, 0, 2, 1),
    ('PT', 1, 1, 1),
    ('att', 0, (2, 3), (1, 2), (3, 2), (2, 2)),
    ('PS', 1, 0, 2, 3),
    ('PS', 1, 1, 2, 3),
    ('PS', 1, 1, 2, 1),
    ('PT', 1, 0, 3),
    ('att', 1, (0, 0), (1, 0), (3, 0), (0, 1)),
    ('PT', 1, 0, 2),
    ('PT', 1, 1, 3),
    ('att', 1, (0, 3), (1, 1), (1, 3), (3, 1)),
    ('PT', 1, 1, 2),
    ('att', 1, (3, 3), (2, 0), (0, 2), (2, 1)),
    ('att', 1, (2, 3), (1, 2), (3, 2), (2, 2)),
)


def remote(src, dst, send, recv, device):
    return pltpu.make_async_remote_copy(
        src_ref=src, dst_ref=dst, send_sem=send, recv_sem=recv, device_id=device, device_id_type=MESH
    )


class Place:
    def __init__(self):
        seq, tp, sec = lax.axis_index("seq"), lax.axis_index("tp"), lax.axis_index("section")
        self.tp, self.z, self.c = tp, tp // 2, tp % 2
        self.x, self.y = seq // 2, sec * 2 + seq % 2
        self.partner = {"tp": self.z * 2 + 1 - self.c}
        self.up = {"tp": ((self.z + 1) % 8) * 2 + self.c}
        self.down = {"tp": ((self.z + 7) % 8) * 2 + self.c}

    def step(self, axis, delta):
        if axis == "x":
            return {"seq": ((self.x + delta) % 4) * 2 + self.y % 2}
        y = (self.y + delta) % 4
        return {"seq": self.x * 2 + y % 2, "section": y // 2}

    def plane(self, dx, dy):
        y = (self.y + dy) % 4
        return {"seq": ((self.x + dx) % 4) * 2 + y % 2, "section": y // 2}

    def image(self, dx, dy):
        y = (self.y + dy) % 4
        return ((self.x + dx) % 4) * 4 + (y % 2) * 2 + y // 2


def greet(devices):
    barrier = pltpu.get_barrier_semaphore()
    for device in devices:
        pl.semaphore_signal(barrier, inc=1, device_id=device, device_id_type=MESH)
    pl.semaphore_wait(barrier, len(devices))


def kernel(
    text, gain, tail, wq, wkv, wout, qgain, kgain, gate, owner, pos, seg, img,
    out,
    nall, wqv, qacc, imgv, pimg, tailv, wkvv, pwkv, acck, accv, rk, rv, vfirst,
    kv, qrows, wexp, total, metas, half, theirs, mhalf, mtheirs, att, patt, wo, pwo, terms, got, sent,
    load_sem, ex_send, ex_recv, bs, br, ps, pr, cs, cr, as_, ar, acs, acr, ws, wr,
    wo_sem, es, er, ds, dr, qs, qr, ts, tr, ms, mr,
):
    me = Place()
    z, c = me.z, me.c
    zpar = z % 2
    loads = [pltpu.make_async_copy(wkv, wkvv, load_sem.at[0])]
    for k in range(2):
        src = img.at[0, pl.ds(pl.multiple_of(c * 2 * BODY + k * BODY, 16), BODY)]
        loads.append(pltpu.make_async_copy(src, imgv.at[pl.ds(k * QUARTER, BODY)], load_sem.at[1 + k]))
    for k in range(4):
        part = pl.ds(k * 2048, 2048)
        loads.append(pltpu.make_async_copy(wq.at[part], wqv.at[part], load_sem.at[3 + k]))
    for load in loads[:3]:
        load.start()

    row = lax.broadcasted_iota(jnp.int32, (16, 512), 0)
    last = tail[...].astype(F32)
    tailv[...] = jnp.where(row == 16 * c, last, 0.0).astype(BF16)
    imgv[BODY:QUARTER, :] = jnp.zeros((16, 512), BF16)
    pimg[BODY:QUARTER, :] = jnp.zeros((16, 512), BF16)
    imgv[QUARTER + BODY :, :] = jnp.where(row == 16 * (1 - c), last, 0.0).astype(BF16)

    nall[me.tp] = (text[...].astype(F32) * gain[...].astype(F32).reshape(1, 512)).astype(BF16)
    for load in loads[3:7]:
        load.start()

    here = me.image(0, 0)
    row = lax.broadcasted_iota(jnp.int32, (8, HD), 0)
    lane = lax.broadcasted_iota(jnp.int32, (8, HD), 1)
    said = jnp.where(row == 0, owner[0], jnp.where(row == 1, pos[0], 0))
    metas[here] = jnp.where(lane == here, said, 0).astype(F32)
    row = lax.broadcasted_iota(jnp.int32, (QUARTER, HD), 0)
    lane = lax.broadcasted_iota(jnp.int32, (QUARTER, HD), 1)
    for q in range(2):
        padding = (lane == IMAGES) & (row >= BODY + zpar * q)

        def name_rows(m, carry):
            kv[m, q * QUARTER : (q + 1) * QUARTER, 0:HD] = jnp.where((lane == m) | padding, 1.0, 0.0).astype(BF16)
            kv[m, q * QUARTER : (q + 1) * QUARTER, 3 * HD :] = jnp.ones((QUARTER, HD), BF16)
            return carry

        lax.fori_loop(0, IMAGES, name_rows, 0)

    across = [(dx, dy) for dx in range(4) for dy in range(4) if (dx, dy) != (0, 0)]
    greet([me.partner, me.up, me.down] + [me.plane(*step) for step in across])
    sends = []

    def send(src, dst, ssem, rsem, device):
        copy = remote(src, dst, ssem, rsem, device)
        copy.start()
        sends.append(copy)

    def arrived(ref, ssem, rsem):
        remote(ref, ref, ssem, rsem, me.partner).wait_recv()

    send(wkv, pwkv, ex_send.at[0], ex_recv.at[0], me.partner)
    for k in range(2):
        src = img.at[0, pl.ds(pl.multiple_of((1 - c) * 2 * BODY + k * BODY, 16), BODY)]
        send(src, pimg.at[pl.ds(k * QUARTER, BODY)], ex_send.at[1 + k], ex_recv.at[1 + k], me.partner)
    end = pimg.at[pl.ds(QUARTER + BODY, 16)]
    send(tailv, end, ex_send.at[3], ex_recv.at[3], me.partner)

    shard = lambda k: ((z + k % 8) % 8) * 2 + c

    def text_send(k, way, hop):
        ref = nall.at[shard(k)]
        if hop == 4:
            ref = ref.at[pl.ds(way * 128, 128)]
        send(ref, ref, as_.at[way, hop - 1], ar.at[way, hop - 1], (me.up, me.down)[way])

    def text_share(k):
        ref = nall.at[shard(k)]
        send(ref, ref, acs.at[k % 8], acr.at[k % 8], me.partner)

    def text_arrived(hop, way):
        k = -hop if way == 0 else hop
        ref = nall.at[shard(k)]
        if hop == 4:
            ref = ref.at[pl.ds(way * 128, 128)]
        arrived(ref, as_.at[way, hop - 1], ar.at[way, hop - 1])

    def text_round(hop):
        for way in (0, 1):
            text_arrived(hop, way)
            if hop < 4:
                k = -hop if way == 0 else hop
                text_send(k, way, hop + 1)
                text_share(k)
        if hop == 4:
            text_share(4)

    def text_compute():
        for k in range(8):
            ref = nall.at[((z + k) % 8) * 2 + 1 - c]
            arrived(ref, acs.at[k], acr.at[k])
        for load in loads[3:7]:
            load.wait()
        qacc[...] = jnp.zeros_like(qacc)

        def use(index, carry):
            w = wqv[pl.ds(pl.multiple_of(index * 512, 512), 512), :]
            qacc[...] += jnp.dot(nall[index], w, preferred_element_type=F32)
            return carry

        lax.fori_loop(0, 16, use, 0)
        for h in range(2):
            q = qacc[:, h * HD : (h + 1) * HD]
            q = q * lax.rsqrt(jnp.mean(q * q, axis=-1, keepdims=True) + EPS) * qgain[...]
            qrows[h * TOK : (h + 1) * TOK, HD:] = q.astype(BF16)

    text_send(0, 0, 1)
    text_send(0, 1, 1)
    text_share(0)
    for dx, dy in across:
        k = dx * 4 + dy
        send(metas.at[here], metas.at[here], ms.at[k], mr.at[k], me.plane(dx, dy))

    def order(n):
        return (z + 4 + jnp.where(n % 2 == 1, -((n + 1) // 2), n // 2)) % 8

    def project(d):
        rows = pl.ds(pl.multiple_of((d % 2) * QUARTER, QUARTER), QUARTER)
        cols = pl.ds(pl.multiple_of((d // 2) * 256, 256), 256)
        part = jnp.dot(imgv[rows, :], wkvv[:, cols], preferred_element_type=F32)
        part += jnp.dot(pimg[rows, :], pwkv[:, cols], preferred_element_type=F32)
        acck[d] = part[:, :HD]
        accv[d] = part[:, HD:]

    def project_next(n, carry):
        project(order(n))
        return carry

    def piece(u, par, part=None):
        start, *sizes = SUBS[u]
        start += par * (sizes[0] + sizes[1])
        pair = sizes[2 * par : 2 * par + 2]
        if part is None:
            return start, pair[0] + pair[1]
        return start + part * pair[0], pair[part]

    def ring_rows(u, way, stage):
        if stage == 0:
            return pl.ds(*piece(u, way))
        return pl.ds(SUBS[u][0], sum(SUBS[u][1:]))

    def ring_send(u, stage):
        for way in (0, 1):
            rows = ring_rows(u, way, stage)
            if stage == 0:
                d = (z + 4) % 8
                vfirst[rows, :] = accv[d, rows, :].astype(BF16)
                srck, srcv = acck.at[d, rows], vfirst.at[rows]
            else:
                srck, srcv = rk.at[way, stage - 1, rows], rv.at[way, stage - 1, rows]
            device = (me.up, me.down)[way]
            send(srck, rk.at[way, stage, rows], bs.at[u, way, stage, 0], br.at[u, way, stage, 0], device)
            send(srcv, rv.at[way, stage, rows], bs.at[u, way, stage, 1], br.at[u, way, stage, 1], device)

    def ring_receive(u, stage):
        for way in (0, 1):
            rows = ring_rows(u, way, stage)
            d = (z + (3 - stage if way == 0 else 5 + stage)) % 8
            if stage == 0:
                other = ring_rows(u, 1 - way, 0)
                rk[way, 0, other, :] = acck[d, other, :]
                rv[way, 0, other, :] = accv[d, other, :].astype(BF16)
            arrived(rk.at[way, stage, rows], bs.at[u, way, stage, 0], br.at[u, way, stage, 0])
            arrived(rv.at[way, stage, rows], bs.at[u, way, stage, 1], br.at[u, way, stage, 1])
            if stage < 3:
                rk[way, stage, rows, :] += acck[d, rows, :]
                rv[way, stage, rows, :] = (rv[way, stage, rows, :].astype(F32) + accv[d, rows, :]).astype(BF16)

    here_rows = lambda start, n: pl.ds(pl.multiple_of(c * QUARTER + start, 16), n)

    def finish(u):
        start, n = SUBS[u][0], sum(SUBS[u][1:])
        rows = pl.ds(start, n)
        key = rk[0, 3, rows, :] + rk[1, 3, rows, :] + acck[z, rows, :]
        val = rv[0, 3, rows, :].astype(F32) + rv[1, 3, rows, :].astype(F32) + accv[z, rows, :]
        key = key * lax.rsqrt(jnp.mean(key * key, axis=-1, keepdims=True) + EPS) * kgain[...]
        kv[here, here_rows(start, n), HD : 2 * HD] = key.astype(BF16)
        kv[here, here_rows(start, n), 2 * HD : 3 * HD] = val.astype(BF16)


    def block(u, par, i, j, part=None):
        m = me.image(i, j) if par == 0 else me.image(j, i)
        return kv.at[m, here_rows(*piece(u, par, part)), pl.ds(HD, 2 * HD)]

    axes = lambda par: ("x", "y") if par == 0 else ("y", "x")

    def spread_first(u, par, i, way, part=None):
        slot = {(0, 0): 0, (0, 1): 1, (3, 0): 2, (1, 1): 3}[(i, way)]
        ref = block(u, par, i, 0, part)
        send(ref, ref, ps.at[u, par, slot], pr.at[u, par, slot], me.step(axes(par)[0], (1, 3)[way]))

    def first_arrived(u, par, i, part=None):
        slot = {(3, None): 0, (1, None): 1, (2, 1): 2, (2, 0): 3}[(i, part)]
        arrived(block(u, par, i, 0, part), ps.at[u, par, slot], pr.at[u, par, slot])

    def spread_second(u, par, i, j, way):
        slot = 4 + 3 * i + (way if j == 0 else 2)
        ref = block(u, par, i, j)
        send(ref, ref, ps.at[u, par, slot], pr.at[u, par, slot], me.step(axes(par)[1], (1, 3)[way]))

    def second_arrived(u, par, i, j):
        slot = 4 + 3 * i + {3: 0, 1: 1, 2: 2}[j]
        arrived(block(u, par, i, j), ps.at[u, par, slot], pr.at[u, par, slot])

    def share(u, par, i, j):
        ref = block(u, par, i, j)
        send(ref, ref, cs.at[u, par, 4 * i + j], cr.at[u, par, 4 * i + j], me.partner)

    def column(u, par, i):
        spread_second(u, par, i, 0, 0)
        spread_second(u, par, i, 0, 1)
        share(u, par, i, 0)

    def spread_start(u):
        for par in (0, 1):
            spread_first(u, par, 0, 0)
            spread_first(u, par, 0, 1)
            column(u, par, 0)

    def spread_first_on(u, par, i):
        first_arrived(u, par, i)
        spread_first(u, par, i, 0 if i == 3 else 1, 1 if i == 3 else 0)
        column(u, par, i)

    def spread_opposite(u, par):
        first_arrived(u, par, 2, 0)
        first_arrived(u, par, 2, 1)
        column(u, par, 2)

    def spread_second_on(u, par, i, j):
        second_arrived(u, par, i, j)
        if (j == 3) == (i < 2):
            spread_second(u, par, i, j, 0 if j == 3 else 1)
        share(u, par, i, j)

    def spread_end(u, par, i):
        second_arrived(u, par, i, 2)
        share(u, par, i, 2)

    total[...] = jnp.zeros_like(total)

    def hide():
        for dx, dy in across:
            ref = metas.at[me.image(dx, dy)]
            k = (4 - dx) % 4 * 4 + (4 - dy) % 4
            arrived(ref, ms.at[k], mr.at[k])
        said = metas[0]
        for m in range(1, IMAGES):
            said += metas[m]
        docs = jnp.broadcast_to(seg[...].astype(F32).reshape(1, TOK), (HD, TOK)).T
        lane = lax.broadcasted_iota(jnp.int32, (TOK, HD), 1)
        place = here * TOK + lax.broadcasted_iota(jnp.int32, (TOK, HD), 0)
        sees = (docs == said[0:1, :]) & (place.astype(F32) >= said[1:2, :])
        unseen = jnp.where(lane < IMAGES, jnp.where(sees, 0.0, HIDDEN), jnp.where(lane == IMAGES, HIDDEN, 0.0))
        for h in range(4):
            qrows[h * TOK : (h + 1) * TOK, 0:HD] = unseen.astype(BF16)

    def attend_images(u, pair):
        start, n = SUBS[u][0], sum(SUBS[u][1:])
        both = lambda lanes: jnp.concatenate(
            [kv[m, q * QUARTER + start : q * QUARTER + start + n, lanes] for m in pair for q in range(2)], axis=0
        )
        keys, values = both(slice(0, 2 * HD)), both(slice(2 * HD, 4 * HD))

        def heads(r, carry):
            at = pl.ds(pl.multiple_of(r * 2 * TOK, 2 * TOK), 2 * TOK)
            rows = qrows[at, :]
            for k0 in range(0, 4 * n, 256):
                width = min(256, 4 * n - k0)
                score = lax.dot_general(
                    rows, keys[k0 : k0 + width, :], (((1,), (1,)), ((), ())), preferred_element_type=F32
                )
                wexp[:, k0 : k0 + width] = jnp.exp2(score * (HD**-0.5 * 1.4426950408889634)).astype(BF16)
            total[at, :] += jnp.dot(wexp[:, 0 : 4 * n], values, preferred_element_type=F32)
            return carry

        lax.fori_loop(0, 2, heads, 0)

    def attend(u, images):
        for dx, dy in images:
            for par, i, j in ((0, dx, dy), (1, dy, dx)):
                start, n = piece(u, par)
                rows = pl.ds(pl.multiple_of((1 - c) * QUARTER + start, 16), n)
                ref = kv.at[me.image(dx, dy), rows, pl.ds(HD, 2 * HD)]
                arrived(ref, cs.at[u, par, 4 * i + j], cr.at[u, par, 4 * i + j])
        codes = [4 * dx + dy for dx, dy in images]

        def one(n, carry):
            chosen = []
            for k in range(2):
                code = codes[k]
                for i in range(2, len(codes), 2):
                    code = jnp.where(n == i // 2, codes[i + k], code)
                chosen.append(me.image(code // 4, code % 4))
            attend_images(u, chosen)
            return carry

        lax.fori_loop(0, len(codes) // 2, one, 0)

    def ring_step(u, stage):
        ring_receive(u, stage)
        if stage < 3:
            ring_send(u, stage + 1)
        else:
            finish(u)
            spread_start(u)

    pair = {"tp": (z + 1 - 2 * zpar) * 2 + c}
    own_rows, pair_rows = pl.ds(0, 2 * TOK), pl.ds(2 * TOK, 2 * TOK)

    def queries_swap():
        text_compute()
        lanes = pl.ds(HD, HD)
        send(qrows.at[own_rows, lanes], qrows.at[pair_rows, lanes], qs, qr, pair)
        hide()

    def queries_arrived():
        arrived(qrows.at[pair_rows, pl.ds(HD, HD)], qs, qr)

    handlers = {
        "start": lambda u: ring_send(u, 0),
        "ring": ring_step,
        "PF": spread_first_on,
        "PG": spread_opposite,
        "PS": spread_second_on,
        "PT": spread_end,
        "text": text_round,
        "textc": queries_swap,
        "q2": queries_arrived,
        "att": lambda u, *images: attend(u, images),
    }

    for load in loads[:3]:
        load.wait()
    arrived(pwkv, ex_send.at[0], ex_recv.at[0])
    for k in range(2):
        arrived(pimg.at[pl.ds(k * QUARTER, BODY)], ex_send.at[1 + k], ex_recv.at[1 + k])
    arrived(end, ex_send.at[3], ex_recv.at[3])
    project((z + 4) % 8)
    for name, *args in EARLY:
        handlers[name](*args)
    lax.fori_loop(1, 8, project_next, 0)
    for k in range(8):
        src = wout.at[:, pl.ds(pl.multiple_of((2 * k + 1 - c) * 512, 512), 512)]
        send(src, pwo.at[k], ws.at[k], wr.at[k], me.partner)
        src = wout.at[:, pl.ds(pl.multiple_of((2 * k + c) * 512, 512), 512)]
        load = pltpu.make_async_copy(src, wo.at[k], wo_sem.at[k])
        load.start()
        loads.append(load)
    for name, *args in ORDER:
        handlers[name](*args)

    half[...] = total[pair_rows, 0:HD].astype(BF16)
    send(half, theirs, ts.at[0], tr.at[0], pair)
    mhalf[...] = total[pair_rows, HD:].T[0:8, :]
    send(mhalf, mtheirs, ts.at[1], tr.at[1], pair)
    arrived(mtheirs, ts.at[1], tr.at[1])
    arrived(theirs, ts.at[0], tr.at[0])
    others = jnp.broadcast_to(mtheirs[0:1, :], (HD, 2 * TOK)).T

    for h in range(2):
        rows = slice(h * TOK, (h + 1) * TOK)
        weight = jnp.maximum(total[rows, HD:] + others[rows], 1.0)
        att[:, h * HD : (h + 1) * HD] = ((total[rows, 0:HD] + theirs[rows, :].astype(F32)) / weight).astype(BF16)

    send(att, patt, es, er, me.partner)

    def term(d):
        part = jnp.dot(att[...], wo[d], preferred_element_type=F32)
        terms[d] = part + jnp.dot(patt[...], pwo[d], preferred_element_type=F32)

    def next_term(n, carry):
        term(order(n))
        return carry

    def term_rows(way, stage):
        return pl.ds(way * 128, 128) if stage == 0 else pl.ds(0, TOK)

    def term_send(e, stage):
        cols = pl.ds(e * 256, 256)
        for way in (0, 1):
            rows = term_rows(way, stage)
            part = terms[(z + (4 - stage if way == 0 else 4 + stage)) % 8, :, cols]
            if stage == 0:
                part = part[way * 128 : way * 128 + 128]
            elif stage == 1:
                parts = [part[:128], part[128:]]
                parts[way] += got[way, 0, way * 128 : way * 128 + 128, cols].astype(F32)
                part = jnp.concatenate(parts, axis=0)
            else:
                part += got[way, stage - 1, :, cols].astype(F32)
            sent[way, stage, rows, cols] = part.astype(BF16)
            send(
                sent.at[way, stage, rows, cols], got.at[way, stage, rows, cols],
                ds.at[e, way, stage], dr.at[e, way, stage], (me.up, me.down)[way],
            )

    def term_arrived(e, stage):
        for way in (0, 1):
            ref = got.at[way, stage, term_rows(way, stage), pl.ds(e * 256, 256)]
            arrived(ref, ds.at[e, way, stage], dr.at[e, way, stage])

    for k in range(8):
        arrived(pwo.at[k], ws.at[k], wr.at[k])
    for load in loads[7:]:
        load.wait()
    arrived(patt, es, er)
    term((z + 4) % 8)
    term_send(0, 0)
    term_send(1, 0)
    lax.fori_loop(1, 8, next_term, 0)
    for stage in range(3):
        for e in (0, 1):
            term_arrived(e, stage)
            term_send(e, stage + 1)
    scale = jnp.tanh(jnp.full((1, 256), gate[0], F32))
    for e in (0, 1):
        term_arrived(e, 3)
        cols = pl.ds(e * 256, 256)
        part = terms[z, :, cols] + got[0, 3, :, cols].astype(F32) + got[1, 3, :, cols].astype(F32)
        out[:, e * 256 : e * 256 + 256] = (scale * part).astype(BF16)

    for copy in sends:
        copy.wait_send()


def fused(*args):
    vmem, anyspace, smem = (pl.BlockSpec(memory_space=m) for m in (pltpu.VMEM, pl.ANY, pltpu.SMEM))
    dma = pltpu.SemaphoreType.DMA
    n = len(SUBS)
    return pl.pallas_call(
        kernel,
        out_shape=jax.ShapeDtypeStruct((TOK, 512), BF16),
        in_specs=[vmem, vmem, vmem, anyspace, anyspace, anyspace, vmem, vmem, smem, smem, smem, vmem, anyspace],
        out_specs=vmem,
        scratch_shapes=[
            pltpu.VMEM((16, TOK, 512), BF16),
            pltpu.VMEM((8192, 256), BF16),
            pltpu.VMEM((TOK, 256), F32),
            pltpu.VMEM((HALF, 512), BF16),
            pltpu.VMEM((HALF, 512), BF16),
            pltpu.VMEM((16, 512), BF16),
            pltpu.VMEM((512, 1024), BF16),
            pltpu.VMEM((512, 1024), BF16),
            pltpu.VMEM((8, QUARTER, HD), F32),
            pltpu.VMEM((8, QUARTER, HD), F32),
            pltpu.VMEM((2, 4, QUARTER, HD), F32),
            pltpu.VMEM((2, 4, QUARTER, HD), BF16),
            pltpu.VMEM((QUARTER, HD), BF16),
            pltpu.VMEM((IMAGES, HALF, 4 * HD), BF16),
            pltpu.VMEM((4 * TOK, 2 * HD), BF16),
            pltpu.VMEM((2 * TOK, 1024), BF16),
            pltpu.VMEM((4 * TOK, 2 * HD), F32),
            pltpu.VMEM((IMAGES, 8, HD), F32),
            pltpu.VMEM((2 * TOK, HD), BF16),
            pltpu.VMEM((2 * TOK, HD), BF16),
            pltpu.VMEM((8, 2 * TOK), F32),
            pltpu.VMEM((8, 2 * TOK), F32),
            pltpu.VMEM((TOK, 256), BF16),
            pltpu.VMEM((TOK, 256), BF16),
            pltpu.VMEM((8, 256, 512), BF16),
            pltpu.VMEM((8, 256, 512), BF16),
            pltpu.VMEM((8, TOK, 512), F32),
            pltpu.VMEM((2, 4, TOK, 512), BF16),
            pltpu.VMEM((2, 4, TOK, 512), BF16),
            dma((7,)),
            dma((4,)),
            dma((4,)),
            dma((n, 2, 4, 2)),
            dma((n, 2, 4, 2)),
            dma((n, 2, 16)),
            dma((n, 2, 16)),
            dma((n, 2, 16)),
            dma((n, 2, 16)),
            dma((2, 4)),
            dma((2, 4)),
            dma((8,)),
            dma((8,)),
            dma((8,)),
            dma((8,)),
            dma((8,)),
            dma,
            dma,
            dma((2, 2, 4)),
            dma((2, 2, 4)),
            dma,
            dma,
            dma((2,)),
            dma((2,)),
            dma((16,)),
            dma((16,)),
        ],
        compiler_params=pltpu.CompilerParams(
            collective_id=0, has_side_effects=True, vmem_limit_bytes=56 * 2**20
        ),
        cost_estimate=pl.CostEstimate(flops=2 * 10**10, bytes_accessed=3 * 10**7, transcendentals=13 * 10**6),
    )(*args)


def on_device(
    text, gain, wq, wkv, wout, qgain, kgain, gate, images, seg, owner, pos
):
    return fused(
        text, gain, images[0, IMG_TOK - 1 :], wq, wkv, wout, qgain.reshape(1, -1), kgain.reshape(1, -1),
        gate, owner, pos, seg, images,
    )


def solution(mesh):
    rows = ("seq", "section")
    return jax.shard_map(
        on_device,
        mesh=mesh,
        in_specs=(
            P(rows, "tp"),
            P("tp"),
            P(None, "tp"),
            P("tp", None),
            P("tp", None),
            P(),
            P(),
            P(),
            P(rows, None, "tp"),
            P(rows),
            P(rows),
            P(rows),
        ),
        out_specs=P(rows, "tp"),
        check_vma=False,
    )
```

```python
import jax
import jax.numpy as jnp
from jax import lax
from jax.experimental import pallas as pl
from jax.experimental.pallas import tpu as pltpu
from jax.sharding import PartitionSpec as P

MESH = pl.DeviceIdType.MESH
F32, BF16 = jnp.float32, jnp.bfloat16
HD = 128
IMG_TOK = 1601
IMAGES = 16
TOK = 256
QUARTER = 416
BODY = 400
HALF = 2 * QUARTER
EPS = 1e-05
HIDDEN = -30000.0

SUBS = ((256, 48, 32, 48, 32), (0, 64, 64, 64, 64))

EARLY = (('start', 0), ('start', 1))
ORDER = (
    ('text', 1),
    ('ring', 0, 0),
    ('ring', 1, 0),
    ('ring', 0, 1),
    ('text', 2),
    ('ring', 1, 1),
    ('ring', 0, 2),
    ('text', 3),
    ('textp',),
    ('ring', 1, 2),
    ('ring', 0, 3),
    ('text', 4),
    ('PF', 0, 0, 3),
    ('PF', 0, 0, 1),
    ('textc',),
    ('PF', 0, 1, 3),
    ('PF', 0, 1, 1),
    ('PS', 0, 0, 0, 3),
    ('PS', 0, 0, 0, 1),
    ('PS', 0, 1, 0, 3),
    ('PS', 0, 1, 0, 1),
    ('PG', 0, 0),
    ('PS', 0, 0, 3, 3),
    ('PS', 0, 0, 3, 1),
    ('ring', 1, 3),
    ('PS', 0, 0, 1, 3),
    ('PS', 0, 0, 1, 1),
    ('PS', 0, 1, 3, 3),
    ('PS', 0, 1, 3, 1),
    ('PG', 0, 1),
    ('PT', 0, 0, 0),
    ('PS', 0, 1, 1, 3),
    ('PS', 0, 1, 1, 1),
    ('PS', 0, 0, 2, 1),
    ('PS', 0, 0, 2, 3),
    ('q2',),
    ('att', 0, (0, 0), (1, 0), (3, 0), (0, 1)),
    ('PF', 1, 0, 3),
    ('PF', 1, 0, 1),
    ('PT', 0, 0, 3),
    ('PT', 0, 1, 0),
    ('PF', 1, 1, 3),
    ('PS', 1, 0, 0, 3),
    ('PS', 1, 0, 0, 1),
    ('PT', 0, 1, 3),
    ('PF', 1, 1, 1),
    ('PT', 0, 0, 1),
    ('PS', 0, 1, 2, 3),
    ('PS', 1, 1, 0, 3),
    ('PS', 0, 1, 2, 1),
    ('PT', 0, 0, 2),
    ('PS', 1, 1, 0, 1),
    ('att', 0, (0, 3), (1, 1), (1, 3), (3, 1)),
    ('PT', 0, 1, 1),
    ('PS', 1, 0, 3, 3),
    ('PS', 1, 0, 3, 1),
    ('PS', 1, 1, 3, 3),
    ('PS', 1, 0, 1, 3),
    ('PS', 1, 1, 3, 1),
    ('PS', 1, 0, 1, 1),
    ('PG', 1, 0),
    ('att', 0, (3, 3), (2, 0), (0, 2), (2, 1)),
    ('PT', 0, 1, 2),
    ('PT', 1, 0, 0),
    ('PT', 1, 1, 0),
    ('PS', 1, 1, 1, 3),
    ('PS', 1, 1, 1, 1),
    ('PG', 1, 1),
    ('PT', 1, 0, 3),
    ('att', 1, (0, 0), (1, 0), (3, 0), (0, 1)),
    ('PT', 1, 0, 1),
    ('PT', 1, 1, 3),
    ('PT', 1, 1, 1),
    ('PS', 1, 0, 2, 3),
    ('PS', 1, 0, 2, 1),
    ('PS', 1, 1, 2, 1),
    ('att', 0, (2, 3), (1, 2), (3, 2), (2, 2)),
    ('PS', 1, 1, 2, 3),
    ('att', 1, (0, 3), (1, 1), (1, 3), (3, 1)),
    ('PT', 1, 0, 2),
    ('PT', 1, 1, 2),
    ('att', 1, (3, 3), (2, 0), (0, 2), (2, 1)),
    ('att', 1, (2, 3), (1, 2), (3, 2), (2, 2)),
)


def remote(src, dst, send, recv, device):
    return pltpu.make_async_remote_copy(
        src_ref=src, dst_ref=dst, send_sem=send, recv_sem=recv, device_id=device, device_id_type=MESH
    )


class Place:
    def __init__(self):
        seq, tp, sec = lax.axis_index("seq"), lax.axis_index("tp"), lax.axis_index("section")
        self.tp, self.z, self.c = tp, tp // 2, tp % 2
        self.x, self.y = seq // 2, sec * 2 + seq % 2
        self.partner = {"tp": self.z * 2 + 1 - self.c}
        self.up = {"tp": ((self.z + 1) % 8) * 2 + self.c}
        self.down = {"tp": ((self.z + 7) % 8) * 2 + self.c}

    def step(self, axis, delta):
        if axis == "x":
            return {"seq": ((self.x + delta) % 4) * 2 + self.y % 2}
        y = (self.y + delta) % 4
        return {"seq": self.x * 2 + y % 2, "section": y // 2}

    def plane(self, dx, dy):
        y = (self.y + dy) % 4
        return {"seq": ((self.x + dx) % 4) * 2 + y % 2, "section": y // 2}

    def image(self, dx, dy):
        y = (self.y + dy) % 4
        return ((self.x + dx) % 4) * 4 + (y % 2) * 2 + y // 2


def greet(devices):
    barrier = pltpu.get_barrier_semaphore()
    for device in devices:
        pl.semaphore_signal(barrier, inc=1, device_id=device, device_id_type=MESH)
    pl.semaphore_wait(barrier, len(devices))


def kernel(
    text, gain, tail, wq, wkv, wout, qgain, kgain, gate, owner, pos, seg, img,
    out,
    nall, wqv, qacc, imgv, pimg, tailv, wkvv, pwkv, acck, accv, rk, rv, vfirst,
    kv, qrows, wexp, total, metas, half, theirs, mhalf, mtheirs, att, patt, wo, pwo, terms, got, sent,
    load_sem, ex_send, ex_recv, bs, br, ps, pr, cs, cr, as_, ar, acs, acr, ws, wr,
    wo_sem, es, er, ds, dr, qs, qr, ts, tr, ms, mr,
):
    me = Place()
    z, c = me.z, me.c
    zpar = z % 2
    loads = [pltpu.make_async_copy(wkv, wkvv, load_sem.at[0])]
    for k in range(2):
        src = img.at[0, pl.ds(pl.multiple_of(c * 2 * BODY + k * BODY, 16), BODY)]
        loads.append(pltpu.make_async_copy(src, imgv.at[pl.ds(k * QUARTER, BODY)], load_sem.at[1 + k]))
    for k in range(4):
        part = pl.ds(k * 2048, 2048)
        loads.append(pltpu.make_async_copy(wq.at[part], wqv.at[part], load_sem.at[3 + k]))
    for load in loads[:3]:
        load.start()

    row = lax.broadcasted_iota(jnp.int32, (16, 512), 0)
    last = tail[...].astype(F32)
    tailv[...] = jnp.where(row == 16 * c, last, 0.0).astype(BF16)
    imgv[BODY:QUARTER, :] = jnp.zeros((16, 512), BF16)
    pimg[BODY:QUARTER, :] = jnp.zeros((16, 512), BF16)
    imgv[QUARTER + BODY :, :] = jnp.where(row == 16 * (1 - c), last, 0.0).astype(BF16)

    nall[me.tp] = (text[...].astype(F32) * gain[...].astype(F32).reshape(1, 512)).astype(BF16)
    for load in loads[3:7]:
        load.start()

    here = me.image(0, 0)
    row = lax.broadcasted_iota(jnp.int32, (8, HD), 0)
    lane = lax.broadcasted_iota(jnp.int32, (8, HD), 1)
    said = jnp.where(row == 0, owner[0], jnp.where(row == 1, pos[0], 0))
    metas[here] = jnp.where(lane == here, said, 0).astype(F32)
    across = [(dx, dy) for dx in range(4) for dy in range(4) if (dx, dy) != (0, 0)]
    greet([me.partner, me.up, me.down] + [me.plane(*step) for step in across])
    sends = []

    def send(src, dst, ssem, rsem, device):
        copy = remote(src, dst, ssem, rsem, device)
        copy.start()
        sends.append(copy)

    def arrived(ref, ssem, rsem):
        remote(ref, ref, ssem, rsem, me.partner).wait_recv()

    send(wkv, pwkv, ex_send.at[0], ex_recv.at[0], me.partner)
    for k in range(2):
        src = img.at[0, pl.ds(pl.multiple_of((1 - c) * 2 * BODY + k * BODY, 16), BODY)]
        send(src, pimg.at[pl.ds(k * QUARTER, BODY)], ex_send.at[1 + k], ex_recv.at[1 + k], me.partner)
    end = pimg.at[pl.ds(QUARTER + BODY, 16)]
    send(tailv, end, ex_send.at[3], ex_recv.at[3], me.partner)

    shard = lambda k: ((z + k % 8) % 8) * 2 + c

    def text_send(k, way, hop):
        ref = nall.at[shard(k)]
        if hop == 4:
            ref = ref.at[pl.ds(way * 128, 128)]
        send(ref, ref, as_.at[way, hop - 1], ar.at[way, hop - 1], (me.up, me.down)[way])

    def text_share(k):
        ref = nall.at[shard(k)]
        send(ref, ref, acs.at[k % 8], acr.at[k % 8], me.partner)

    def text_arrived(hop, way):
        k = -hop if way == 0 else hop
        ref = nall.at[shard(k)]
        if hop == 4:
            ref = ref.at[pl.ds(way * 128, 128)]
        arrived(ref, as_.at[way, hop - 1], ar.at[way, hop - 1])

    def text_round(hop):
        for way in (0, 1):
            text_arrived(hop, way)
            if hop < 4:
                k = -hop if way == 0 else hop
                text_send(k, way, hop + 1)
                text_share(k)
        if hop == 4:
            text_share(4)

    def text_use(index):
        w = wqv[pl.ds(pl.multiple_of(index * 512, 512), 512), :]
        qacc[...] += jnp.dot(nall[index], w, preferred_element_type=F32)

    def text_shared(k):
        ref = nall.at[((z + k) % 8) * 2 + 1 - c]
        arrived(ref, acs.at[k], acr.at[k])

    def text_most():
        for k in (0, 1, 7, 2, 6, 3, 5):
            text_shared(k)
        for load in loads[3:7]:
            load.wait()
        qacc[...] = jnp.zeros_like(qacc)

        def use(n, carry):
            text_use(((z + 5 + n // 2) % 8) * 2 + n % 2)
            return carry

        lax.fori_loop(0, 14, use, 0)

    def text_compute():
        text_shared(4)
        for k in range(2):
            text_use(((z + 4) % 8) * 2 + k)
        for h in range(2):
            q = qacc[:, h * HD : (h + 1) * HD]
            q = q * lax.rsqrt(jnp.mean(q * q, axis=-1, keepdims=True) + EPS) * qgain[...]
            qrows[h * TOK : (h + 1) * TOK, HD:] = q.astype(BF16)

    text_send(0, 0, 1)
    text_send(0, 1, 1)
    text_share(0)
    for dx, dy in across:
        k = dx * 4 + dy
        send(metas.at[here], metas.at[here], ms.at[k], mr.at[k], me.plane(dx, dy))

    row = lax.broadcasted_iota(jnp.int32, (QUARTER, HD), 0)
    lane = lax.broadcasted_iota(jnp.int32, (QUARTER, HD), 1)
    for q in range(2):
        padding = (lane == IMAGES) & (row >= BODY + zpar * q)

        def name_rows(m, carry):
            kv[m, q * QUARTER : (q + 1) * QUARTER, 0:HD] = jnp.where((lane == m) | padding, 1.0, 0.0).astype(BF16)
            kv[m, q * QUARTER : (q + 1) * QUARTER, 3 * HD :] = jnp.ones((QUARTER, HD), BF16)
            return carry

        lax.fori_loop(0, IMAGES, name_rows, 0)

    def order(n):
        return (z + 4 + jnp.where(n % 2 == 1, -((n + 1) // 2), n // 2)) % 8

    def project(d):
        rows = pl.ds(pl.multiple_of((d % 2) * QUARTER, QUARTER), QUARTER)
        cols = pl.ds(pl.multiple_of((d // 2) * 256, 256), 256)
        part = jnp.dot(imgv[rows, :], wkvv[:, cols], preferred_element_type=F32)
        part += jnp.dot(pimg[rows, :], pwkv[:, cols], preferred_element_type=F32)
        acck[d] = part[:, :HD]
        accv[d] = part[:, HD:]

    def project_next(n, carry):
        project(order(n))
        return carry

    def piece(u, par, part=None):
        start, *sizes = SUBS[u]
        start += par * (sizes[0] + sizes[1])
        pair = sizes[2 * par : 2 * par + 2]
        if part is None:
            return start, pair[0] + pair[1]
        return start + part * pair[0], pair[part]

    def ring_rows(u, way, stage):
        if stage == 0:
            return pl.ds(*piece(u, way))
        return pl.ds(SUBS[u][0], sum(SUBS[u][1:]))

    def ring_send(u, stage):
        for way in (0, 1):
            rows = ring_rows(u, way, stage)
            if stage == 0:
                d = (z + 4) % 8
                vfirst[rows, :] = accv[d, rows, :].astype(BF16)
                srck, srcv = acck.at[d, rows], vfirst.at[rows]
            else:
                srck, srcv = rk.at[way, stage - 1, rows], rv.at[way, stage - 1, rows]
            device = (me.up, me.down)[way]
            send(srck, rk.at[way, stage, rows], bs.at[u, way, stage, 0], br.at[u, way, stage, 0], device)
            send(srcv, rv.at[way, stage, rows], bs.at[u, way, stage, 1], br.at[u, way, stage, 1], device)

    def ring_receive(u, stage):
        for way in (0, 1):
            rows = ring_rows(u, way, stage)
            d = (z + (3 - stage if way == 0 else 5 + stage)) % 8
            if stage == 0:
                other = ring_rows(u, 1 - way, 0)
                rk[way, 0, other, :] = acck[d, other, :]
                rv[way, 0, other, :] = accv[d, other, :].astype(BF16)
            arrived(rk.at[way, stage, rows], bs.at[u, way, stage, 0], br.at[u, way, stage, 0])
            arrived(rv.at[way, stage, rows], bs.at[u, way, stage, 1], br.at[u, way, stage, 1])
            if stage < 3:
                rk[way, stage, rows, :] += acck[d, rows, :]
                rv[way, stage, rows, :] = (rv[way, stage, rows, :].astype(F32) + accv[d, rows, :]).astype(BF16)

    here_rows = lambda start, n: pl.ds(pl.multiple_of(c * QUARTER + start, 16), n)

    def finish(u):
        start, n = SUBS[u][0], sum(SUBS[u][1:])
        rows = pl.ds(start, n)
        key = rk[0, 3, rows, :] + rk[1, 3, rows, :] + acck[z, rows, :]
        val = rv[0, 3, rows, :].astype(F32) + rv[1, 3, rows, :].astype(F32) + accv[z, rows, :]
        key = key * lax.rsqrt(jnp.mean(key * key, axis=-1, keepdims=True) + EPS) * kgain[...]
        kv[here, here_rows(start, n), HD : 2 * HD] = key.astype(BF16)
        kv[here, here_rows(start, n), 2 * HD : 3 * HD] = val.astype(BF16)


    def block(u, par, i, j, part=None):
        m = me.image(i, j) if par == 0 else me.image(j, i)
        return kv.at[m, here_rows(*piece(u, par, part)), pl.ds(HD, 2 * HD)]

    axes = lambda par: ("x", "y") if par == 0 else ("y", "x")

    def spread_first(u, par, i, way, part=None):
        slot = {(0, 0): 0, (0, 1): 1, (3, 0): 2, (1, 1): 3}[(i, way)]
        ref = block(u, par, i, 0, part)
        send(ref, ref, ps.at[u, par, slot], pr.at[u, par, slot], me.step(axes(par)[0], (1, 3)[way]))

    def first_arrived(u, par, i, part=None):
        slot = {(3, None): 0, (1, None): 1, (2, 1): 2, (2, 0): 3}[(i, part)]
        arrived(block(u, par, i, 0, part), ps.at[u, par, slot], pr.at[u, par, slot])

    def spread_second(u, par, i, j, way):
        slot = 4 + 3 * i + (way if j == 0 else 2)
        ref = block(u, par, i, j)
        send(ref, ref, ps.at[u, par, slot], pr.at[u, par, slot], me.step(axes(par)[1], (1, 3)[way]))

    def second_arrived(u, par, i, j):
        slot = 4 + 3 * i + {3: 0, 1: 1, 2: 2}[j]
        arrived(block(u, par, i, j), ps.at[u, par, slot], pr.at[u, par, slot])

    def share(u, par, i, j):
        ref = block(u, par, i, j)
        send(ref, ref, cs.at[u, par, 4 * i + j], cr.at[u, par, 4 * i + j], me.partner)

    def column(u, par, i):
        spread_second(u, par, i, 0, 0)
        spread_second(u, par, i, 0, 1)
        share(u, par, i, 0)

    def spread_start(u):
        for par in (0, 1):
            spread_first(u, par, 0, 0)
            spread_first(u, par, 0, 1)
            column(u, par, 0)

    def spread_first_on(u, par, i):
        first_arrived(u, par, i)
        spread_first(u, par, i, 0 if i == 3 else 1, 1 if i == 3 else 0)
        column(u, par, i)

    def spread_opposite(u, par):
        first_arrived(u, par, 2, 0)
        first_arrived(u, par, 2, 1)
        column(u, par, 2)

    def spread_second_on(u, par, i, j):
        second_arrived(u, par, i, j)
        if (j == 3) == (i < 2):
            spread_second(u, par, i, j, 0 if j == 3 else 1)
        share(u, par, i, j)

    def spread_end(u, par, i):
        second_arrived(u, par, i, 2)
        share(u, par, i, 2)

    total[...] = jnp.zeros_like(total)

    def hide():
        for dx, dy in across:
            ref = metas.at[me.image(dx, dy)]
            k = (4 - dx) % 4 * 4 + (4 - dy) % 4
            arrived(ref, ms.at[k], mr.at[k])
        said = metas[0]
        for m in range(1, IMAGES):
            said += metas[m]
        docs = jnp.broadcast_to(seg[...].astype(F32).reshape(1, TOK), (HD, TOK)).T
        lane = lax.broadcasted_iota(jnp.int32, (TOK, HD), 1)
        place = here * TOK + lax.broadcasted_iota(jnp.int32, (TOK, HD), 0)
        sees = (docs == said[0:1, :]) & (place.astype(F32) >= said[1:2, :])
        unseen = jnp.where(lane < IMAGES, jnp.where(sees, 0.0, HIDDEN), jnp.where(lane == IMAGES, HIDDEN, 0.0))
        for h in range(4):
            qrows[h * TOK : (h + 1) * TOK, 0:HD] = unseen.astype(BF16)

    def attend_images(u, pair):
        start, n = SUBS[u][0], sum(SUBS[u][1:])
        both = lambda lanes: jnp.concatenate(
            [kv[m, q * QUARTER + start : q * QUARTER + start + n, lanes] for m in pair for q in range(2)], axis=0
        )
        keys, values = both(slice(0, 2 * HD)), both(slice(2 * HD, 4 * HD))

        rows = qrows[...]
        for k0 in range(0, 4 * n, 256):
            width = min(256, 4 * n - k0)
            score = lax.dot_general(
                rows, keys[k0 : k0 + width, :], (((1,), (1,)), ((), ())), preferred_element_type=F32
            )
            wexp[:, k0 : k0 + width] = jnp.exp2(score * (HD**-0.5 * 1.4426950408889634)).astype(BF16)
        total[...] += jnp.dot(wexp[:, 0 : 4 * n], values, preferred_element_type=F32)

    def attend(u, images):
        for dx, dy in images:
            for par, i, j in ((0, dx, dy), (1, dy, dx)):
                start, n = piece(u, par)
                rows = pl.ds(pl.multiple_of((1 - c) * QUARTER + start, 16), n)
                ref = kv.at[me.image(dx, dy), rows, pl.ds(HD, 2 * HD)]
                arrived(ref, cs.at[u, par, 4 * i + j], cr.at[u, par, 4 * i + j])
        codes = [4 * dx + dy for dx, dy in images]

        def one(n, carry):
            chosen = []
            for k in range(2):
                code = codes[k]
                for i in range(2, len(codes), 2):
                    code = jnp.where(n == i // 2, codes[i + k], code)
                chosen.append(me.image(code // 4, code % 4))
            attend_images(u, chosen)
            return carry

        lax.fori_loop(0, len(codes) // 2, one, 0)

    def ring_step(u, stage):
        ring_receive(u, stage)
        if stage < 3:
            ring_send(u, stage + 1)
        else:
            finish(u)
            spread_start(u)

    pair = {"tp": (z + 1 - 2 * zpar) * 2 + c}
    own_rows, pair_rows = pl.ds(0, 2 * TOK), pl.ds(2 * TOK, 2 * TOK)

    def queries_swap():
        text_compute()
        lanes = pl.ds(HD, HD)
        send(qrows.at[own_rows, lanes], qrows.at[pair_rows, lanes], qs, qr, pair)
        hide()

    def queries_arrived():
        arrived(qrows.at[pair_rows, pl.ds(HD, HD)], qs, qr)

    handlers = {
        "start": lambda u: ring_send(u, 0),
        "ring": ring_step,
        "PF": spread_first_on,
        "PG": spread_opposite,
        "PS": spread_second_on,
        "PT": spread_end,
        "text": text_round,
        "textp": text_most,
        "textc": queries_swap,
        "q2": queries_arrived,
        "att": lambda u, *images: attend(u, images),
    }

    for load in loads[:3]:
        load.wait()
    arrived(pwkv, ex_send.at[0], ex_recv.at[0])
    for k in range(2):
        arrived(pimg.at[pl.ds(k * QUARTER, BODY)], ex_send.at[1 + k], ex_recv.at[1 + k])
    arrived(end, ex_send.at[3], ex_recv.at[3])
    project((z + 4) % 8)
    for name, *args in EARLY:
        handlers[name](*args)
    lax.fori_loop(1, 8, project_next, 0)
    for k in range(8):
        src = wout.at[:, pl.ds(pl.multiple_of((2 * k + 1 - c) * 512, 512), 512)]
        send(src, pwo.at[k], ws.at[k], wr.at[k], me.partner)
        src = wout.at[:, pl.ds(pl.multiple_of((2 * k + c) * 512, 512), 512)]
        load = pltpu.make_async_copy(src, wo.at[k], wo_sem.at[k])
        load.start()
        loads.append(load)
    for name, *args in ORDER:
        handlers[name](*args)

    half[...] = total[pair_rows, 0:HD].astype(BF16)
    send(half, theirs, ts.at[0], tr.at[0], pair)
    mhalf[...] = total[pair_rows, HD:].T[0:8, :]
    send(mhalf, mtheirs, ts.at[1], tr.at[1], pair)
    arrived(mtheirs, ts.at[1], tr.at[1])
    arrived(theirs, ts.at[0], tr.at[0])
    others = jnp.broadcast_to(mtheirs[0:1, :], (HD, 2 * TOK)).T

    for h in range(2):
        rows = slice(h * TOK, (h + 1) * TOK)
        weight = jnp.maximum(total[rows, HD:] + others[rows], 1.0)
        att[:, h * HD : (h + 1) * HD] = ((total[rows, 0:HD] + theirs[rows, :].astype(F32)) / weight).astype(BF16)

    send(att, patt, es, er, me.partner)

    def term(d):
        part = jnp.dot(att[...], wo[d], preferred_element_type=F32)
        terms[d] = part + jnp.dot(patt[...], pwo[d], preferred_element_type=F32)

    def next_term(n, carry):
        term(order(n))
        return carry

    def term_rows(way, stage):
        return pl.ds(way * 128, 128) if stage == 0 else pl.ds(0, TOK)

    def term_send(e, stage):
        cols = pl.ds(e * 256, 256)
        for way in (0, 1):
            rows = term_rows(way, stage)
            part = terms[(z + (4 - stage if way == 0 else 4 + stage)) % 8, :, cols]
            if stage == 0:
                part = part[way * 128 : way * 128 + 128]
            elif stage == 1:
                parts = [part[:128], part[128:]]
                parts[way] += got[way, 0, way * 128 : way * 128 + 128, cols].astype(F32)
                part = jnp.concatenate(parts, axis=0)
            else:
                part += got[way, stage - 1, :, cols].astype(F32)
            sent[way, stage, rows, cols] = part.astype(BF16)
            send(
                sent.at[way, stage, rows, cols], got.at[way, stage, rows, cols],
                ds.at[e, way, stage], dr.at[e, way, stage], (me.up, me.down)[way],
            )

    def term_arrived(e, stage):
        for way in (0, 1):
            ref = got.at[way, stage, term_rows(way, stage), pl.ds(e * 256, 256)]
            arrived(ref, ds.at[e, way, stage], dr.at[e, way, stage])

    for k in range(8):
        arrived(pwo.at[k], ws.at[k], wr.at[k])
    for load in loads[7:]:
        load.wait()
    arrived(patt, es, er)
    term((z + 4) % 8)
    term_send(0, 0)
    term_send(1, 0)
    lax.fori_loop(1, 8, next_term, 0)
    for stage in range(3):
        for e in (0, 1):
            term_arrived(e, stage)
            term_send(e, stage + 1)
    scale = jnp.tanh(jnp.full((1, 256), gate[0], F32))
    for e in (0, 1):
        term_arrived(e, 3)
        cols = pl.ds(e * 256, 256)
        part = terms[z, :, cols] + got[0, 3, :, cols].astype(F32) + got[1, 3, :, cols].astype(F32)
        out[:, e * 256 : e * 256 + 256] = (scale * part).astype(BF16)

    for copy in sends:
        copy.wait_send()


def fused(*args):
    vmem, anyspace, smem = (pl.BlockSpec(memory_space=m) for m in (pltpu.VMEM, pl.ANY, pltpu.SMEM))
    dma = pltpu.SemaphoreType.DMA
    n = len(SUBS)
    return pl.pallas_call(
        kernel,
        out_shape=jax.ShapeDtypeStruct((TOK, 512), BF16),
        in_specs=[vmem, vmem, vmem, anyspace, anyspace, anyspace, vmem, vmem, smem, smem, smem, vmem, anyspace],
        out_specs=vmem,
        scratch_shapes=[
            pltpu.VMEM((16, TOK, 512), BF16),
            pltpu.VMEM((8192, 256), BF16),
            pltpu.VMEM((TOK, 256), F32),
            pltpu.VMEM((HALF, 512), BF16),
            pltpu.VMEM((HALF, 512), BF16),
            pltpu.VMEM((16, 512), BF16),
            pltpu.VMEM((512, 1024), BF16),
            pltpu.VMEM((512, 1024), BF16),
            pltpu.VMEM((8, QUARTER, HD), F32),
            pltpu.VMEM((8, QUARTER, HD), F32),
            pltpu.VMEM((2, 4, QUARTER, HD), F32),
            pltpu.VMEM((2, 4, QUARTER, HD), BF16),
            pltpu.VMEM((QUARTER, HD), BF16),
            pltpu.VMEM((IMAGES, HALF, 4 * HD), BF16),
            pltpu.VMEM((4 * TOK, 2 * HD), BF16),
            pltpu.VMEM((4 * TOK, 4 * max(sum(sub[1:]) for sub in SUBS)), BF16),
            pltpu.VMEM((4 * TOK, 2 * HD), F32),
            pltpu.VMEM((IMAGES, 8, HD), F32),
            pltpu.VMEM((2 * TOK, HD), BF16),
            pltpu.VMEM((2 * TOK, HD), BF16),
            pltpu.VMEM((8, 2 * TOK), F32),
            pltpu.VMEM((8, 2 * TOK), F32),
            pltpu.VMEM((TOK, 256), BF16),
            pltpu.VMEM((TOK, 256), BF16),
            pltpu.VMEM((8, 256, 512), BF16),
            pltpu.VMEM((8, 256, 512), BF16),
            pltpu.VMEM((8, TOK, 512), F32),
            pltpu.VMEM((2, 4, TOK, 512), BF16),
            pltpu.VMEM((2, 4, TOK, 512), BF16),
            dma((7,)),
            dma((4,)),
            dma((4,)),
            dma((n, 2, 4, 2)),
            dma((n, 2, 4, 2)),
            dma((n, 2, 16)),
            dma((n, 2, 16)),
            dma((n, 2, 16)),
            dma((n, 2, 16)),
            dma((2, 4)),
            dma((2, 4)),
            dma((8,)),
            dma((8,)),
            dma((8,)),
            dma((8,)),
            dma((8,)),
            dma,
            dma,
            dma((2, 2, 4)),
            dma((2, 2, 4)),
            dma,
            dma,
            dma((2,)),
            dma((2,)),
            dma((16,)),
            dma((16,)),
        ],
        compiler_params=pltpu.CompilerParams(
            collective_id=0, has_side_effects=True, vmem_limit_bytes=54 * 2**20
        ),
        cost_estimate=pl.CostEstimate(flops=2 * 10**10, bytes_accessed=3 * 10**7, transcendentals=13 * 10**6),
    )(*args)


def on_device(
    text, gain, wq, wkv, wout, qgain, kgain, gate, images, seg, owner, pos
):
    return fused(
        text, gain, images[0, IMG_TOK - 1 :], wq, wkv, wout, qgain.reshape(1, -1), kgain.reshape(1, -1),
        gate, owner, pos, seg, images,
    )


def solution(mesh):
    rows = ("seq", "section")
    return jax.shard_map(
        on_device,
        mesh=mesh,
        in_specs=(
            P(rows, "tp"),
            P("tp"),
            P(None, "tp"),
            P("tp", None),
            P("tp", None),
            P(),
            P(),
            P(),
            P(rows, None, "tp"),
            P(rows),
            P(rows),
            P(rows),
        ),
        out_specs=P(rows, "tp"),
        check_vma=False,
    )
```

```python
import jax
import jax.numpy as jnp
from jax import lax
from jax.experimental import pallas as pl
from jax.experimental.pallas import tpu as pltpu
from jax.sharding import PartitionSpec as P

MESH = pl.DeviceIdType.MESH
F32, BF16 = jnp.float32, jnp.bfloat16
HD = 128
IMG_TOK = 1601
IMAGES = 16
TOK = 256
QUARTER = 416
BODY = 400
HALF = 2 * QUARTER
EPS = 1e-05
HIDDEN = -30000.0

SUBS = ((256, 48, 32, 48, 32), (0, 64, 64, 64, 64))

EARLY = (('start', 0), ('start', 1))
ORDER = (
    ('text', 1),
    ('ring', 0, 0),
    ('ring', 1, 0),
    ('text', 2),
    ('ring', 0, 1),
    ('ring', 1, 1),
    ('ring', 0, 2),
    ('text', 3),
    ('textp',),
    ('ring', 1, 2),
    ('ring', 0, 3),
    ('text', 4),
    ('PF', 0, 0, 3),
    ('PF', 0, 0, 1),
    ('textc',),
    ('PF', 0, 1, 3),
    ('PF', 0, 1, 1),
    ('PS', 0, 0, 0, 3),
    ('PS', 0, 0, 0, 1),
    ('PS', 0, 1, 0, 3),
    ('PS', 0, 1, 0, 1),
    ('PG', 0, 0),
    ('PS', 0, 0, 3, 3),
    ('PS', 0, 0, 3, 1),
    ('ring', 1, 3),
    ('PS', 0, 0, 1, 3),
    ('PS', 0, 0, 1, 1),
    ('PS', 0, 1, 3, 3),
    ('PS', 0, 1, 3, 1),
    ('PG', 0, 1),
    ('PT', 0, 0, 0),
    ('PS', 0, 1, 1, 3),
    ('PS', 0, 1, 1, 1),
    ('PS', 0, 0, 2, 1),
    ('PS', 0, 0, 2, 3),
    ('q2',),
    ('att', 0, (0, 0), (1, 0), (3, 0), (0, 1)),
    ('PF', 1, 0, 3),
    ('PF', 1, 0, 1),
    ('PT', 0, 0, 3),
    ('PT', 0, 1, 0),
    ('PF', 1, 1, 3),
    ('PS', 1, 0, 0, 3),
    ('PS', 1, 0, 0, 1),
    ('PT', 0, 1, 3),
    ('PF', 1, 1, 1),
    ('PT', 0, 0, 1),
    ('PS', 0, 1, 2, 3),
    ('PS', 1, 1, 0, 3),
    ('PS', 0, 1, 2, 1),
    ('PT', 0, 0, 2),
    ('PS', 1, 1, 0, 1),
    ('att', 0, (0, 3), (1, 1), (1, 3), (3, 1)),
    ('PT', 0, 1, 1),
    ('PS', 1, 0, 3, 3),
    ('PS', 1, 0, 3, 1),
    ('PS', 1, 1, 3, 3),
    ('PS', 1, 0, 1, 3),
    ('PS', 1, 1, 3, 1),
    ('PS', 1, 0, 1, 1),
    ('PG', 1, 0),
    ('att', 0, (3, 3), (2, 0), (0, 2), (2, 1)),
    ('PT', 0, 1, 2),
    ('PT', 1, 0, 0),
    ('PT', 1, 1, 0),
    ('PS', 1, 1, 1, 3),
    ('PS', 1, 1, 1, 1),
    ('PG', 1, 1),
    ('PT', 1, 0, 3),
    ('att', 1, (0, 0), (1, 0), (3, 0), (0, 1)),
    ('PT', 1, 0, 1),
    ('PT', 1, 1, 3),
    ('PT', 1, 1, 1),
    ('PS', 1, 0, 2, 3),
    ('PS', 1, 0, 2, 1),
    ('PS', 1, 1, 2, 1),
    ('att', 0, (2, 3), (1, 2), (3, 2), (2, 2)),
    ('PS', 1, 1, 2, 3),
    ('att', 1, (0, 3), (1, 1), (1, 3), (3, 1)),
    ('PT', 1, 0, 2),
    ('PT', 1, 1, 2),
    ('att', 1, (3, 3), (2, 0), (0, 2), (2, 1)),
    ('att', 1, (2, 3), (1, 2), (3, 2), (2, 2)),
)


def remote(src, dst, send, recv, device):
    return pltpu.make_async_remote_copy(
        src_ref=src, dst_ref=dst, send_sem=send, recv_sem=recv, device_id=device, device_id_type=MESH
    )


class Place:
    def __init__(self):
        seq, tp, sec = lax.axis_index("seq"), lax.axis_index("tp"), lax.axis_index("section")
        self.tp, self.z, self.c = tp, tp // 2, tp % 2
        self.x, self.y = seq // 2, sec * 2 + seq % 2
        self.partner = {"tp": self.z * 2 + 1 - self.c}
        self.up = {"tp": ((self.z + 1) % 8) * 2 + self.c}
        self.down = {"tp": ((self.z + 7) % 8) * 2 + self.c}

    def step(self, axis, delta):
        if axis == "x":
            return {"seq": ((self.x + delta) % 4) * 2 + self.y % 2}
        y = (self.y + delta) % 4
        return {"seq": self.x * 2 + y % 2, "section": y // 2}

    def plane(self, dx, dy):
        y = (self.y + dy) % 4
        return {"seq": ((self.x + dx) % 4) * 2 + y % 2, "section": y // 2}

    def image(self, dx, dy):
        y = (self.y + dy) % 4
        return ((self.x + dx) % 4) * 4 + (y % 2) * 2 + y // 2


def greet(devices):
    barrier = pltpu.get_barrier_semaphore()
    for device in devices:
        pl.semaphore_signal(barrier, inc=1, device_id=device, device_id_type=MESH)
    pl.semaphore_wait(barrier, len(devices))


def kernel(
    text, gain, tail, wq, wkv, wout, qgain, kgain, gate, owner, pos, seg, img,
    out,
    nall, wqv, qacc, imgv, pimg, tailv, wkvv, pwkv, acc, rkv, rk, rv, kv0, k3,
    kv, qrows, wexp, total, metas, half, theirs, mhalf, mtheirs, att, patt, wo, pwo, terms, got, sent,
    load_sem, ex_send, ex_recv, bs, br, ps, pr, cs, cr, as_, ar, acs, acr, ws, wr,
    wo_sem, es, er, ds, dr, qs, qr, ts, tr, ms, mr,
):
    me = Place()
    z, c = me.z, me.c
    zpar = z % 2
    loads = [pltpu.make_async_copy(wkv, wkvv, load_sem.at[0])]
    for k in range(2):
        src = img.at[0, pl.ds(pl.multiple_of(c * 2 * BODY + k * BODY, 16), BODY)]
        loads.append(pltpu.make_async_copy(src, imgv.at[pl.ds(k * QUARTER, BODY)], load_sem.at[1 + k]))
    for k in range(4):
        part = pl.ds(k * 2048, 2048)
        loads.append(pltpu.make_async_copy(wq.at[part], wqv.at[part], load_sem.at[3 + k]))
    for load in loads[:3]:
        load.start()

    row = lax.broadcasted_iota(jnp.int32, (16, 512), 0)
    last = tail[...].astype(F32)
    tailv[...] = jnp.where(row == 16 * c, last, 0.0).astype(BF16)
    imgv[BODY:QUARTER, :] = jnp.zeros((16, 512), BF16)
    pimg[BODY:QUARTER, :] = jnp.zeros((16, 512), BF16)
    imgv[QUARTER + BODY :, :] = jnp.where(row == 16 * (1 - c), last, 0.0).astype(BF16)

    nall[me.tp] = (text[...].astype(F32) * gain[...].astype(F32).reshape(1, 512)).astype(BF16)
    for load in loads[3:7]:
        load.start()

    here = me.image(0, 0)
    row = lax.broadcasted_iota(jnp.int32, (8, HD), 0)
    lane = lax.broadcasted_iota(jnp.int32, (8, HD), 1)
    said = jnp.where(row == 0, owner[0], jnp.where(row == 1, pos[0], 0))
    metas[here] = jnp.where(lane == here, said, 0).astype(F32)
    across = [(dx, dy) for dx in range(4) for dy in range(4) if (dx, dy) != (0, 0)]
    greet([me.partner, me.up, me.down] + [me.plane(*step) for step in across])
    sends = []

    def send(src, dst, ssem, rsem, device):
        copy = remote(src, dst, ssem, rsem, device)
        copy.start()
        sends.append(copy)

    def arrived(ref, ssem, rsem):
        remote(ref, ref, ssem, rsem, me.partner).wait_recv()

    send(wkv, pwkv, ex_send.at[0], ex_recv.at[0], me.partner)
    for k in range(2):
        src = img.at[0, pl.ds(pl.multiple_of((1 - c) * 2 * BODY + k * BODY, 16), BODY)]
        send(src, pimg.at[pl.ds(k * QUARTER, BODY)], ex_send.at[1 + k], ex_recv.at[1 + k], me.partner)
    end = pimg.at[pl.ds(QUARTER + BODY, 16)]
    send(tailv, end, ex_send.at[3], ex_recv.at[3], me.partner)

    shard = lambda k: ((z + k % 8) % 8) * 2 + c

    def text_send(k, way, hop):
        ref = nall.at[shard(k)]
        if hop == 4:
            ref = ref.at[pl.ds(way * 128, 128)]
        send(ref, ref, as_.at[way, hop - 1], ar.at[way, hop - 1], (me.up, me.down)[way])

    def text_share(k):
        ref = nall.at[shard(k)]
        send(ref, ref, acs.at[k % 8], acr.at[k % 8], me.partner)

    def text_arrived(hop, way):
        k = -hop if way == 0 else hop
        ref = nall.at[shard(k)]
        if hop == 4:
            ref = ref.at[pl.ds(way * 128, 128)]
        arrived(ref, as_.at[way, hop - 1], ar.at[way, hop - 1])

    def text_round(hop):
        for way in (0, 1):
            text_arrived(hop, way)
            if hop < 4:
                k = -hop if way == 0 else hop
                text_send(k, way, hop + 1)
                text_share(k)
        if hop == 4:
            text_share(4)

    def text_use(index):
        w = wqv[pl.ds(pl.multiple_of(index * 512, 512), 512), :]
        qacc[...] += jnp.dot(nall[index], w, preferred_element_type=F32)

    def text_shared(k):
        ref = nall.at[((z + k) % 8) * 2 + 1 - c]
        arrived(ref, acs.at[k], acr.at[k])

    def text_most():
        for k in (0, 1, 7, 2, 6, 3, 5):
            text_shared(k)
        for load in loads[3:7]:
            load.wait()
        qacc[...] = jnp.zeros_like(qacc)

        def use(n, carry):
            text_use(((z + 5 + n // 2) % 8) * 2 + n % 2)
            return carry

        lax.fori_loop(0, 14, use, 0)

    def text_compute():
        text_shared(4)
        for k in range(2):
            text_use(((z + 4) % 8) * 2 + k)
        for h in range(2):
            q = qacc[:, h * HD : (h + 1) * HD]
            q = q * lax.rsqrt(jnp.mean(q * q, axis=-1, keepdims=True) + EPS) * qgain[...]
            qrows[h * TOK : (h + 1) * TOK, HD:] = q.astype(BF16)

    text_send(0, 0, 1)
    text_send(0, 1, 1)
    text_share(0)
    for dx, dy in across:
        k = dx * 4 + dy
        send(metas.at[here], metas.at[here], ms.at[k], mr.at[k], me.plane(dx, dy))

    row = lax.broadcasted_iota(jnp.int32, (QUARTER, HD), 0)
    lane = lax.broadcasted_iota(jnp.int32, (QUARTER, HD), 1)
    for q in range(2):
        padding = (lane == IMAGES) & (row >= BODY + zpar * q)

        def name_rows(m, carry):
            kv[m, q * QUARTER : (q + 1) * QUARTER, 0:HD] = jnp.where((lane == m) | padding, 1.0, 0.0).astype(BF16)
            kv[m, q * QUARTER : (q + 1) * QUARTER, 3 * HD :] = jnp.ones((QUARTER, HD), BF16)
            return carry

        lax.fori_loop(0, IMAGES, name_rows, 0)

    def order(n):
        return (z + 4 + jnp.where(n % 2 == 1, -((n + 1) // 2), n // 2)) % 8

    def project(d):
        rows = pl.ds(pl.multiple_of((d % 2) * QUARTER, QUARTER), QUARTER)
        cols = pl.ds(pl.multiple_of((d // 2) * 256, 256), 256)
        part = jnp.dot(imgv[rows, :], wkvv[:, cols], preferred_element_type=F32)
        part += jnp.dot(pimg[rows, :], pwkv[:, cols], preferred_element_type=F32)
        acc[d] = part

    def project_next(n, carry):
        project(order(n))
        return carry

    def piece(u, par, part=None):
        start, *sizes = SUBS[u]
        start += par * (sizes[0] + sizes[1])
        pair = sizes[2 * par : 2 * par + 2]
        if part is None:
            return start, pair[0] + pair[1]
        return start + part * pair[0], pair[part]

    def ring_rows(u, way, stage):
        if stage == 0:
            return pl.ds(*piece(u, way))
        return pl.ds(SUBS[u][0], sum(SUBS[u][1:]))

    def ring_send(u, stage):
        for way in (0, 1):
            rows = ring_rows(u, way, stage)
            device = (me.up, me.down)[way]
            if stage == 0:
                kv0[rows, :] = acc[(z + 4) % 8, rows, :].astype(BF16)
            if stage < 3:
                src = kv0.at[rows] if stage == 0 else rkv.at[way, stage - 1, rows]
                send(src, rkv.at[way, stage, rows], bs.at[u, way, stage], br.at[u, way, stage], device)
            else:
                send(k3.at[way, rows], rk.at[way, rows], bs.at[u, way, 3], br.at[u, way, 3], device)
                send(rkv.at[way, 2, rows, pl.ds(HD, HD)], rv.at[way, rows], bs.at[u, way, 4], br.at[u, way, 4], device)

    def ring_receive(u, stage):
        for way in (0, 1):
            rows = ring_rows(u, way, stage)
            if stage == 3:
                arrived(rk.at[way, rows], bs.at[u, way, 3], br.at[u, way, 3])
                arrived(rv.at[way, rows], bs.at[u, way, 4], br.at[u, way, 4])
                continue
            d = (z + (3 - stage if way == 0 else 5 + stage)) % 8
            if stage == 0:
                other = ring_rows(u, 1 - way, 0)
                rkv[way, 0, other, :] = acc[d, other, :].astype(BF16)
            arrived(rkv.at[way, stage, rows], bs.at[u, way, stage], br.at[u, way, stage])
            part = rkv[way, stage, rows, :].astype(F32) + acc[d, rows, :]
            if stage < 2:
                rkv[way, stage, rows, :] = part.astype(BF16)
            else:
                k3[way, rows, :] = part[:, :HD]
                rkv[way, 2, rows, HD:] = part[:, HD:].astype(BF16)

    here_rows = lambda start, n: pl.ds(pl.multiple_of(c * QUARTER + start, 16), n)

    def finish(u):
        start, n = SUBS[u][0], sum(SUBS[u][1:])
        rows = pl.ds(start, n)
        key = rk[0, rows, :] + rk[1, rows, :] + acc[z, rows, 0:HD]
        val = rv[0, rows, :].astype(F32) + rv[1, rows, :].astype(F32) + acc[z, rows, HD:]
        key = key * lax.rsqrt(jnp.mean(key * key, axis=-1, keepdims=True) + EPS) * kgain[...]
        kv[here, here_rows(start, n), HD : 2 * HD] = key.astype(BF16)
        kv[here, here_rows(start, n), 2 * HD : 3 * HD] = val.astype(BF16)


    def block(u, par, i, j, part=None):
        m = me.image(i, j) if par == 0 else me.image(j, i)
        return kv.at[m, here_rows(*piece(u, par, part)), pl.ds(HD, 2 * HD)]

    axes = lambda par: ("x", "y") if par == 0 else ("y", "x")

    def spread_first(u, par, i, way, part=None):
        slot = {(0, 0): 0, (0, 1): 1, (3, 0): 2, (1, 1): 3}[(i, way)]
        ref = block(u, par, i, 0, part)
        send(ref, ref, ps.at[u, par, slot], pr.at[u, par, slot], me.step(axes(par)[0], (1, 3)[way]))

    def first_arrived(u, par, i, part=None):
        slot = {(3, None): 0, (1, None): 1, (2, 1): 2, (2, 0): 3}[(i, part)]
        arrived(block(u, par, i, 0, part), ps.at[u, par, slot], pr.at[u, par, slot])

    def spread_second(u, par, i, j, way):
        slot = 4 + 3 * i + (way if j == 0 else 2)
        ref = block(u, par, i, j)
        send(ref, ref, ps.at[u, par, slot], pr.at[u, par, slot], me.step(axes(par)[1], (1, 3)[way]))

    def second_arrived(u, par, i, j):
        slot = 4 + 3 * i + {3: 0, 1: 1, 2: 2}[j]
        arrived(block(u, par, i, j), ps.at[u, par, slot], pr.at[u, par, slot])

    def share(u, par, i, j):
        ref = block(u, par, i, j)
        send(ref, ref, cs.at[u, par, 4 * i + j], cr.at[u, par, 4 * i + j], me.partner)

    def column(u, par, i):
        spread_second(u, par, i, 0, 0)
        spread_second(u, par, i, 0, 1)
        share(u, par, i, 0)

    def spread_start(u):
        for par in (0, 1):
            spread_first(u, par, 0, 0)
            spread_first(u, par, 0, 1)
            column(u, par, 0)

    def spread_first_on(u, par, i):
        first_arrived(u, par, i)
        spread_first(u, par, i, 0 if i == 3 else 1, 1 if i == 3 else 0)
        column(u, par, i)

    def spread_opposite(u, par):
        first_arrived(u, par, 2, 0)
        first_arrived(u, par, 2, 1)
        column(u, par, 2)

    def spread_second_on(u, par, i, j):
        second_arrived(u, par, i, j)
        if (j == 3) == (i < 2):
            spread_second(u, par, i, j, 0 if j == 3 else 1)
        share(u, par, i, j)

    def spread_end(u, par, i):
        second_arrived(u, par, i, 2)
        share(u, par, i, 2)

    total[...] = jnp.zeros_like(total)

    def hide():
        for dx, dy in across:
            ref = metas.at[me.image(dx, dy)]
            k = (4 - dx) % 4 * 4 + (4 - dy) % 4
            arrived(ref, ms.at[k], mr.at[k])
        said = metas[0]
        for m in range(1, IMAGES):
            said += metas[m]
        docs = jnp.broadcast_to(seg[...].astype(F32).reshape(1, TOK), (HD, TOK)).T
        lane = lax.broadcasted_iota(jnp.int32, (TOK, HD), 1)
        place = here * TOK + lax.broadcasted_iota(jnp.int32, (TOK, HD), 0)
        sees = (docs == said[0:1, :]) & (place.astype(F32) >= said[1:2, :])
        unseen = jnp.where(lane < IMAGES, jnp.where(sees, 0.0, HIDDEN), jnp.where(lane == IMAGES, HIDDEN, 0.0))
        for h in range(4):
            qrows[h * TOK : (h + 1) * TOK, 0:HD] = unseen.astype(BF16)

    def attend_images(u, pair):
        start, n = SUBS[u][0], sum(SUBS[u][1:])
        both = lambda lanes: jnp.concatenate(
            [kv[m, q * QUARTER + start : q * QUARTER + start + n, lanes] for m in pair for q in range(2)], axis=0
        )
        keys, values = both(slice(0, 2 * HD)), both(slice(2 * HD, 4 * HD))

        rows = qrows[...]
        for k0 in range(0, 4 * n, 256):
            width = min(256, 4 * n - k0)
            score = lax.dot_general(
                rows, keys[k0 : k0 + width, :], (((1,), (1,)), ((), ())), preferred_element_type=F32
            )
            wexp[:, k0 : k0 + width] = jnp.exp2(score * (HD**-0.5 * 1.4426950408889634)).astype(BF16)
        total[...] += jnp.dot(wexp[:, 0 : 4 * n], values, preferred_element_type=F32)

    def attend(u, images):
        for dx, dy in images:
            for par, i, j in ((0, dx, dy), (1, dy, dx)):
                start, n = piece(u, par)
                rows = pl.ds(pl.multiple_of((1 - c) * QUARTER + start, 16), n)
                ref = kv.at[me.image(dx, dy), rows, pl.ds(HD, 2 * HD)]
                arrived(ref, cs.at[u, par, 4 * i + j], cr.at[u, par, 4 * i + j])
        codes = [4 * dx + dy for dx, dy in images]

        def one(n, carry):
            chosen = []
            for k in range(2):
                code = codes[k]
                for i in range(2, len(codes), 2):
                    code = jnp.where(n == i // 2, codes[i + k], code)
                chosen.append(me.image(code // 4, code % 4))
            attend_images(u, chosen)
            return carry

        lax.fori_loop(0, len(codes) // 2, one, 0)

    def ring_step(u, stage):
        ring_receive(u, stage)
        if stage < 3:
            ring_send(u, stage + 1)
        else:
            finish(u)
            spread_start(u)

    pair = {"tp": (z + 1 - 2 * zpar) * 2 + c}
    own_rows, pair_rows = pl.ds(0, 2 * TOK), pl.ds(2 * TOK, 2 * TOK)

    def queries_swap():
        text_compute()
        lanes = pl.ds(HD, HD)
        send(qrows.at[own_rows, lanes], qrows.at[pair_rows, lanes], qs, qr, pair)
        hide()

    def queries_arrived():
        arrived(qrows.at[pair_rows, pl.ds(HD, HD)], qs, qr)

    handlers = {
        "start": lambda u: ring_send(u, 0),
        "ring": ring_step,
        "PF": spread_first_on,
        "PG": spread_opposite,
        "PS": spread_second_on,
        "PT": spread_end,
        "text": text_round,
        "textp": text_most,
        "textc": queries_swap,
        "q2": queries_arrived,
        "att": lambda u, *images: attend(u, images),
    }

    for load in loads[:3]:
        load.wait()
    arrived(pwkv, ex_send.at[0], ex_recv.at[0])
    for k in range(2):
        arrived(pimg.at[pl.ds(k * QUARTER, BODY)], ex_send.at[1 + k], ex_recv.at[1 + k])
    arrived(end, ex_send.at[3], ex_recv.at[3])
    project((z + 4) % 8)
    for name, *args in EARLY:
        handlers[name](*args)
    lax.fori_loop(1, 8, project_next, 0)
    for k in range(8):
        src = wout.at[:, pl.ds(pl.multiple_of((2 * k + 1 - c) * 512, 512), 512)]
        send(src, pwo.at[k], ws.at[k], wr.at[k], me.partner)
        src = wout.at[:, pl.ds(pl.multiple_of((2 * k + c) * 512, 512), 512)]
        load = pltpu.make_async_copy(src, wo.at[k], wo_sem.at[k])
        load.start()
        loads.append(load)
    for name, *args in ORDER:
        handlers[name](*args)

    half[...] = total[pair_rows, 0:HD].astype(BF16)
    send(half, theirs, ts.at[0], tr.at[0], pair)
    mhalf[...] = total[pair_rows, HD:].T[0:8, :]
    send(mhalf, mtheirs, ts.at[1], tr.at[1], pair)
    arrived(mtheirs, ts.at[1], tr.at[1])
    arrived(theirs, ts.at[0], tr.at[0])
    others = jnp.broadcast_to(mtheirs[0:1, :], (HD, 2 * TOK)).T

    for h in range(2):
        rows = slice(h * TOK, (h + 1) * TOK)
        weight = jnp.maximum(total[rows, HD:] + others[rows], 1.0)
        att[:, h * HD : (h + 1) * HD] = ((total[rows, 0:HD] + theirs[rows, :].astype(F32)) / weight).astype(BF16)

    send(att, patt, es, er, me.partner)

    def term(d):
        part = jnp.dot(att[...], wo[d], preferred_element_type=F32)
        terms[d] = part + jnp.dot(patt[...], pwo[d], preferred_element_type=F32)

    def next_term(n, carry):
        term(order(n))
        return carry

    def term_rows(way, stage):
        return pl.ds(way * 128, 128) if stage == 0 else pl.ds(0, TOK)

    def term_send(e, stage):
        cols = pl.ds(e * 256, 256)
        for way in (0, 1):
            rows = term_rows(way, stage)
            part = terms[(z + (4 - stage if way == 0 else 4 + stage)) % 8, :, cols]
            if stage == 0:
                part = part[way * 128 : way * 128 + 128]
            elif stage == 1:
                parts = [part[:128], part[128:]]
                parts[way] += got[way, 0, way * 128 : way * 128 + 128, cols].astype(F32)
                part = jnp.concatenate(parts, axis=0)
            else:
                part += got[way, stage - 1, :, cols].astype(F32)
            sent[way, stage, rows, cols] = part.astype(BF16)
            send(
                sent.at[way, stage, rows, cols], got.at[way, stage, rows, cols],
                ds.at[e, way, stage], dr.at[e, way, stage], (me.up, me.down)[way],
            )

    def term_arrived(e, stage):
        for way in (0, 1):
            ref = got.at[way, stage, term_rows(way, stage), pl.ds(e * 256, 256)]
            arrived(ref, ds.at[e, way, stage], dr.at[e, way, stage])

    for k in range(8):
        arrived(pwo.at[k], ws.at[k], wr.at[k])
    for load in loads[7:]:
        load.wait()
    arrived(patt, es, er)
    term((z + 4) % 8)
    term_send(0, 0)
    term_send(1, 0)
    lax.fori_loop(1, 8, next_term, 0)
    for stage in range(3):
        for e in (0, 1):
            term_arrived(e, stage)
            term_send(e, stage + 1)
    scale = jnp.tanh(jnp.full((1, 256), gate[0], F32))
    for e in (0, 1):
        term_arrived(e, 3)
        cols = pl.ds(e * 256, 256)
        part = terms[z, :, cols] + got[0, 3, :, cols].astype(F32) + got[1, 3, :, cols].astype(F32)
        out[:, e * 256 : e * 256 + 256] = (scale * part).astype(BF16)

    for copy in sends:
        copy.wait_send()


def fused(*args):
    vmem, anyspace, smem = (pl.BlockSpec(memory_space=m) for m in (pltpu.VMEM, pl.ANY, pltpu.SMEM))
    dma = pltpu.SemaphoreType.DMA
    n = len(SUBS)
    return pl.pallas_call(
        kernel,
        out_shape=jax.ShapeDtypeStruct((TOK, 512), BF16),
        in_specs=[vmem, vmem, vmem, anyspace, anyspace, anyspace, vmem, vmem, smem, smem, smem, vmem, anyspace],
        out_specs=vmem,
        scratch_shapes=[
            pltpu.VMEM((16, TOK, 512), BF16),
            pltpu.VMEM((8192, 256), BF16),
            pltpu.VMEM((TOK, 256), F32),
            pltpu.VMEM((HALF, 512), BF16),
            pltpu.VMEM((HALF, 512), BF16),
            pltpu.VMEM((16, 512), BF16),
            pltpu.VMEM((512, 1024), BF16),
            pltpu.VMEM((512, 1024), BF16),
            pltpu.VMEM((8, QUARTER, 2 * HD), F32),
            pltpu.VMEM((2, 3, QUARTER, 2 * HD), BF16),
            pltpu.VMEM((2, QUARTER, HD), F32),
            pltpu.VMEM((2, QUARTER, HD), BF16),
            pltpu.VMEM((QUARTER, 2 * HD), BF16),
            pltpu.VMEM((2, QUARTER, HD), F32),
            pltpu.VMEM((IMAGES, HALF, 4 * HD), BF16),
            pltpu.VMEM((4 * TOK, 2 * HD), BF16),
            pltpu.VMEM((4 * TOK, 4 * max(sum(sub[1:]) for sub in SUBS)), BF16),
            pltpu.VMEM((4 * TOK, 2 * HD), F32),
            pltpu.VMEM((IMAGES, 8, HD), F32),
            pltpu.VMEM((2 * TOK, HD), BF16),
            pltpu.VMEM((2 * TOK, HD), BF16),
            pltpu.VMEM((8, 2 * TOK), F32),
            pltpu.VMEM((8, 2 * TOK), F32),
            pltpu.VMEM((TOK, 256), BF16),
            pltpu.VMEM((TOK, 256), BF16),
            pltpu.VMEM((8, 256, 512), BF16),
            pltpu.VMEM((8, 256, 512), BF16),
            pltpu.VMEM((8, TOK, 512), F32),
            pltpu.VMEM((2, 4, TOK, 512), BF16),
            pltpu.VMEM((2, 4, TOK, 512), BF16),
            dma((7,)),
            dma((4,)),
            dma((4,)),
            dma((n, 2, 5)),
            dma((n, 2, 5)),
            dma((n, 2, 16)),
            dma((n, 2, 16)),
            dma((n, 2, 16)),
            dma((n, 2, 16)),
            dma((2, 4)),
            dma((2, 4)),
            dma((8,)),
            dma((8,)),
            dma((8,)),
            dma((8,)),
            dma((8,)),
            dma,
            dma,
            dma((2, 2, 4)),
            dma((2, 2, 4)),
            dma,
            dma,
            dma((2,)),
            dma((2,)),
            dma((16,)),
            dma((16,)),
        ],
        compiler_params=pltpu.CompilerParams(
            collective_id=0, has_side_effects=True, vmem_limit_bytes=52 * 2**20
        ),
        cost_estimate=pl.CostEstimate(flops=2 * 10**10, bytes_accessed=3 * 10**7, transcendentals=13 * 10**6),
    )(*args)


def on_device(
    text, gain, wq, wkv, wout, qgain, kgain, gate, images, seg, owner, pos
):
    return fused(
        text, gain, images[0, IMG_TOK - 1 :], wq, wkv, wout, qgain.reshape(1, -1), kgain.reshape(1, -1),
        gate, owner, pos, seg, images,
    )


def solution(mesh):
    rows = ("seq", "section")
    return jax.shard_map(
        on_device,
        mesh=mesh,
        in_specs=(
            P(rows, "tp"),
            P("tp"),
            P(None, "tp"),
            P("tp", None),
            P("tp", None),
            P(),
            P(),
            P(),
            P(rows, None, "tp"),
            P(rows),
            P(rows),
            P(rows),
        ),
        out_specs=P(rows, "tp"),
        check_vma=False,
    )
```

```python
import jax
import jax.numpy as jnp
from jax import lax
from jax.experimental import pallas as pl
from jax.experimental.pallas import tpu as pltpu
from jax.sharding import PartitionSpec as P

MESH = pl.DeviceIdType.MESH
F32, BF16 = jnp.float32, jnp.bfloat16
HD = 128
IMG_TOK = 1601
IMAGES = 16
TOK = 256
QUARTER = 416
BODY = 400
HALF = 2 * QUARTER
EPS = 1e-05
HIDDEN = -30000.0

SUBS = ((288, 32, 32, 32, 32), (0, 48, 32, 48, 32), (160, 32, 32, 32, 32))

EARLY = (('start', 0), ('start', 1))
ORDER = (
    ('text', 1),
    ('ring', 0, 0),
    ('ring', 1, 0),
    ('text', 2),
    ('ring', 0, 1),
    ('start', 2),
    ('ring', 1, 1),
    ('ring', 0, 2),
    ('ring', 2, 0),
    ('text', 3),
    ('textp',),
    ('ring', 0, 3),
    ('ring', 1, 2),
    ('ring', 2, 1),
    ('PF', 0, 0, 3),
    ('PF', 0, 0, 1),
    ('PS', 0, 0, 0, 3),
    ('PS', 0, 0, 0, 1),
    ('PS', 0, 1, 0, 3),
    ('PF', 0, 1, 3),
    ('PF', 0, 1, 1),
    ('PS', 0, 1, 0, 1),
    ('text', 4),
    ('textc',),
    ('PS', 0, 0, 3, 3),
    ('PS', 0, 0, 3, 1),
    ('ring', 1, 3),
    ('PT', 0, 1, 0),
    ('PS', 0, 0, 1, 3),
    ('PS', 0, 0, 1, 1),
    ('PS', 0, 1, 3, 1),
    ('PG', 0, 0),
    ('PS', 0, 1, 3, 3),
    ('PT', 0, 0, 0),
    ('PS', 0, 1, 1, 1),
    ('PG', 0, 1),
    ('PS', 0, 1, 1, 3),
    ('ring', 2, 2),
    ('PT', 0, 0, 3),
    ('PF', 1, 0, 3),
    ('PF', 1, 0, 1),
    ('PS', 1, 0, 0, 3),
    ('PS', 1, 0, 0, 1),
    ('PS', 1, 1, 0, 3),
    ('PF', 1, 1, 3),
    ('PS', 1, 1, 0, 1),
    ('q2',),
    ('att', 0, (0, 0), (1, 0), (3, 0), (0, 1)),
    ('PT', 0, 0, 1),
    ('PT', 0, 1, 3),
    ('PT', 0, 1, 1),
    ('PF', 1, 1, 1),
    ('PS', 0, 0, 2, 3),
    ('PS', 0, 0, 2, 1),
    ('ring', 2, 3),
    ('PS', 0, 1, 2, 3),
    ('PS', 0, 1, 2, 1),
    ('PS', 1, 0, 3, 3),
    ('PS', 1, 0, 3, 1),
    ('PG', 1, 0),
    ('att', 0, (0, 3), (1, 1), (1, 3), (3, 1)),
    ('PT', 1, 0, 0),
    ('PT', 1, 1, 0),
    ('PS', 1, 0, 1, 3),
    ('PS', 1, 0, 1, 1),
    ('PS', 1, 1, 3, 3),
    ('PS', 1, 1, 3, 1),
    ('PG', 1, 1),
    ('att', 0, (3, 3), (2, 0), (0, 2), (2, 1)),
    ('PT', 0, 0, 2),
    ('PF', 2, 0, 3),
    ('PF', 2, 0, 1),
    ('PF', 2, 1, 3),
    ('PF', 2, 1, 1),
    ('PS', 1, 0, 2, 3),
    ('PS', 1, 1, 1, 3),
    ('PS', 1, 1, 1, 1),
    ('PS', 2, 0, 0, 3),
    ('PS', 2, 0, 0, 1),
    ('PT', 0, 1, 2),
    ('PS', 2, 1, 0, 3),
    ('PS', 2, 1, 0, 1),
    ('att', 1, (0, 0), (1, 0), (3, 0), (0, 1)),
    ('PT', 1, 0, 3),
    ('PT', 1, 0, 1),
    ('PT', 1, 1, 3),
    ('PS', 1, 0, 2, 1),
    ('PS', 1, 1, 2, 3),
    ('PS', 1, 1, 2, 1),
    ('PS', 2, 0, 3, 3),
    ('PS', 2, 0, 3, 1),
    ('PG', 2, 0),
    ('att', 0, (2, 3), (1, 2), (3, 2), (2, 2)),
    ('PT', 2, 0, 0),
    ('PS', 2, 0, 1, 3),
    ('PS', 2, 0, 1, 1),
    ('PT', 1, 1, 1),
    ('PS', 2, 1, 3, 3),
    ('PS', 2, 1, 3, 1),
    ('PS', 2, 1, 1, 3),
    ('PS', 2, 1, 1, 1),
    ('PG', 2, 1),
    ('att', 1, (0, 3), (1, 1), (1, 3), (3, 1)),
    ('PT', 1, 0, 2),
    ('PT', 1, 1, 2),
    ('PT', 2, 0, 3),
    ('PT', 2, 1, 0),
    ('PS', 2, 0, 2, 3),
    ('att', 1, (3, 3), (2, 0), (0, 2), (2, 1)),
    ('PT', 2, 0, 1),
    ('PT', 2, 1, 3),
    ('PT', 2, 1, 1),
    ('PS', 2, 0, 2, 1),
    ('PS', 2, 1, 2, 3),
    ('PS', 2, 1, 2, 1),
    ('att', 1, (2, 3), (1, 2), (3, 2), (2, 2)),
    ('att', 2, (0, 0), (1, 0), (3, 0), (0, 1)),
    ('PT', 2, 0, 2),
    ('PT', 2, 1, 2),
    ('att', 2, (0, 3), (1, 1), (1, 3), (3, 1)),
    ('fin', 2, (3, 3), (2, 0), (0, 2), (2, 1), (2, 3), (1, 2), (3, 2), (2, 2)),
)


def remote(src, dst, send, recv, device):
    return pltpu.make_async_remote_copy(
        src_ref=src, dst_ref=dst, send_sem=send, recv_sem=recv, device_id=device, device_id_type=MESH
    )


class Place:
    def __init__(self):
        seq, tp, sec = lax.axis_index("seq"), lax.axis_index("tp"), lax.axis_index("section")
        self.tp, self.z, self.c = tp, tp // 2, tp % 2
        self.x, self.y = seq // 2, sec * 2 + seq % 2
        self.partner = {"tp": self.z * 2 + 1 - self.c}
        self.up = {"tp": ((self.z + 1) % 8) * 2 + self.c}
        self.down = {"tp": ((self.z + 7) % 8) * 2 + self.c}

    def step(self, axis, delta):
        if axis == "x":
            return {"seq": ((self.x + delta) % 4) * 2 + self.y % 2}
        y = (self.y + delta) % 4
        return {"seq": self.x * 2 + y % 2, "section": y // 2}

    def plane(self, dx, dy):
        y = (self.y + dy) % 4
        return {"seq": ((self.x + dx) % 4) * 2 + y % 2, "section": y // 2}

    def image(self, dx, dy):
        y = (self.y + dy) % 4
        return ((self.x + dx) % 4) * 4 + (y % 2) * 2 + y // 2


def greet(devices):
    barrier = pltpu.get_barrier_semaphore()
    for device in devices:
        pl.semaphore_signal(barrier, inc=1, device_id=device, device_id_type=MESH)
    pl.semaphore_wait(barrier, len(devices))


def kernel(
    text, gain, tail, wq, wkv, wout, qgain, kgain, gate, owner, pos, seg, img,
    out,
    nall, wqv, qacc, imgv, pimg, tailv, wkvv, pwkv, acck, accv, rk, rv, vfirst,
    kv, qrows, wexp, total, metas, half, theirs, mhalf, mtheirs, att, patt, wo, pwo, terms, got, sent,
    load_sem, ex_send, ex_recv, bs, br, ps, pr, cs, cr, as_, ar, acs, acr, ws, wr,
    wo_sem, es, er, ds, dr, qs, qr, ts, tr, ms, mr,
):
    me = Place()
    z, c = me.z, me.c
    zpar = z % 2
    loads = [pltpu.make_async_copy(wkv, wkvv, load_sem.at[0])]
    for k in range(2):
        src = img.at[0, pl.ds(pl.multiple_of(c * 2 * BODY + k * BODY, 16), BODY)]
        loads.append(pltpu.make_async_copy(src, imgv.at[pl.ds(k * QUARTER, BODY)], load_sem.at[1 + k]))
    for k in range(4):
        part = pl.ds(k * 2048, 2048)
        loads.append(pltpu.make_async_copy(wq.at[part], wqv.at[part], load_sem.at[3 + k]))
    for load in loads[:3]:
        load.start()

    row = lax.broadcasted_iota(jnp.int32, (16, 512), 0)
    last = tail[...].astype(F32)
    tailv[...] = jnp.where(row == 16 * c, last, 0.0).astype(BF16)
    imgv[BODY:QUARTER, :] = jnp.zeros((16, 512), BF16)
    pimg[BODY:QUARTER, :] = jnp.zeros((16, 512), BF16)
    imgv[QUARTER + BODY :, :] = jnp.where(row == 16 * (1 - c), last, 0.0).astype(BF16)

    nall[me.tp] = (text[...].astype(F32) * gain[...].astype(F32).reshape(1, 512)).astype(BF16)
    for load in loads[3:7]:
        load.start()

    here = me.image(0, 0)
    row = lax.broadcasted_iota(jnp.int32, (8, HD), 0)
    lane = lax.broadcasted_iota(jnp.int32, (8, HD), 1)
    said = jnp.where(row == 0, owner[0], jnp.where(row == 1, pos[0], 0))
    metas[here] = jnp.where(lane == here, said, 0).astype(F32)
    across = [(dx, dy) for dx in range(4) for dy in range(4) if (dx, dy) != (0, 0)]
    greet([me.partner, me.up, me.down] + [me.plane(*step) for step in across])
    sends = []

    def send(src, dst, ssem, rsem, device):
        copy = remote(src, dst, ssem, rsem, device)
        copy.start()
        sends.append(copy)

    def arrived(ref, ssem, rsem):
        remote(ref, ref, ssem, rsem, me.partner).wait_recv()

    send(wkv, pwkv, ex_send.at[0], ex_recv.at[0], me.partner)
    for k in range(2):
        src = img.at[0, pl.ds(pl.multiple_of((1 - c) * 2 * BODY + k * BODY, 16), BODY)]
        send(src, pimg.at[pl.ds(k * QUARTER, BODY)], ex_send.at[1 + k], ex_recv.at[1 + k], me.partner)
    end = pimg.at[pl.ds(QUARTER + BODY, 16)]
    send(tailv, end, ex_send.at[3], ex_recv.at[3], me.partner)

    shard = lambda k: ((z + k % 8) % 8) * 2 + c

    def text_send(k, way, hop):
        ref = nall.at[shard(k)]
        if hop == 4:
            ref = ref.at[pl.ds(way * 128, 128)]
        send(ref, ref, as_.at[way, hop - 1], ar.at[way, hop - 1], (me.up, me.down)[way])

    def text_share(k):
        ref = nall.at[shard(k)]
        send(ref, ref, acs.at[k % 8], acr.at[k % 8], me.partner)

    def text_arrived(hop, way):
        k = -hop if way == 0 else hop
        ref = nall.at[shard(k)]
        if hop == 4:
            ref = ref.at[pl.ds(way * 128, 128)]
        arrived(ref, as_.at[way, hop - 1], ar.at[way, hop - 1])

    def text_round(hop):
        for way in (0, 1):
            text_arrived(hop, way)
            if hop < 4:
                k = -hop if way == 0 else hop
                text_send(k, way, hop + 1)
                text_share(k)
        if hop == 4:
            text_share(4)

    def text_use(index):
        w = wqv[pl.ds(pl.multiple_of(index * 512, 512), 512), :]
        qacc[...] += jnp.dot(nall[index], w, preferred_element_type=F32)

    def text_shared(k):
        ref = nall.at[((z + k) % 8) * 2 + 1 - c]
        arrived(ref, acs.at[k], acr.at[k])

    def text_most():
        for k in (0, 1, 7, 2, 6, 3, 5):
            text_shared(k)
        for load in loads[3:7]:
            load.wait()
        qacc[...] = jnp.zeros_like(qacc)

        def use(n, carry):
            text_use(((z + 5 + n // 2) % 8) * 2 + n % 2)
            return carry

        lax.fori_loop(0, 14, use, 0)

    def text_compute():
        text_shared(4)
        for k in range(2):
            text_use(((z + 4) % 8) * 2 + k)
        for h in range(2):
            q = qacc[:, h * HD : (h + 1) * HD]
            q = q * lax.rsqrt(jnp.mean(q * q, axis=-1, keepdims=True) + EPS) * qgain[...]
            qrows[h * TOK : (h + 1) * TOK, HD:] = q.astype(BF16)

    text_send(0, 0, 1)
    text_send(0, 1, 1)
    text_share(0)
    for dx, dy in across:
        k = dx * 4 + dy
        send(metas.at[here], metas.at[here], ms.at[k], mr.at[k], me.plane(dx, dy))

    row = lax.broadcasted_iota(jnp.int32, (QUARTER, HD), 0)
    lane = lax.broadcasted_iota(jnp.int32, (QUARTER, HD), 1)
    for q in range(2):
        padding = (lane == IMAGES) & (row >= BODY + zpar * q)

        def name_rows(m, carry):
            kv[m, q * QUARTER : (q + 1) * QUARTER, 0:HD] = jnp.where((lane == m) | padding, 1.0, 0.0).astype(BF16)
            kv[m, q * QUARTER : (q + 1) * QUARTER, 3 * HD :] = jnp.ones((QUARTER, HD), BF16)
            return carry

        lax.fori_loop(0, IMAGES, name_rows, 0)

    def order(n):
        return (z + 4 + jnp.where(n % 2 == 1, -((n + 1) // 2), n // 2)) % 8

    def project(d):
        rows = pl.ds(pl.multiple_of((d % 2) * QUARTER, QUARTER), QUARTER)
        cols = pl.ds(pl.multiple_of((d // 2) * 256, 256), 256)
        part = jnp.dot(imgv[rows, :], wkvv[:, cols], preferred_element_type=F32)
        part += jnp.dot(pimg[rows, :], pwkv[:, cols], preferred_element_type=F32)
        acck[d] = part[:, :HD]
        accv[d] = part[:, HD:]

    def project_next(n, carry):
        project(order(n))
        return carry

    def piece(u, par, part=None):
        start, *sizes = SUBS[u]
        start += par * (sizes[0] + sizes[1])
        pair = sizes[2 * par : 2 * par + 2]
        if part is None:
            return start, pair[0] + pair[1]
        return start + part * pair[0], pair[part]

    def ring_rows(u, way, stage):
        if stage == 0:
            return pl.ds(*piece(u, way))
        return pl.ds(SUBS[u][0], sum(SUBS[u][1:]))

    def ring_send(u, stage):
        for way in (0, 1):
            rows = ring_rows(u, way, stage)
            if stage == 0:
                d = (z + 4) % 8
                vfirst[rows, :] = accv[d, rows, :].astype(BF16)
                srck, srcv = acck.at[d, rows], vfirst.at[rows]
            else:
                srck, srcv = rk.at[way, stage - 1, rows], rv.at[way, stage - 1, rows]
            device = (me.up, me.down)[way]
            send(srck, rk.at[way, stage, rows], bs.at[u, way, stage, 0], br.at[u, way, stage, 0], device)
            send(srcv, rv.at[way, stage, rows], bs.at[u, way, stage, 1], br.at[u, way, stage, 1], device)

    def ring_receive(u, stage):
        for way in (0, 1):
            rows = ring_rows(u, way, stage)
            d = (z + (3 - stage if way == 0 else 5 + stage)) % 8
            if stage == 0:
                other = ring_rows(u, 1 - way, 0)
                rk[way, 0, other, :] = acck[d, other, :]
                rv[way, 0, other, :] = accv[d, other, :].astype(BF16)
            arrived(rk.at[way, stage, rows], bs.at[u, way, stage, 0], br.at[u, way, stage, 0])
            arrived(rv.at[way, stage, rows], bs.at[u, way, stage, 1], br.at[u, way, stage, 1])
            if stage < 3:
                rk[way, stage, rows, :] += acck[d, rows, :]
                rv[way, stage, rows, :] = (rv[way, stage, rows, :].astype(F32) + accv[d, rows, :]).astype(BF16)

    here_rows = lambda start, n: pl.ds(pl.multiple_of(c * QUARTER + start, 16), n)

    def finish(u):
        start, n = SUBS[u][0], sum(SUBS[u][1:])
        rows = pl.ds(start, n)
        key = rk[0, 3, rows, :] + rk[1, 3, rows, :] + acck[z, rows, :]
        val = rv[0, 3, rows, :].astype(F32) + rv[1, 3, rows, :].astype(F32) + accv[z, rows, :]
        key = key * lax.rsqrt(jnp.mean(key * key, axis=-1, keepdims=True) + EPS) * kgain[...]
        kv[here, here_rows(start, n), HD : 2 * HD] = key.astype(BF16)
        kv[here, here_rows(start, n), 2 * HD : 3 * HD] = val.astype(BF16)


    def block(u, par, i, j, part=None):
        m = me.image(i, j) if par == 0 else me.image(j, i)
        return kv.at[m, here_rows(*piece(u, par, part)), pl.ds(HD, 2 * HD)]

    axes = lambda par: ("x", "y") if par == 0 else ("y", "x")

    def spread_first(u, par, i, way, part=None):
        slot = {(0, 0): 0, (0, 1): 1, (3, 0): 2, (1, 1): 3}[(i, way)]
        ref = block(u, par, i, 0, part)
        send(ref, ref, ps.at[u, par, slot], pr.at[u, par, slot], me.step(axes(par)[0], (1, 3)[way]))

    def first_arrived(u, par, i, part=None):
        slot = {(3, None): 0, (1, None): 1, (2, 1): 2, (2, 0): 3}[(i, part)]
        arrived(block(u, par, i, 0, part), ps.at[u, par, slot], pr.at[u, par, slot])

    def spread_second(u, par, i, j, way):
        slot = 4 + 3 * i + (way if j == 0 else 2)
        ref = block(u, par, i, j)
        send(ref, ref, ps.at[u, par, slot], pr.at[u, par, slot], me.step(axes(par)[1], (1, 3)[way]))

    def second_arrived(u, par, i, j):
        slot = 4 + 3 * i + {3: 0, 1: 1, 2: 2}[j]
        arrived(block(u, par, i, j), ps.at[u, par, slot], pr.at[u, par, slot])

    def share(u, par, i, j):
        ref = block(u, par, i, j)
        send(ref, ref, cs.at[u, par, 4 * i + j], cr.at[u, par, 4 * i + j], me.partner)

    def column(u, par, i):
        spread_second(u, par, i, 0, 0)
        spread_second(u, par, i, 0, 1)
        share(u, par, i, 0)

    def spread_start(u):
        for par in (0, 1):
            spread_first(u, par, 0, 0)
            spread_first(u, par, 0, 1)
            column(u, par, 0)

    def spread_first_on(u, par, i):
        first_arrived(u, par, i)
        spread_first(u, par, i, 0 if i == 3 else 1, 1 if i == 3 else 0)
        column(u, par, i)

    def spread_opposite(u, par):
        first_arrived(u, par, 2, 0)
        first_arrived(u, par, 2, 1)
        column(u, par, 2)

    def spread_second_on(u, par, i, j):
        second_arrived(u, par, i, j)
        if (j == 3) == (i < 2):
            spread_second(u, par, i, j, 0 if j == 3 else 1)
        share(u, par, i, j)

    def spread_end(u, par, i):
        second_arrived(u, par, i, 2)
        share(u, par, i, 2)

    total[...] = jnp.zeros_like(total)

    def hide():
        for dx, dy in across:
            ref = metas.at[me.image(dx, dy)]
            k = (4 - dx) % 4 * 4 + (4 - dy) % 4
            arrived(ref, ms.at[k], mr.at[k])
        said = metas[0]
        for m in range(1, IMAGES):
            said += metas[m]
        docs = jnp.broadcast_to(seg[...].astype(F32).reshape(1, TOK), (HD, TOK)).T
        lane = lax.broadcasted_iota(jnp.int32, (TOK, HD), 1)
        place = here * TOK + lax.broadcasted_iota(jnp.int32, (TOK, HD), 0)
        sees = (docs == said[0:1, :]) & (place.astype(F32) >= said[1:2, :])
        unseen = jnp.where(lane < IMAGES, jnp.where(sees, 0.0, HIDDEN), jnp.where(lane == IMAGES, HIDDEN, 0.0))
        for h in range(4):
            qrows[h * TOK : (h + 1) * TOK, 0:HD] = unseen.astype(BF16)

    def attend_images(u, pair, at=slice(0, 4 * TOK)):
        start, n = SUBS[u][0], sum(SUBS[u][1:])
        both = lambda lanes: jnp.concatenate(
            [kv[m, q * QUARTER + start : q * QUARTER + start + n, lanes] for m in pair for q in range(2)], axis=0
        )
        keys, values = both(slice(0, 2 * HD)), both(slice(2 * HD, 4 * HD))

        rows = qrows[at, :]
        for k0 in range(0, 4 * n, 256):
            width = min(256, 4 * n - k0)
            score = lax.dot_general(
                rows, keys[k0 : k0 + width, :], (((1,), (1,)), ((), ())), preferred_element_type=F32
            )
            wexp[at, k0 : k0 + width] = jnp.exp2(score * (HD**-0.5 * 1.4426950408889634)).astype(BF16)
        total[at, :] += jnp.dot(wexp[at, 0 : 4 * n], values, preferred_element_type=F32)

    def blocks_arrived(u, images):
        for dx, dy in images:
            for par, i, j in ((0, dx, dy), (1, dy, dx)):
                start, n = piece(u, par)
                rows = pl.ds(pl.multiple_of((1 - c) * QUARTER + start, 16), n)
                ref = kv.at[me.image(dx, dy), rows, pl.ds(HD, 2 * HD)]
                arrived(ref, cs.at[u, par, 4 * i + j], cr.at[u, par, 4 * i + j])

    def attend(u, images, at=slice(0, 4 * TOK)):
        codes = [4 * dx + dy for dx, dy in images]

        def one(n, carry):
            chosen = []
            for k in range(2):
                code = codes[k]
                for i in range(2, len(codes), 2):
                    code = jnp.where(n == i // 2, codes[i + k], code)
                chosen.append(me.image(code // 4, code % 4))
            attend_images(u, chosen, at)
            return carry

        lax.fori_loop(0, len(codes) // 2, one, 0)

    def attend_both(u, *images):
        blocks_arrived(u, images)
        attend(u, images)

    def attend_last(u, *images):
        blocks_arrived(u, images)
        attend(u, images, slice(2 * TOK, 4 * TOK))
        half[...] = total[pair_rows, 0:HD].astype(BF16)
        send(half, theirs, ts.at[0], tr.at[0], pair)
        mhalf[...] = total[pair_rows, HD:].T[0:8, :]
        send(mhalf, mtheirs, ts.at[1], tr.at[1], pair)
        attend(u, images, slice(0, 2 * TOK))

    def ring_step(u, stage):
        ring_receive(u, stage)
        if stage < 3:
            ring_send(u, stage + 1)
        else:
            finish(u)
            spread_start(u)

    pair = {"tp": (z + 1 - 2 * zpar) * 2 + c}
    own_rows, pair_rows = pl.ds(0, 2 * TOK), pl.ds(2 * TOK, 2 * TOK)

    def queries_swap():
        text_compute()
        lanes = pl.ds(HD, HD)
        send(qrows.at[own_rows, lanes], qrows.at[pair_rows, lanes], qs, qr, pair)
        hide()

    def queries_arrived():
        arrived(qrows.at[pair_rows, pl.ds(HD, HD)], qs, qr)

    handlers = {
        "start": lambda u: ring_send(u, 0),
        "ring": ring_step,
        "PF": spread_first_on,
        "PG": spread_opposite,
        "PS": spread_second_on,
        "PT": spread_end,
        "text": text_round,
        "textp": text_most,
        "textc": queries_swap,
        "q2": queries_arrived,
        "att": attend_both,
        "fin": attend_last,
    }

    for load in loads[:3]:
        load.wait()
    arrived(pwkv, ex_send.at[0], ex_recv.at[0])
    for k in range(2):
        arrived(pimg.at[pl.ds(k * QUARTER, BODY)], ex_send.at[1 + k], ex_recv.at[1 + k])
    arrived(end, ex_send.at[3], ex_recv.at[3])
    project((z + 4) % 8)
    for name, *args in EARLY:
        handlers[name](*args)
    lax.fori_loop(1, 8, project_next, 0)
    for k in range(8):
        src = wout.at[:, pl.ds(pl.multiple_of((2 * k + 1 - c) * 512, 512), 512)]
        send(src, pwo.at[k], ws.at[k], wr.at[k], me.partner)
        src = wout.at[:, pl.ds(pl.multiple_of((2 * k + c) * 512, 512), 512)]
        load = pltpu.make_async_copy(src, wo.at[k], wo_sem.at[k])
        load.start()
        loads.append(load)
    for name, *args in ORDER:
        handlers[name](*args)

    arrived(mtheirs, ts.at[1], tr.at[1])
    arrived(theirs, ts.at[0], tr.at[0])
    others = jnp.broadcast_to(mtheirs[0:1, :], (HD, 2 * TOK)).T

    for h in range(2):
        rows = slice(h * TOK, (h + 1) * TOK)
        weight = jnp.maximum(total[rows, HD:] + others[rows], 1.0)
        att[:, h * HD : (h + 1) * HD] = ((total[rows, 0:HD] + theirs[rows, :].astype(F32)) / weight).astype(BF16)

    send(att, patt, es, er, me.partner)

    def term(d):
        part = jnp.dot(att[...], wo[d], preferred_element_type=F32)
        terms[d] = part + jnp.dot(patt[...], pwo[d], preferred_element_type=F32)

    def next_term(n, carry):
        term(order(n))
        return carry

    def term_rows(way, stage):
        return pl.ds(way * 128, 128) if stage == 0 else pl.ds(0, TOK)

    def term_send(e, stage):
        cols = pl.ds(e * 256, 256)
        for way in (0, 1):
            rows = term_rows(way, stage)
            part = terms[(z + (4 - stage if way == 0 else 4 + stage)) % 8, :, cols]
            if stage == 0:
                part = part[way * 128 : way * 128 + 128]
            elif stage == 1:
                parts = [part[:128], part[128:]]
                parts[way] += got[way, 0, way * 128 : way * 128 + 128, cols].astype(F32)
                part = jnp.concatenate(parts, axis=0)
            else:
                part += got[way, stage - 1, :, cols].astype(F32)
            sent[way, stage, rows, cols] = part.astype(BF16)
            send(
                sent.at[way, stage, rows, cols], got.at[way, stage, rows, cols],
                ds.at[e, way, stage], dr.at[e, way, stage], (me.up, me.down)[way],
            )

    def term_arrived(e, stage):
        for way in (0, 1):
            ref = got.at[way, stage, term_rows(way, stage), pl.ds(e * 256, 256)]
            arrived(ref, ds.at[e, way, stage], dr.at[e, way, stage])

    for k in range(8):
        arrived(pwo.at[k], ws.at[k], wr.at[k])
    for load in loads[7:]:
        load.wait()
    arrived(patt, es, er)
    term((z + 4) % 8)
    term_send(0, 0)
    term_send(1, 0)
    lax.fori_loop(1, 8, next_term, 0)
    for stage in range(3):
        for e in (0, 1):
            term_arrived(e, stage)
            term_send(e, stage + 1)
    scale = jnp.tanh(jnp.full((1, 256), gate[0], F32))
    for e in (0, 1):
        term_arrived(e, 3)
        cols = pl.ds(e * 256, 256)
        part = terms[z, :, cols] + got[0, 3, :, cols].astype(F32) + got[1, 3, :, cols].astype(F32)
        out[:, e * 256 : e * 256 + 256] = (scale * part).astype(BF16)

    for copy in sends:
        copy.wait_send()


def fused(*args):
    vmem, anyspace, smem = (pl.BlockSpec(memory_space=m) for m in (pltpu.VMEM, pl.ANY, pltpu.SMEM))
    dma = pltpu.SemaphoreType.DMA
    n = len(SUBS)
    return pl.pallas_call(
        kernel,
        out_shape=jax.ShapeDtypeStruct((TOK, 512), BF16),
        in_specs=[vmem, vmem, vmem, anyspace, anyspace, anyspace, vmem, vmem, smem, smem, smem, vmem, anyspace],
        out_specs=vmem,
        scratch_shapes=[
            pltpu.VMEM((16, TOK, 512), BF16),
            pltpu.VMEM((8192, 256), BF16),
            pltpu.VMEM((TOK, 256), F32),
            pltpu.VMEM((HALF, 512), BF16),
            pltpu.VMEM((HALF, 512), BF16),
            pltpu.VMEM((16, 512), BF16),
            pltpu.VMEM((512, 1024), BF16),
            pltpu.VMEM((512, 1024), BF16),
            pltpu.VMEM((8, QUARTER, HD), F32),
            pltpu.VMEM((8, QUARTER, HD), F32),
            pltpu.VMEM((2, 4, QUARTER, HD), F32),
            pltpu.VMEM((2, 4, QUARTER, HD), BF16),
            pltpu.VMEM((QUARTER, HD), BF16),
            pltpu.VMEM((IMAGES, HALF, 4 * HD), BF16),
            pltpu.VMEM((4 * TOK, 2 * HD), BF16),
            pltpu.VMEM((4 * TOK, 4 * max(sum(sub[1:]) for sub in SUBS)), BF16),
            pltpu.VMEM((4 * TOK, 2 * HD), F32),
            pltpu.VMEM((IMAGES, 8, HD), F32),
            pltpu.VMEM((2 * TOK, HD), BF16),
            pltpu.VMEM((2 * TOK, HD), BF16),
            pltpu.VMEM((8, 2 * TOK), F32),
            pltpu.VMEM((8, 2 * TOK), F32),
            pltpu.VMEM((TOK, 256), BF16),
            pltpu.VMEM((TOK, 256), BF16),
            pltpu.VMEM((8, 256, 512), BF16),
            pltpu.VMEM((8, 256, 512), BF16),
            pltpu.VMEM((8, TOK, 512), F32),
            pltpu.VMEM((2, 4, TOK, 512), BF16),
            pltpu.VMEM((2, 4, TOK, 512), BF16),
            dma((7,)),
            dma((4,)),
            dma((4,)),
            dma((n, 2, 4, 2)),
            dma((n, 2, 4, 2)),
            dma((n, 2, 16)),
            dma((n, 2, 16)),
            dma((n, 2, 16)),
            dma((n, 2, 16)),
            dma((2, 4)),
            dma((2, 4)),
            dma((8,)),
            dma((8,)),
            dma((8,)),
            dma((8,)),
            dma((8,)),
            dma,
            dma,
            dma((2, 2, 4)),
            dma((2, 2, 4)),
            dma,
            dma,
            dma((2,)),
            dma((2,)),
            dma((16,)),
            dma((16,)),
        ],
        compiler_params=pltpu.CompilerParams(
            collective_id=0, has_side_effects=True, vmem_limit_bytes=52 * 2**20
        ),
        cost_estimate=pl.CostEstimate(flops=2 * 10**10, bytes_accessed=3 * 10**7, transcendentals=13 * 10**6),
    )(*args)


def on_device(
    text, gain, wq, wkv, wout, qgain, kgain, gate, images, seg, owner, pos
):
    return fused(
        text, gain, images[0, IMG_TOK - 1 :], wq, wkv, wout, qgain.reshape(1, -1), kgain.reshape(1, -1),
        gate, owner, pos, seg, images,
    )


def solution(mesh):
    rows = ("seq", "section")
    return jax.shard_map(
        on_device,
        mesh=mesh,
        in_specs=(
            P(rows, "tp"),
            P("tp"),
            P(None, "tp"),
            P("tp", None),
            P("tp", None),
            P(),
            P(),
            P(),
            P(rows, None, "tp"),
            P(rows),
            P(rows),
            P(rows),
        ),
        out_specs=P(rows, "tp"),
        check_vma=False,
    )
```

```python
import jax
import jax.numpy as jnp
from jax import lax
from jax.experimental import pallas as pl
from jax.experimental.pallas import tpu as pltpu
from jax.sharding import PartitionSpec as P

MESH = pl.DeviceIdType.MESH
F32, BF16 = jnp.float32, jnp.bfloat16
HD = 128
IMG_TOK = 1601
IMAGES = 16
TOK = 256
QUARTER = 416
BODY = 400
HALF = 2 * QUARTER
EPS = 1e-05
HIDDEN = -30000.0

SUBS = ((256, 48, 32, 48, 32), (0, 64, 64, 64, 64))

EARLY = (('start', 0), ('start', 1))
ORDER = (
    ('text', 1),
    ('ring', 0, 0),
    ('ring', 1, 0),
    ('ring', 0, 1),
    ('text', 2),
    ('ring', 1, 1),
    ('ring', 0, 2),
    ('text', 3),
    ('textp',),
    ('ring', 1, 2),
    ('ring', 0, 3),
    ('text', 4),
    ('PF', 0, 0, 3),
    ('PF', 0, 0, 1),
    ('textc',),
    ('PF', 0, 1, 3),
    ('PF', 0, 1, 1),
    ('PS', 0, 0, 0, 3),
    ('PS', 0, 0, 0, 1),
    ('PS', 0, 1, 0, 3),
    ('PS', 0, 1, 0, 1),
    ('PG', 0, 0),
    ('PS', 0, 0, 3, 3),
    ('PS', 0, 0, 3, 1),
    ('ring', 1, 3),
    ('PS', 0, 0, 1, 3),
    ('PS', 0, 0, 1, 1),
    ('PS', 0, 1, 3, 3),
    ('PS', 0, 1, 3, 1),
    ('PG', 0, 1),
    ('PT', 0, 0, 0),
    ('PS', 0, 1, 1, 3),
    ('PS', 0, 1, 1, 1),
    ('PS', 0, 0, 2, 1),
    ('PS', 0, 0, 2, 3),
    ('q2',),
    ('att', 0, (0, 0), (1, 0), (3, 0), (0, 1)),
    ('PF', 1, 0, 3),
    ('PF', 1, 0, 1),
    ('PT', 0, 0, 3),
    ('PT', 0, 1, 0),
    ('PF', 1, 1, 3),
    ('PS', 1, 0, 0, 3),
    ('PS', 1, 0, 0, 1),
    ('PT', 0, 1, 3),
    ('PF', 1, 1, 1),
    ('PT', 0, 0, 1),
    ('PS', 0, 1, 2, 3),
    ('PS', 1, 1, 0, 3),
    ('PS', 0, 1, 2, 1),
    ('PT', 0, 0, 2),
    ('PS', 1, 1, 0, 1),
    ('att', 0, (0, 3), (1, 1), (1, 3), (3, 1)),
    ('PT', 0, 1, 1),
    ('PS', 1, 0, 3, 3),
    ('PS', 1, 0, 3, 1),
    ('PS', 1, 1, 3, 3),
    ('PS', 1, 0, 1, 3),
    ('PS', 1, 1, 3, 1),
    ('PS', 1, 0, 1, 1),
    ('PG', 1, 0),
    ('att', 0, (3, 3), (2, 0), (0, 2), (2, 1)),
    ('PT', 0, 1, 2),
    ('PT', 1, 0, 0),
    ('PT', 1, 1, 0),
    ('PS', 1, 1, 1, 3),
    ('PS', 1, 1, 1, 1),
    ('PG', 1, 1),
    ('PT', 1, 0, 3),
    ('att', 1, (0, 0), (1, 0), (3, 0), (0, 1)),
    ('PT', 1, 0, 1),
    ('PT', 1, 1, 3),
    ('PT', 1, 1, 1),
    ('PS', 1, 0, 2, 3),
    ('PS', 1, 0, 2, 1),
    ('PS', 1, 1, 2, 1),
    ('att', 0, (2, 3), (1, 2), (3, 2), (2, 2)),
    ('PS', 1, 1, 2, 3),
    ('att', 1, (0, 3), (1, 1), (1, 3), (3, 1)),
    ('PT', 1, 0, 2),
    ('PT', 1, 1, 2),
    ('fin', 1, (3, 3), (2, 0), (0, 2), (2, 1), (2, 3), (1, 2), (3, 2), (2, 2)),
)


def remote(src, dst, send, recv, device):
    return pltpu.make_async_remote_copy(
        src_ref=src, dst_ref=dst, send_sem=send, recv_sem=recv, device_id=device, device_id_type=MESH
    )


class Place:
    def __init__(self):
        seq, tp, sec = lax.axis_index("seq"), lax.axis_index("tp"), lax.axis_index("section")
        self.tp, self.z, self.c = tp, tp // 2, tp % 2
        self.x, self.y = seq // 2, sec * 2 + seq % 2
        self.partner = {"tp": self.z * 2 + 1 - self.c}
        self.up = {"tp": ((self.z + 1) % 8) * 2 + self.c}
        self.down = {"tp": ((self.z + 7) % 8) * 2 + self.c}

    def step(self, axis, delta):
        if axis == "x":
            return {"seq": ((self.x + delta) % 4) * 2 + self.y % 2}
        y = (self.y + delta) % 4
        return {"seq": self.x * 2 + y % 2, "section": y // 2}

    def plane(self, dx, dy):
        y = (self.y + dy) % 4
        return {"seq": ((self.x + dx) % 4) * 2 + y % 2, "section": y // 2}

    def image(self, dx, dy):
        y = (self.y + dy) % 4
        return ((self.x + dx) % 4) * 4 + (y % 2) * 2 + y // 2


def greet(devices):
    barrier = pltpu.get_barrier_semaphore()
    for device in devices:
        pl.semaphore_signal(barrier, inc=1, device_id=device, device_id_type=MESH)
    pl.semaphore_wait(barrier, len(devices))


def kernel(
    text, gain, tail, wq, wkv, wout, qgain, kgain, gate, owner, pos, seg, img,
    out,
    nall, wqv, qacc, imgv, pimg, tailv, wkvv, pwkv, acck, accv, rk, rv, vfirst,
    kv, qrows, wexp, total, metas, half, theirs, mhalf, mtheirs, att, patt, wo, pwo, terms, got, sent,
    load_sem, ex_send, ex_recv, bs, br, ps, pr, cs, cr, as_, ar, acs, acr, ws, wr,
    wo_sem, es, er, ds, dr, qs, qr, ts, tr, ms, mr,
):
    me = Place()
    z, c = me.z, me.c
    zpar = z % 2
    loads = [pltpu.make_async_copy(wkv, wkvv, load_sem.at[0])]
    for k in range(2):
        src = img.at[0, pl.ds(pl.multiple_of(c * 2 * BODY + k * BODY, 16), BODY)]
        loads.append(pltpu.make_async_copy(src, imgv.at[pl.ds(k * QUARTER, BODY)], load_sem.at[1 + k]))
    for k in range(4):
        part = pl.ds(k * 2048, 2048)
        loads.append(pltpu.make_async_copy(wq.at[part], wqv.at[part], load_sem.at[3 + k]))
    for load in loads[:3]:
        load.start()

    row = lax.broadcasted_iota(jnp.int32, (16, 512), 0)
    last = tail[...].astype(F32)
    tailv[...] = jnp.where(row == 16 * c, last, 0.0).astype(BF16)
    imgv[BODY:QUARTER, :] = jnp.zeros((16, 512), BF16)
    pimg[BODY:QUARTER, :] = jnp.zeros((16, 512), BF16)
    imgv[QUARTER + BODY :, :] = jnp.where(row == 16 * (1 - c), last, 0.0).astype(BF16)

    nall[me.tp] = (text[...].astype(F32) * gain[...].astype(F32).reshape(1, 512)).astype(BF16)
    for load in loads[3:7]:
        load.start()

    here = me.image(0, 0)
    row = lax.broadcasted_iota(jnp.int32, (8, HD), 0)
    lane = lax.broadcasted_iota(jnp.int32, (8, HD), 1)
    said = jnp.where(row == 0, owner[0], jnp.where(row == 1, pos[0], 0))
    metas[here] = jnp.where(lane == here, said, 0).astype(F32)
    across = [(dx, dy) for dx in range(4) for dy in range(4) if (dx, dy) != (0, 0)]
    greet([me.partner, me.up, me.down] + [me.plane(*step) for step in across])
    sends = []

    def send(src, dst, ssem, rsem, device):
        copy = remote(src, dst, ssem, rsem, device)
        copy.start()
        sends.append(copy)

    def arrived(ref, ssem, rsem):
        remote(ref, ref, ssem, rsem, me.partner).wait_recv()

    send(wkv, pwkv, ex_send.at[0], ex_recv.at[0], me.partner)
    for k in range(2):
        src = img.at[0, pl.ds(pl.multiple_of((1 - c) * 2 * BODY + k * BODY, 16), BODY)]
        send(src, pimg.at[pl.ds(k * QUARTER, BODY)], ex_send.at[1 + k], ex_recv.at[1 + k], me.partner)
    end = pimg.at[pl.ds(QUARTER + BODY, 16)]
    send(tailv, end, ex_send.at[3], ex_recv.at[3], me.partner)

    shard = lambda k: ((z + k % 8) % 8) * 2 + c

    def text_send(k, way, hop):
        ref = nall.at[shard(k)]
        if hop == 4:
            ref = ref.at[pl.ds(way * 128, 128)]
        send(ref, ref, as_.at[way, hop - 1], ar.at[way, hop - 1], (me.up, me.down)[way])

    def text_share(k):
        ref = nall.at[shard(k)]
        send(ref, ref, acs.at[k % 8], acr.at[k % 8], me.partner)

    def text_arrived(hop, way):
        k = -hop if way == 0 else hop
        ref = nall.at[shard(k)]
        if hop == 4:
            ref = ref.at[pl.ds(way * 128, 128)]
        arrived(ref, as_.at[way, hop - 1], ar.at[way, hop - 1])

    def text_round(hop):
        for way in (0, 1):
            text_arrived(hop, way)
            if hop < 4:
                k = -hop if way == 0 else hop
                text_send(k, way, hop + 1)
                text_share(k)
        if hop == 4:
            text_share(4)

    def text_use(index):
        w = wqv[pl.ds(pl.multiple_of(index * 512, 512), 512), :]
        qacc[...] += jnp.dot(nall[index], w, preferred_element_type=F32)

    def text_shared(k):
        ref = nall.at[((z + k) % 8) * 2 + 1 - c]
        arrived(ref, acs.at[k], acr.at[k])

    def text_most():
        for k in (0, 1, 7, 2, 6, 3, 5):
            text_shared(k)
        for load in loads[3:7]:
            load.wait()
        qacc[...] = jnp.zeros_like(qacc)

        def use(n, carry):
            text_use(((z + 5 + n // 2) % 8) * 2 + n % 2)
            return carry

        lax.fori_loop(0, 14, use, 0)

    def text_compute():
        text_shared(4)
        for k in range(2):
            text_use(((z + 4) % 8) * 2 + k)
        for h in range(2):
            q = qacc[:, h * HD : (h + 1) * HD]
            q = q * lax.rsqrt(jnp.mean(q * q, axis=-1, keepdims=True) + EPS) * qgain[...]
            qrows[h * TOK : (h + 1) * TOK, HD:] = q.astype(BF16)

    text_send(0, 0, 1)
    text_send(0, 1, 1)
    text_share(0)
    for dx, dy in across:
        k = dx * 4 + dy
        send(metas.at[here], metas.at[here], ms.at[k], mr.at[k], me.plane(dx, dy))

    row = lax.broadcasted_iota(jnp.int32, (QUARTER, HD), 0)
    lane = lax.broadcasted_iota(jnp.int32, (QUARTER, HD), 1)
    for q in range(2):
        padding = (lane == IMAGES) & (row >= BODY + zpar * q)

        def name_rows(m, carry):
            kv[m, q * QUARTER : (q + 1) * QUARTER, 0:HD] = jnp.where((lane == m) | padding, 1.0, 0.0).astype(BF16)
            kv[m, q * QUARTER : (q + 1) * QUARTER, 3 * HD :] = jnp.ones((QUARTER, HD), BF16)
            return carry

        lax.fori_loop(0, IMAGES, name_rows, 0)

    def order(n):
        return (z + 4 + jnp.where(n % 2 == 1, -((n + 1) // 2), n // 2)) % 8

    def project(d):
        rows = pl.ds(pl.multiple_of((d % 2) * QUARTER, QUARTER), QUARTER)
        cols = pl.ds(pl.multiple_of((d // 2) * 256, 256), 256)
        part = jnp.dot(imgv[rows, :], wkvv[:, cols], preferred_element_type=F32)
        part += jnp.dot(pimg[rows, :], pwkv[:, cols], preferred_element_type=F32)
        acck[d] = part[:, :HD]
        accv[d] = part[:, HD:]

    def project_next(n, carry):
        project(order(n))
        return carry

    def piece(u, par, part=None):
        start, *sizes = SUBS[u]
        start += par * (sizes[0] + sizes[1])
        pair = sizes[2 * par : 2 * par + 2]
        if part is None:
            return start, pair[0] + pair[1]
        return start + part * pair[0], pair[part]

    def ring_rows(u, way, stage):
        if stage == 0:
            return pl.ds(*piece(u, way))
        return pl.ds(SUBS[u][0], sum(SUBS[u][1:]))

    def ring_send(u, stage):
        for way in (0, 1):
            rows = ring_rows(u, way, stage)
            if stage == 0:
                d = (z + 4) % 8
                vfirst[rows, :] = accv[d, rows, :].astype(BF16)
                srck, srcv = acck.at[d, rows], vfirst.at[rows]
            else:
                srck, srcv = rk.at[way, stage - 1, rows], rv.at[way, stage - 1, rows]
            device = (me.up, me.down)[way]
            send(srck, rk.at[way, stage, rows], bs.at[u, way, stage, 0], br.at[u, way, stage, 0], device)
            send(srcv, rv.at[way, stage, rows], bs.at[u, way, stage, 1], br.at[u, way, stage, 1], device)

    def ring_receive(u, stage):
        for way in (0, 1):
            rows = ring_rows(u, way, stage)
            d = (z + (3 - stage if way == 0 else 5 + stage)) % 8
            if stage == 0:
                other = ring_rows(u, 1 - way, 0)
                rk[way, 0, other, :] = acck[d, other, :]
                rv[way, 0, other, :] = accv[d, other, :].astype(BF16)
            arrived(rk.at[way, stage, rows], bs.at[u, way, stage, 0], br.at[u, way, stage, 0])
            arrived(rv.at[way, stage, rows], bs.at[u, way, stage, 1], br.at[u, way, stage, 1])
            if stage < 3:
                rk[way, stage, rows, :] += acck[d, rows, :]
                rv[way, stage, rows, :] = (rv[way, stage, rows, :].astype(F32) + accv[d, rows, :]).astype(BF16)

    here_rows = lambda start, n: pl.ds(pl.multiple_of(c * QUARTER + start, 16), n)

    def finish(u):
        start, n = SUBS[u][0], sum(SUBS[u][1:])
        rows = pl.ds(start, n)
        key = rk[0, 3, rows, :] + rk[1, 3, rows, :] + acck[z, rows, :]
        val = rv[0, 3, rows, :].astype(F32) + rv[1, 3, rows, :].astype(F32) + accv[z, rows, :]
        key = key * lax.rsqrt(jnp.mean(key * key, axis=-1, keepdims=True) + EPS) * kgain[...]
        kv[here, here_rows(start, n), HD : 2 * HD] = key.astype(BF16)
        kv[here, here_rows(start, n), 2 * HD : 3 * HD] = val.astype(BF16)


    def block(u, par, i, j, part=None):
        m = me.image(i, j) if par == 0 else me.image(j, i)
        return kv.at[m, here_rows(*piece(u, par, part)), pl.ds(HD, 2 * HD)]

    axes = lambda par: ("x", "y") if par == 0 else ("y", "x")

    def spread_first(u, par, i, way, part=None):
        slot = {(0, 0): 0, (0, 1): 1, (3, 0): 2, (1, 1): 3}[(i, way)]
        ref = block(u, par, i, 0, part)
        send(ref, ref, ps.at[u, par, slot], pr.at[u, par, slot], me.step(axes(par)[0], (1, 3)[way]))

    def first_arrived(u, par, i, part=None):
        slot = {(3, None): 0, (1, None): 1, (2, 1): 2, (2, 0): 3}[(i, part)]
        arrived(block(u, par, i, 0, part), ps.at[u, par, slot], pr.at[u, par, slot])

    def spread_second(u, par, i, j, way):
        slot = 4 + 3 * i + (way if j == 0 else 2)
        ref = block(u, par, i, j)
        send(ref, ref, ps.at[u, par, slot], pr.at[u, par, slot], me.step(axes(par)[1], (1, 3)[way]))

    def second_arrived(u, par, i, j):
        slot = 4 + 3 * i + {3: 0, 1: 1, 2: 2}[j]
        arrived(block(u, par, i, j), ps.at[u, par, slot], pr.at[u, par, slot])

    def share(u, par, i, j):
        ref = block(u, par, i, j)
        send(ref, ref, cs.at[u, par, 4 * i + j], cr.at[u, par, 4 * i + j], me.partner)

    def column(u, par, i):
        spread_second(u, par, i, 0, 0)
        spread_second(u, par, i, 0, 1)
        share(u, par, i, 0)

    def spread_start(u):
        for par in (0, 1):
            spread_first(u, par, 0, 0)
            spread_first(u, par, 0, 1)
            column(u, par, 0)

    def spread_first_on(u, par, i):
        first_arrived(u, par, i)
        spread_first(u, par, i, 0 if i == 3 else 1, 1 if i == 3 else 0)
        column(u, par, i)

    def spread_opposite(u, par):
        first_arrived(u, par, 2, 0)
        first_arrived(u, par, 2, 1)
        column(u, par, 2)

    def spread_second_on(u, par, i, j):
        second_arrived(u, par, i, j)
        if (j == 3) == (i < 2):
            spread_second(u, par, i, j, 0 if j == 3 else 1)
        share(u, par, i, j)

    def spread_end(u, par, i):
        second_arrived(u, par, i, 2)
        share(u, par, i, 2)

    total[...] = jnp.zeros_like(total)

    def hide():
        for dx, dy in across:
            ref = metas.at[me.image(dx, dy)]
            k = (4 - dx) % 4 * 4 + (4 - dy) % 4
            arrived(ref, ms.at[k], mr.at[k])
        said = metas[0]
        for m in range(1, IMAGES):
            said += metas[m]
        docs = jnp.broadcast_to(seg[...].astype(F32).reshape(1, TOK), (HD, TOK)).T
        lane = lax.broadcasted_iota(jnp.int32, (TOK, HD), 1)
        place = here * TOK + lax.broadcasted_iota(jnp.int32, (TOK, HD), 0)
        sees = (docs == said[0:1, :]) & (place.astype(F32) >= said[1:2, :])
        unseen = jnp.where(lane < IMAGES, jnp.where(sees, 0.0, HIDDEN), jnp.where(lane == IMAGES, HIDDEN, 0.0))
        for h in range(4):
            qrows[h * TOK : (h + 1) * TOK, 0:HD] = unseen.astype(BF16)

    def attend_images(u, pair, at=slice(0, 4 * TOK)):
        start, n = SUBS[u][0], sum(SUBS[u][1:])
        both = lambda lanes: jnp.concatenate(
            [kv[m, q * QUARTER + start : q * QUARTER + start + n, lanes] for m in pair for q in range(2)], axis=0
        )
        keys, values = both(slice(0, 2 * HD)), both(slice(2 * HD, 4 * HD))

        rows = qrows[at, :]
        for k0 in range(0, 4 * n, 256):
            width = min(256, 4 * n - k0)
            score = lax.dot_general(
                rows, keys[k0 : k0 + width, :], (((1,), (1,)), ((), ())), preferred_element_type=F32
            )
            wexp[at, k0 : k0 + width] = jnp.exp2(score * (HD**-0.5 * 1.4426950408889634)).astype(BF16)
        total[at, :] += jnp.dot(wexp[at, 0 : 4 * n], values, preferred_element_type=F32)

    def blocks_arrived(u, images):
        for dx, dy in images:
            for par, i, j in ((0, dx, dy), (1, dy, dx)):
                start, n = piece(u, par)
                rows = pl.ds(pl.multiple_of((1 - c) * QUARTER + start, 16), n)
                ref = kv.at[me.image(dx, dy), rows, pl.ds(HD, 2 * HD)]
                arrived(ref, cs.at[u, par, 4 * i + j], cr.at[u, par, 4 * i + j])

    def attend(u, images, at=slice(0, 4 * TOK)):
        codes = [4 * dx + dy for dx, dy in images]

        def one(n, carry):
            chosen = []
            for k in range(2):
                code = codes[k]
                for i in range(2, len(codes), 2):
                    code = jnp.where(n == i // 2, codes[i + k], code)
                chosen.append(me.image(code // 4, code % 4))
            attend_images(u, chosen, at)
            return carry

        lax.fori_loop(0, len(codes) // 2, one, 0)

    def attend_both(u, *images):
        blocks_arrived(u, images)
        attend(u, images)

    def attend_last(u, *images):
        blocks_arrived(u, images)
        attend(u, images, slice(2 * TOK, 4 * TOK))
        half[...] = total[pair_rows, 0:HD].astype(BF16)
        send(half, theirs, ts.at[0], tr.at[0], pair)
        mhalf[...] = total[pair_rows, HD:].T[0:8, :]
        send(mhalf, mtheirs, ts.at[1], tr.at[1], pair)
        attend(u, images, slice(0, 2 * TOK))

    def ring_step(u, stage):
        ring_receive(u, stage)
        if stage < 3:
            ring_send(u, stage + 1)
        else:
            finish(u)
            spread_start(u)

    pair = {"tp": (z + 1 - 2 * zpar) * 2 + c}
    own_rows, pair_rows = pl.ds(0, 2 * TOK), pl.ds(2 * TOK, 2 * TOK)

    def queries_swap():
        text_compute()
        lanes = pl.ds(HD, HD)
        send(qrows.at[own_rows, lanes], qrows.at[pair_rows, lanes], qs, qr, pair)
        hide()

    def queries_arrived():
        arrived(qrows.at[pair_rows, pl.ds(HD, HD)], qs, qr)

    handlers = {
        "start": lambda u: ring_send(u, 0),
        "ring": ring_step,
        "PF": spread_first_on,
        "PG": spread_opposite,
        "PS": spread_second_on,
        "PT": spread_end,
        "text": text_round,
        "textp": text_most,
        "textc": queries_swap,
        "q2": queries_arrived,
        "att": attend_both,
        "fin": attend_last,
    }

    for load in loads[:3]:
        load.wait()
    arrived(pwkv, ex_send.at[0], ex_recv.at[0])
    for k in range(2):
        arrived(pimg.at[pl.ds(k * QUARTER, BODY)], ex_send.at[1 + k], ex_recv.at[1 + k])
    arrived(end, ex_send.at[3], ex_recv.at[3])
    project((z + 4) % 8)
    for name, *args in EARLY:
        handlers[name](*args)
    lax.fori_loop(1, 8, project_next, 0)
    for k in range(8):
        src = wout.at[:, pl.ds(pl.multiple_of((2 * k + 1 - c) * 512, 512), 512)]
        send(src, pwo.at[k], ws.at[k], wr.at[k], me.partner)
        src = wout.at[:, pl.ds(pl.multiple_of((2 * k + c) * 512, 512), 512)]
        load = pltpu.make_async_copy(src, wo.at[k], wo_sem.at[k])
        load.start()
        loads.append(load)
    for name, *args in ORDER:
        handlers[name](*args)

    arrived(mtheirs, ts.at[1], tr.at[1])
    arrived(theirs, ts.at[0], tr.at[0])
    others = jnp.broadcast_to(mtheirs[0:1, :], (HD, 2 * TOK)).T

    for h in range(2):
        rows = slice(h * TOK, (h + 1) * TOK)
        weight = jnp.maximum(total[rows, HD:] + others[rows], 1.0)
        att[:, h * HD : (h + 1) * HD] = ((total[rows, 0:HD] + theirs[rows, :].astype(F32)) / weight).astype(BF16)

    send(att, patt, es, er, me.partner)

    def term(d):
        part = jnp.dot(att[...], wo[d], preferred_element_type=F32)
        terms[d] = part + jnp.dot(patt[...], pwo[d], preferred_element_type=F32)

    def next_term(n, carry):
        term(order(n))
        return carry

    def term_rows(way, stage):
        return pl.ds(way * 128, 128) if stage == 0 else pl.ds(0, TOK)

    def term_send(e, stage):
        cols = pl.ds(e * 256, 256)
        for way in (0, 1):
            rows = term_rows(way, stage)
            part = terms[(z + (4 - stage if way == 0 else 4 + stage)) % 8, :, cols]
            if stage == 0:
                part = part[way * 128 : way * 128 + 128]
            elif stage == 1:
                parts = [part[:128], part[128:]]
                parts[way] += got[way, 0, way * 128 : way * 128 + 128, cols].astype(F32)
                part = jnp.concatenate(parts, axis=0)
            else:
                part += got[way, stage - 1, :, cols].astype(F32)
            sent[way, stage, rows, cols] = part.astype(BF16)
            send(
                sent.at[way, stage, rows, cols], got.at[way, stage, rows, cols],
                ds.at[e, way, stage], dr.at[e, way, stage], (me.up, me.down)[way],
            )

    def term_arrived(e, stage):
        for way in (0, 1):
            ref = got.at[way, stage, term_rows(way, stage), pl.ds(e * 256, 256)]
            arrived(ref, ds.at[e, way, stage], dr.at[e, way, stage])

    for k in range(8):
        arrived(pwo.at[k], ws.at[k], wr.at[k])
    for load in loads[7:]:
        load.wait()
    arrived(patt, es, er)
    term((z + 4) % 8)
    term_send(0, 0)
    term_send(1, 0)
    lax.fori_loop(1, 8, next_term, 0)
    for stage in range(3):
        for e in (0, 1):
            term_arrived(e, stage)
            term_send(e, stage + 1)
    scale = jnp.tanh(jnp.full((1, 256), gate[0], F32))
    for e in (0, 1):
        term_arrived(e, 3)
        cols = pl.ds(e * 256, 256)
        part = terms[z, :, cols] + got[0, 3, :, cols].astype(F32) + got[1, 3, :, cols].astype(F32)
        out[:, e * 256 : e * 256 + 256] = (scale * part).astype(BF16)

    for copy in sends:
        copy.wait_send()


def fused(*args):
    vmem, anyspace, smem = (pl.BlockSpec(memory_space=m) for m in (pltpu.VMEM, pl.ANY, pltpu.SMEM))
    dma = pltpu.SemaphoreType.DMA
    n = len(SUBS)
    return pl.pallas_call(
        kernel,
        out_shape=jax.ShapeDtypeStruct((TOK, 512), BF16),
        in_specs=[vmem, vmem, vmem, anyspace, anyspace, anyspace, vmem, vmem, smem, smem, smem, vmem, anyspace],
        out_specs=vmem,
        scratch_shapes=[
            pltpu.VMEM((16, TOK, 512), BF16),
            pltpu.VMEM((8192, 256), BF16),
            pltpu.VMEM((TOK, 256), F32),
            pltpu.VMEM((HALF, 512), BF16),
            pltpu.VMEM((HALF, 512), BF16),
            pltpu.VMEM((16, 512), BF16),
            pltpu.VMEM((512, 1024), BF16),
            pltpu.VMEM((512, 1024), BF16),
            pltpu.VMEM((8, QUARTER, HD), F32),
            pltpu.VMEM((8, QUARTER, HD), F32),
            pltpu.VMEM((2, 4, QUARTER, HD), F32),
            pltpu.VMEM((2, 4, QUARTER, HD), BF16),
            pltpu.VMEM((QUARTER, HD), BF16),
            pltpu.VMEM((IMAGES, HALF, 4 * HD), BF16),
            pltpu.VMEM((4 * TOK, 2 * HD), BF16),
            pltpu.VMEM((4 * TOK, 4 * max(sum(sub[1:]) for sub in SUBS)), BF16),
            pltpu.VMEM((4 * TOK, 2 * HD), F32),
            pltpu.VMEM((IMAGES, 8, HD), F32),
            pltpu.VMEM((2 * TOK, HD), BF16),
            pltpu.VMEM((2 * TOK, HD), BF16),
            pltpu.VMEM((8, 2 * TOK), F32),
            pltpu.VMEM((8, 2 * TOK), F32),
            pltpu.VMEM((TOK, 256), BF16),
            pltpu.VMEM((TOK, 256), BF16),
            pltpu.VMEM((8, 256, 512), BF16),
            pltpu.VMEM((8, 256, 512), BF16),
            pltpu.VMEM((8, TOK, 512), F32),
            pltpu.VMEM((2, 4, TOK, 512), BF16),
            pltpu.VMEM((2, 4, TOK, 512), BF16),
            dma((7,)),
            dma((4,)),
            dma((4,)),
            dma((n, 2, 4, 2)),
            dma((n, 2, 4, 2)),
            dma((n, 2, 16)),
            dma((n, 2, 16)),
            dma((n, 2, 16)),
            dma((n, 2, 16)),
            dma((2, 4)),
            dma((2, 4)),
            dma((8,)),
            dma((8,)),
            dma((8,)),
            dma((8,)),
            dma((8,)),
            dma,
            dma,
            dma((2, 2, 4)),
            dma((2, 2, 4)),
            dma,
            dma,
            dma((2,)),
            dma((2,)),
            dma((16,)),
            dma((16,)),
        ],
        compiler_params=pltpu.CompilerParams(
            collective_id=0, has_side_effects=True, vmem_limit_bytes=52 * 2**20
        ),
        cost_estimate=pl.CostEstimate(flops=2 * 10**10, bytes_accessed=3 * 10**7, transcendentals=13 * 10**6),
    )(*args)


def on_device(
    text, gain, wq, wkv, wout, qgain, kgain, gate, images, seg, owner, pos
):
    return fused(
        text, gain, images[0, IMG_TOK - 1 :], wq, wkv, wout, qgain.reshape(1, -1), kgain.reshape(1, -1),
        gate, owner, pos, seg, images,
    )


def solution(mesh):
    rows = ("seq", "section")
    return jax.shard_map(
        on_device,
        mesh=mesh,
        in_specs=(
            P(rows, "tp"),
            P("tp"),
            P(None, "tp"),
            P("tp", None),
            P("tp", None),
            P(),
            P(),
            P(),
            P(rows, None, "tp"),
            P(rows),
            P(rows),
            P(rows),
        ),
        out_specs=P(rows, "tp"),
        check_vma=False,
    )
```
